32 devices in a mesh: dp: 16 (over z, x, core), seq: 2 (over y).
Axes of the slice: x: 2, y: 2, z: 4, core: 2. Of those that a mesh axis runs over, the one named last changes fastest.
Arguments:
- tokens: bfloat16 [16384, 1024], P(('dp', 'seq')), may hold values from -6 to 6
- lengths: int32 [16, 3], P('dp'), may hold values from 1 to 512, 1024 in all within a row
- attn_gain: float32 [1024], replicated, may hold values from 0.25 to 1.75
- attn_shift: float32 [1024], replicated, may hold values from -1.5 to 1.5
- w_qkv: bfloat16 [1024, 3072], P('dp'), may hold values from -0.1875 to 0.1875
- w_out: bfloat16 [1024, 1024], P('dp'), may hold values from -0.5 to 0.5
- ffn_gain: float32 [1024], replicated, may hold values from 0.25 to 1.75
- ffn_shift: float32 [1024], replicated, may hold values from -1.5 to 1.5
- w_up: bfloat16 [1024, 4096], P('dp'), may hold values from -0.1875 to 0.1875
- b_up: float32 [4096], replicated, may hold values from -2.5 to 2.5
- w_down: bfloat16 [4096, 1024], P('dp'), may hold values from -0.125 to 0.125
- b_down: float32 [1024], replicated, may hold values from -2.5 to 2.5
- cotangent: bfloat16 [16384, 1024], P(('dp', 'seq')), may hold values from -6 to 6
Outputs:
- block_out: bfloat16 [16384, 1024], P(('dp', 'seq'))
- grad_tokens: bfloat16 [16384, 1024], P(('dp', 'seq'))
- grad_attn_gain: float32 [1024], replicated
- grad_attn_shift: float32 [1024], replicated
- grad_w_qkv: float32 [1024, 3072], replicated
- grad_w_out: float32 [1024, 1024], replicated
- grad_ffn_gain: float32 [1024], replicated
- grad_ffn_shift: float32 [1024], replicated
- grad_w_up: float32 [1024, 4096], replicated
- grad_b_up: float32 [4096], replicated
- grad_w_down: float32 [4096, 1024], replicated
- grad_b_down: float32 [1024], replicated
The draws below stay inside these ranges and needn't reach their ends.
Inputs may be any that keep to these rules, and one draw needn't show every extreme that they name: Each row of lengths sums to 1024.
All inputs are finite; a program needn't handle non-finite values.
Results may differ from the reference program's by a relative error of at most 0.02.
Values may be sent and summed in bfloat16 or wider, within the bound.
A program may use at most 256 MiB of HBM per device.

```python
import math
import jax
import jax.numpy as jnp
import numpy as np
from jax import lax

D = 1024
HEADS = 8
FF = 4096
ITEMS = 3
GROUP_TOK = 1024
LONGEST = 512
TOKENS = 16384
N_DP = 16


def strengthened(values, rng, source, target, blocks, factor):
    def block_of(position):
        return (jnp.arange(values.shape[position]) // (values.shape[position] // blocks)).reshape((-1,) + (1,) * (values.ndim - 1 - position))

    near = jax.random.permutation(rng, blocks)[block_of(target)]
    far = (block_of(target) + blocks // 2) % blocks
    return jnp.where((block_of(source) == near) | (block_of(source) == far), factor * values, values)


def level_of(own_key, dims, cuts, low, high):
    factor_of = 1.0
    for axis_at, blocks in cuts:
        draws = jax.random.uniform(jax.random.fold_in(jax.random.fold_in(own_key, 6), axis_at), (blocks,), jnp.float32, low / len(cuts), high / len(cuts))
        factor_of = factor_of * jnp.repeat(jnp.exp(draws), dims[axis_at] // blocks).reshape((-1,) + (1,) * (len(dims) - 1 - axis_at))
    return factor_of


def profile(number_of, total, reach, skew):
    loads = [(1 << 20) // math.isqrt(rank ** skew) + 1 for rank in range(2, number_of + 1)]
    rest, given = total - reach - (number_of - 1), [1] * (number_of - 1)
    while rest > 0:
        movable = [i for i in range(number_of - 1) if given[i] < reach]
        pool, budget = sum([loads[i] for i in movable]), rest
        for i in movable:
            more = min(reach - given[i], max(1, budget * loads[i] // pool), rest)
            given[i] = given[i] + more
            rest = rest - more
    return np.array([reach] + given)


def ragged_sizes(key, number_of, total, bound, lean):
    if number_of == 2:
        one = jax.random.randint(key, (), max(1, total - bound), min(bound, total - 1) + 1)
        return jnp.stack([one, total - one])
    tallies = jnp.asarray(profile(number_of, total, bound, lean), jnp.int32)
    pairs = (number_of - 1) // 2
    donor, taker = tallies[1:1 + 2 * pairs:2], tallies[2:2 + 2 * pairs:2]
    slack = jnp.minimum(donor - 1, bound - taker)
    moved = jax.random.randint(jax.random.fold_in(key, 1), (pairs,), 0, 1 << 20) % (slack + 1)
    tallies = tallies.at[1:1 + 2 * pairs:2].set(donor - moved).at[2:2 + 2 * pairs:2].set(taker + moved)
    return tallies[jax.random.permutation(jax.random.fold_in(key, 2), number_of)]


def scatter_about(key, shape, deviation, reach, cuts=(), held_as=jnp.bfloat16):
    drawn = deviation * jax.random.normal(key, shape, jnp.float32)
    if cuts:
        drawn = drawn * level_of(key, shape, cuts, -0.22, 0.18)
    return jnp.clip(drawn, -reach, reach).astype(held_as)


def noise_with(stream_key, shape, deviation, bound, split, heavy, kind=jnp.bfloat16):
    values = deviation * jax.random.normal(stream_key, shape, jnp.float32)
    if split:
        values = values * level_of(stream_key, shape, split, -0.22, 0.18)
    return jnp.clip(strengthened(values, jax.random.fold_in(stream_key, 3), *heavy), -bound, bound).astype(kind)


def setup_inputs(seed: int = 0) -> dict:
    seeds = jax.random.split(jax.random.key(seed), 14)
    tokens = scatter_about(seeds[0], (TOKENS, D), 1.0, 6.0, ((0, 32),))
    lengths = jax.vmap(lambda own: ragged_sizes(own, ITEMS, GROUP_TOK, LONGEST, 2))(jax.random.split(seeds[1], N_DP)).reshape((N_DP, ITEMS)).astype(jnp.int32)
    attn_gain = jnp.clip(1.0 + 0.15 * jax.random.normal(seeds[2], (D,), jnp.float32), 0.25, 1.75)
    attn_shift = scatter_about(seeds[3], (D,), 0.3, 1.5, (), jnp.float32)
    w_qkv = scatter_about(seeds[4], (D, 3 * D), D ** -0.5, 0.1875, ((0, 16),))
    w_out = scatter_about(seeds[5], (D, D), (D // 8) ** -0.5, 0.5, ((0, 16),))
    ffn_gain = jnp.clip(1.0 + 0.15 * jax.random.normal(seeds[6], (D,), jnp.float32), 0.25, 1.75)
    ffn_shift = scatter_about(seeds[7], (D,), 0.3, 1.5, (), jnp.float32)
    w_up = scatter_about(seeds[8], (D, FF), D ** -0.5, 0.1875, ((0, 16),))
    b_up = scatter_about(seeds[9], (FF,), 0.5, 2.5, (), jnp.float32)
    w_down = scatter_about(seeds[10], (FF, D), (FF // 2) ** -0.5, 0.125, ((0, 16),))
    b_down = scatter_about(seeds[11], (D,), 0.5, 2.5, (), jnp.float32)
    cotangent = noise_with(seeds[12], (TOKENS, D), 1.0, 6.0, ((0, 32),), (0, 1, 32, 2.75))
    return {"tokens": tokens, "lengths": lengths, "attn_gain": attn_gain, "attn_shift": attn_shift, "w_qkv": w_qkv, "w_out": w_out, "ffn_gain": ffn_gain, "ffn_shift": ffn_shift, "w_up": w_up, "b_up": b_up, "w_down": w_down, "b_down": b_down, "cotangent": cotangent}


EPS = 1e-05
HIGH = lax.Precision.HIGHEST

@jax.custom_vjp
def low(v):
    return lax.optimization_barrier(v.astype(jnp.bfloat16)).astype(jnp.float32)

@jax.custom_vjp
def low_back(v):
    return v

def low_keep(v):
    return (low(v), None)

def low_pass(kept, grad):
    return (grad,)

def back_keep(v):
    return (v, None)

def back_low(kept, grad):
    return (low(grad),)
low.defvjp(low_keep, low_pass)
low_back.defvjp(back_keep, back_low)

def matmul(left, right):
    return jnp.dot(left, right, precision=HIGH, preferred_element_type=jnp.float32)

def layer_norm(values, gain, shift):
    mean = lax.optimization_barrier(jnp.mean(values, axis=-1, keepdims=True))
    centred = values - mean
    variance = lax.optimization_barrier(jnp.mean(centred * centred, axis=-1, keepdims=True))
    return centred * lax.rsqrt(variance + EPS) * gain + shift

def item_ids(item_lengths, count):
    item_ends = jnp.cumsum(item_lengths.astype(jnp.int32), dtype=jnp.int32).astype(jnp.int32)
    places = jnp.arange(count, dtype=jnp.int32)
    hits = (places[:, None] >= item_ends[None, :]).astype(jnp.int32)
    return lax.optimization_barrier(jnp.sum(hits, axis=1, dtype=jnp.int32)).astype(jnp.int32)

def head_attention(query, keys, values, slope, item_of):
    count = query.shape[0]
    places = jnp.arange(count, dtype=jnp.int32)
    distance = (places[:, None] - places[None, :]).astype(jnp.float32)
    allowed = (item_of[:, None] == item_of[None, :]) & (places[None, :] <= places[:, None])
    scale = query.shape[-1] ** (-0.5)
    scores = matmul(query, keys.T) * scale - slope * distance
    scores = low_back(jnp.where(allowed, scores, jnp.float32(-1000000000.0)))
    top = lax.optimization_barrier(jnp.max(scores, axis=-1, keepdims=True))
    weights = jnp.exp(scores - top)
    probs = low(weights / lax.optimization_barrier(jnp.sum(weights, axis=-1, keepdims=True)))
    return matmul(probs, values)

def group_forward(params, inputs, item_lengths):
    attn_gain, attn_shift, w_qkv, w_out, ffn_gain, ffn_shift, w_up, b_up, w_down, b_down = params
    count, width = inputs.shape
    item_of = item_ids(item_lengths, count)
    first_in = low(layer_norm(inputs, attn_gain, attn_shift))
    projected = low(low_back(matmul(first_in, w_qkv))).reshape(count, 3, HEADS, width // HEADS)
    projected = jnp.transpose(projected, (1, 2, 0, 3))
    exponents = (jnp.arange(HEADS, dtype=jnp.int32) + 1).astype(jnp.float32)
    slopes = jnp.exp2(-exponents)

    def one_head(pieces):
        return head_attention(pieces[0], pieces[1], pieces[2], pieces[3], item_of)
    mixed = lax.map(jax.checkpoint(one_head), (projected[0], projected[1], projected[2], slopes))
    joined = jnp.transpose(mixed, (1, 0, 2)).reshape(count, width)
    joined = low(low_back(joined))
    middle = inputs + low_back(matmul(joined, w_out))
    second_in = low(layer_norm(middle, ffn_gain, ffn_shift))
    active = low(jax.nn.gelu(low_back(matmul(second_in, w_up)) + b_up, approximate=True))
    return middle + low_back(matmul(active, w_down)) + b_down

def reference(tokens, lengths, attn_gain, attn_shift, w_qkv, w_out, ffn_gain, ffn_shift, w_up, b_up, w_down, b_down, cotangent):
    params = tuple((p.astype(jnp.float32) for p in (attn_gain, attn_shift, w_qkv, w_out, ffn_gain, ffn_shift, w_up, b_up, w_down, b_down)))
    inputs = tokens.astype(jnp.float32).reshape(N_DP, GROUP_TOK, D)
    upstream = cotangent.astype(jnp.float32).reshape(N_DP, GROUP_TOK, D)
    group_lengths = lengths.astype(jnp.int32)

    def forward(weights, values):

        def one_group(piece):
            return group_forward(weights, piece[0], piece[1])
        return lax.map(one_group, (values, group_lengths))
    outputs, pullback = jax.vjp(forward, params, inputs)
    grads, grad_inputs = pullback(upstream)
    return (outputs.reshape(TOKENS, D).astype(jnp.bfloat16), grad_inputs.reshape(TOKENS, D).astype(jnp.bfloat16), grads[0], grads[1], grads[2], grads[3], grads[4], grads[5], grads[6], grads[7], grads[8], grads[9])
```

```python
import functools

import jax
import jax.numpy as jnp
from jax import lax
from jax.experimental import pallas as pl
from jax.experimental.pallas import tpu as pltpu
from jax.sharding import PartitionSpec as P

HEADS = 8


EPS = 1e-05


def inner_rows(left, right):
    return lax.dot_general(
        left, right, (((0,), (0,)), ((), ())), preferred_element_type=jnp.float32
    )


def times_transposed(left, right):
    return lax.dot_general(
        left, right, (((1,), (1,)), ((), ())), preferred_element_type=jnp.float32
    )


def smooth_act(values):
    return jax.nn.gelu(values, approximate=True)


def norm_forward(values, gain, shift):
    mean = jnp.mean(values, axis=-1, keepdims=True)
    centred = values - mean
    variance = jnp.mean(centred * centred, axis=-1, keepdims=True)
    factor = lax.rsqrt(variance + EPS)
    normed = centred * factor
    return (normed * gain + shift, normed, factor)


def norm_backward(grad_out, normed, factor, gain):
    grad_normed = grad_out * gain
    centre_term = jnp.mean(grad_normed, axis=-1, keepdims=True)
    along_term = jnp.mean(grad_normed * normed, axis=-1, keepdims=True)
    grad_in = factor * (grad_normed - centre_term - normed * along_term)
    return (grad_in, jnp.sum(grad_out * normed, axis=0), jnp.sum(grad_out, axis=0))


def item_ids(item_lengths, count):
    item_ends = jnp.cumsum(item_lengths, dtype=jnp.int32)
    places = jnp.arange(count, dtype=jnp.int32)
    hits = (places[:, None] >= item_ends[None, :]).astype(jnp.int32)
    return jnp.sum(hits, axis=1, dtype=jnp.int32)


def block_scores(query_block, keys, start, item_of, slopes):
    rows = query_block.shape[0]
    count = keys.shape[0]
    scale = query_block.shape[-1] ** (-0.5)
    raw = jnp.einsum("qhd,khd->hqk", query_block, keys, preferred_element_type=jnp.float32)
    row_places = start + jnp.arange(rows, dtype=jnp.int32)
    col_places = jnp.arange(count, dtype=jnp.int32)
    distance = (row_places[:, None] - col_places[None, :]).astype(jnp.float32)
    row_items = lax.dynamic_slice_in_dim(item_of, start, rows)
    allowed = (row_items[:, None] == item_of[None, :]) & (
        col_places[None, :] <= row_places[:, None]
    )
    scores = raw * scale - slopes[:, None, None] * distance[None]
    return jnp.where(allowed[None], scores, jnp.float32(-1000000000.0))


def attend(heads_qkv, item_of, slopes):
    count = heads_qkv.shape[0]
    rows = min(512, count)
    queries = heads_qkv[:, 0]
    keys = heads_qkv[:, 1]
    values = heads_qkv[:, 2]

    def one_block(index):
        start = index * rows
        query_block = lax.dynamic_slice_in_dim(queries, start, rows)
        scores = block_scores(query_block, keys, start, item_of, slopes)
        top = jnp.max(scores, axis=-1, keepdims=True)
        weights = jnp.exp(scores - top)
        total = jnp.sum(weights, axis=-1, keepdims=True)
        probs = (weights / total).astype(jnp.bfloat16)
        mixed = jnp.einsum("hqk,khd->qhd", probs, values, preferred_element_type=jnp.float32)
        return (mixed.astype(jnp.bfloat16), (top + jnp.log(total))[..., 0])

    mixed, log_norm = lax.map(one_block, jnp.arange(count // rows, dtype=jnp.int32))
    return (mixed.reshape(count, mixed.shape[2], mixed.shape[3]), log_norm)


def attend_back(heads_qkv, heads_out, grad_heads, log_norm, item_of, slopes):
    count = heads_qkv.shape[0]
    rows = min(512, count)
    queries = heads_qkv[:, 0]
    keys = heads_qkv[:, 1]
    values = heads_qkv[:, 2]
    scale = queries.shape[-1] ** (-0.5)
    row_dots = jnp.sum(grad_heads.astype(jnp.float32) * heads_out.astype(jnp.float32), axis=-1)

    def one_block(carry, index):
        grad_keys, grad_values = carry
        start = index * rows
        query_block = lax.dynamic_slice_in_dim(queries, start, rows)
        grad_block = lax.dynamic_slice_in_dim(grad_heads, start, rows)
        dots = lax.dynamic_slice_in_dim(row_dots, start, rows)
        scores = block_scores(query_block, keys, start, item_of, slopes)
        probs = jnp.exp(scores - log_norm[index][:, :, None])
        probs_low = probs.astype(jnp.bfloat16)
        grad_values = grad_values + jnp.einsum(
            "hqk,qhd->khd", probs_low, grad_block, preferred_element_type=jnp.float32
        )
        grad_probs = jnp.einsum(
            "qhd,khd->hqk", grad_block, values, preferred_element_type=jnp.float32
        )
        grad_scores = (probs * (grad_probs - jnp.transpose(dots)[:, :, None])).astype(jnp.bfloat16)
        grad_query = (
            jnp.einsum("hqk,khd->qhd", grad_scores, keys, preferred_element_type=jnp.float32)
            * scale
        )
        grad_keys = (
            grad_keys
            + jnp.einsum(
                "hqk,qhd->khd", grad_scores, query_block, preferred_element_type=jnp.float32
            )
            * scale
        )
        return ((grad_keys, grad_values), grad_query)

    empty = jnp.zeros(keys.shape, jnp.float32)
    (grad_keys, grad_values), grad_query = lax.scan(
        one_block, (empty, empty), jnp.arange(count // rows, dtype=jnp.int32)
    )
    grad_query = grad_query.reshape(keys.shape)
    return jnp.stack([grad_query, grad_keys, grad_values], axis=1).astype(jnp.bfloat16)


def on_device(
    tokens,
    lengths,
    attn_gain,
    attn_shift,
    w_qkv,
    w_out,
    ffn_gain,
    ffn_shift,
    w_up,
    b_up,
    w_down,
    b_down,
    cotangent,
):
    w_qkv, w_out, w_up, w_down = (
        lax.all_gather(w_qkv, "dp", axis=0, tiled=True),
        lax.all_gather(w_out, "dp", axis=0, tiled=True),
        lax.all_gather(w_up, "dp", axis=0, tiled=True),
        lax.all_gather(w_down, "dp", axis=0, tiled=True),
    )
    local, width = tokens.shape
    groups = lax.axis_size("seq")
    per_head = width // HEADS
    local_heads = HEADS // groups
    count = local * groups
    item_of = item_ids(lengths[0], count)
    first_head = lax.axis_index("seq") * local_heads
    exponents = (first_head + jnp.arange(local_heads, dtype=jnp.int32) + 1).astype(jnp.float32)
    slopes = jnp.exp2(-exponents)
    inputs = tokens.astype(jnp.float32)
    normed_in, unit_in, factor_in = norm_forward(inputs, attn_gain, attn_shift)
    first_in = normed_in.astype(jnp.bfloat16)
    projected = jnp.dot(first_in, w_qkv, preferred_element_type=jnp.float32).astype(jnp.bfloat16)
    projected = projected.reshape(local, 3, HEADS, per_head)
    heads_qkv = lax.all_to_all(projected, "seq", split_axis=2, concat_axis=0, tiled=True)
    heads_out, log_norm = attend(heads_qkv, item_of, slopes)
    joined = lax.all_to_all(heads_out, "seq", split_axis=0, concat_axis=1, tiled=True).reshape(
        local, width
    )
    middle = inputs + jnp.dot(joined, w_out, preferred_element_type=jnp.float32)
    normed_mid, unit_mid, factor_mid = norm_forward(middle, ffn_gain, ffn_shift)
    second_in = normed_mid.astype(jnp.bfloat16)
    pre_act = jnp.dot(second_in, w_up, preferred_element_type=jnp.float32) + b_up
    act_value, act_pull = jax.vjp(smooth_act, pre_act)
    active = act_value.astype(jnp.bfloat16)
    block_out = (
        middle + jnp.dot(active, w_down, preferred_element_type=jnp.float32) + b_down
    ).astype(jnp.bfloat16)
    grad_out = cotangent.astype(jnp.float32)
    grad_b_down = jnp.sum(grad_out, axis=0)
    grad_w_down = inner_rows(active, cotangent)
    grad_active = times_transposed(cotangent, w_down)
    grad_pre = act_pull(grad_active)[0]
    grad_b_up = jnp.sum(grad_pre, axis=0)
    grad_pre_low = grad_pre.astype(jnp.bfloat16)
    grad_w_up = inner_rows(second_in, grad_pre_low)
    grad_second = times_transposed(grad_pre_low, w_up)
    grad_mid_norm, grad_ffn_gain, grad_ffn_shift = norm_backward(
        grad_second, unit_mid, factor_mid, ffn_gain
    )
    grad_middle = grad_out + grad_mid_norm
    grad_branch = grad_middle.astype(jnp.bfloat16)
    grad_w_out = inner_rows(joined, grad_branch)
    grad_joined = (
        times_transposed(grad_branch, w_out).astype(jnp.bfloat16).reshape(local, HEADS, per_head)
    )
    grad_heads = lax.all_to_all(grad_joined, "seq", split_axis=1, concat_axis=0, tiled=True)
    grad_qkv_heads = attend_back(heads_qkv, heads_out, grad_heads, log_norm, item_of, slopes)
    grad_projected = lax.all_to_all(
        grad_qkv_heads, "seq", split_axis=0, concat_axis=2, tiled=True
    ).reshape(local, 3 * width)
    grad_w_qkv = inner_rows(first_in, grad_projected)
    grad_first = times_transposed(grad_projected, w_qkv)
    grad_in_norm, grad_attn_gain, grad_attn_shift = norm_backward(
        grad_first, unit_in, factor_in, attn_gain
    )
    grad_tokens = (grad_middle + grad_in_norm).astype(jnp.bfloat16)
    all_part = (
        lax.psum_scatter(
            grad_attn_gain.astype(jnp.bfloat16), "dp", scatter_dimension=0, tiled=True
        ).astype(jnp.float32),
        lax.psum_scatter(
            grad_attn_shift.astype(jnp.bfloat16), "dp", scatter_dimension=0, tiled=True
        ).astype(jnp.float32),
        lax.psum_scatter(
            grad_w_qkv.astype(jnp.bfloat16), "dp", scatter_dimension=0, tiled=True
        ).astype(jnp.float32),
        lax.psum_scatter(
            grad_w_out.astype(jnp.bfloat16), "dp", scatter_dimension=0, tiled=True
        ).astype(jnp.float32),
        lax.psum_scatter(
            grad_ffn_gain.astype(jnp.bfloat16), "dp", scatter_dimension=0, tiled=True
        ).astype(jnp.float32),
        lax.psum_scatter(
            grad_ffn_shift.astype(jnp.bfloat16), "dp", scatter_dimension=0, tiled=True
        ).astype(jnp.float32),
        lax.psum_scatter(
            grad_w_up.astype(jnp.bfloat16), "dp", scatter_dimension=0, tiled=True
        ).astype(jnp.float32),
        lax.psum_scatter(
            grad_b_up.astype(jnp.bfloat16), "dp", scatter_dimension=0, tiled=True
        ).astype(jnp.float32),
        lax.psum_scatter(
            grad_w_down.astype(jnp.bfloat16), "dp", scatter_dimension=0, tiled=True
        ).astype(jnp.float32),
        lax.psum_scatter(
            grad_b_down.astype(jnp.bfloat16), "dp", scatter_dimension=0, tiled=True
        ).astype(jnp.float32),
    )
    all_part = (
        lax.psum(all_part[0].astype(jnp.bfloat16), "seq").astype(jnp.float32),
        lax.psum(all_part[1].astype(jnp.bfloat16), "seq").astype(jnp.float32),
        lax.psum(all_part[2].astype(jnp.bfloat16), "seq").astype(jnp.float32),
        lax.psum(all_part[3].astype(jnp.bfloat16), "seq").astype(jnp.float32),
        lax.psum(all_part[4].astype(jnp.bfloat16), "seq").astype(jnp.float32),
        lax.psum(all_part[5].astype(jnp.bfloat16), "seq").astype(jnp.float32),
        lax.psum(all_part[6].astype(jnp.bfloat16), "seq").astype(jnp.float32),
        lax.psum(all_part[7].astype(jnp.bfloat16), "seq").astype(jnp.float32),
        lax.psum(all_part[8].astype(jnp.bfloat16), "seq").astype(jnp.float32),
        lax.psum(all_part[9].astype(jnp.bfloat16), "seq").astype(jnp.float32),
    )
    summed = (
        lax.all_gather(all_part[0].astype(jnp.bfloat16), "dp", axis=0, tiled=True).astype(
            jnp.float32
        ),
        lax.all_gather(all_part[1].astype(jnp.bfloat16), "dp", axis=0, tiled=True).astype(
            jnp.float32
        ),
        lax.all_gather(all_part[2].astype(jnp.bfloat16), "dp", axis=0, tiled=True).astype(
            jnp.float32
        ),
        lax.all_gather(all_part[3].astype(jnp.bfloat16), "dp", axis=0, tiled=True).astype(
            jnp.float32
        ),
        lax.all_gather(all_part[4].astype(jnp.bfloat16), "dp", axis=0, tiled=True).astype(
            jnp.float32
        ),
        lax.all_gather(all_part[5].astype(jnp.bfloat16), "dp", axis=0, tiled=True).astype(
            jnp.float32
        ),
        lax.all_gather(all_part[6].astype(jnp.bfloat16), "dp", axis=0, tiled=True).astype(
            jnp.float32
        ),
        lax.all_gather(all_part[7].astype(jnp.bfloat16), "dp", axis=0, tiled=True).astype(
            jnp.float32
        ),
        lax.all_gather(all_part[8].astype(jnp.bfloat16), "dp", axis=0, tiled=True).astype(
            jnp.float32
        ),
        lax.all_gather(all_part[9].astype(jnp.bfloat16), "dp", axis=0, tiled=True).astype(
            jnp.float32
        ),
    )
    return (
        block_out,
        grad_tokens,
        summed[0],
        summed[1],
        summed[2],
        summed[3],
        summed[4],
        summed[5],
        summed[6],
        summed[7],
        summed[8],
        summed[9],
    )


MESH = pl.DeviceIdType.MESH


class Place:
    def __init__(self, n_z):
        dp = lax.axis_index("dp")
        self.n_z = n_z
        self.dp = dp
        self.y = lax.axis_index("seq")
        self.core = dp % 2
        self.chip = dp // 2
        self.x = self.chip % 2
        self.z = self.chip // 2
        self.quarter = 2 * self.core + self.y

    def device(self, z=None, x=None, core=None, y=None):
        z = self.z if z is None else z
        x = self.x if x is None else x
        core = self.core if core is None else core
        y = self.y if y is None else y
        return ((z * 2 + x) * 2 + core, y)

    def across_core(self):
        return self.device(core=1 - self.core)

    def across_x(self):
        return self.device(x=1 - self.x)

    def across_y(self):
        return self.device(y=1 - self.y)

    def z_after(self, k):
        return (self.z + k) % self.n_z

    def z_before(self, k):
        return (self.z + self.n_z - k) % self.n_z

    def along_z(self, k):
        return self.device(z=self.z_after(k))


class Copies:
    def __init__(self, send, recv, near):
        self.send, self.recv, self.near = send, recv, near
        self.sent, self.held, self.n, self.m = [], [], 0, 0

    def remote(self, src, dst, device):
        copy = pltpu.make_async_remote_copy(
            src_ref=src,
            dst_ref=dst,
            send_sem=self.send.at[self.n],
            recv_sem=self.recv.at[self.n],
            device_id=device,
            device_id_type=MESH,
        )
        self.n += 1
        copy.start()
        self.sent.append(copy)
        self.held.append(copy)
        return copy

    def local(self, src, dst):
        copy = pltpu.make_async_copy(src, dst, self.near.at[self.m])
        self.m += 1
        copy.start()
        return copy

    def arrive(self, *copies):
        for copy in copies:
            copy.wait_recv()
            self.held = [other for other in self.held if other is not copy]

    def finish(self):
        for copy in self.held:
            copy.wait_recv()
        for copy in self.sent:
            copy.wait_send()
        self.held, self.sent = [], []


def meet(devices):
    barrier = pltpu.get_barrier_semaphore()
    for device in devices:
        pl.semaphore_signal(barrier, inc=1, device_id=device, device_id_type=MESH)
    pl.semaphore_wait(barrier, len(devices))


def at(start, size, unit):
    return pl.ds(pl.multiple_of(start, unit), size)


def communicate(kernel, out_shapes, ins, out_specs, in_specs, counts, scratch=(), call_id=0, limit=None):
    return pl.pallas_call(
        kernel,
        out_shape=out_shapes,
        in_specs=in_specs,
        out_specs=out_specs,
        scratch_shapes=list(scratch)
        + [
            pltpu.SemaphoreType.DMA((counts[0],)),
            pltpu.SemaphoreType.DMA((counts[0],)),
            pltpu.SemaphoreType.DMA((counts[1],)),
        ],
        compiler_params=pltpu.CompilerParams(
            collective_id=call_id, has_side_effects=True, vmem_limit_bytes=limit or (56 << 20)
        ),
    )(*ins)


HBM = pl.BlockSpec(memory_space=pltpu.HBM)
VMEM = pl.BlockSpec(memory_space=pltpu.VMEM)
SMEM = pl.BlockSpec(memory_space=pltpu.SMEM)


def gather_kernel(n_z, wq, wo, wu, wd, tok, cot, lens, WQ, WO, WU, WD, XQ, CQ, LQ, send, recv, near):
    me = Place(n_z)
    run = Copies(send, recv, near)
    quarter, other = me.quarter, 2 * (1 - me.core) + me.y
    rows = wq.shape[0]
    third = wq.shape[1] // 3
    cut = third // 4
    chips = 2 * n_z
    span = wu.shape[1] // chips
    unit = span // 4
    meet(
        [me.across_core(), me.across_x(), me.across_y()] + [me.along_z(k) for k in range(1, n_z)]
    )
    mine = at(me.dp * rows, rows, 16)
    pair = at(me.chip * 2 * rows, 2 * rows, 16)

    def pair_of(z):
        return at((z * 2 + me.x) * 2 * rows, 2 * rows, 16)

    begun = []
    landed_q = []
    for p in range(3):
        into = WQ.at[mine, p * cut : (p + 1) * cut]
        begun.append(run.local(wq.at[:, at(p * third + quarter * cut, cut, 128)], into))
        landed_q.append(
            run.remote(wq.at[:, at(p * third + other * cut, cut, 128)], into, me.across_core())
        )
    block = tok.shape[0]
    half = block // 2

    def spread(src, dst):
        keep = run.local(src, dst.at[quarter])
        over = [
            run.remote(src.at[h * half : (h + 1) * half], dst.at[quarter, h * half : (h + 1) * half], me.across_y())
            for h in range(2)
        ]
        run.remote(src, dst.at[quarter], me.across_core())
        return keep, over

    def pass_on(over, dst):
        slot = 2 * me.core + 1 - me.y
        for h in range(2):
            run.arrive(over[h])
            part = dst.at[slot, h * half : (h + 1) * half]
            run.remote(part, part, me.across_core())

    last = [run.local(lens, LQ.at[me.core])]
    run.remote(lens, LQ.at[me.core], me.across_core())
    keep_x, over_x = spread(tok, XQ)
    last.append(keep_x)
    landed_u, begun_u = [], []
    for s in range(chips):
        into = WU.at[mine, s * unit : (s + 1) * unit]
        begun_u.append(run.local(wu.at[:, at(s * span + quarter * unit, unit, 128)], into))
        landed_u.append(
            run.remote(wu.at[:, at(s * span + other * unit, unit, 128)], into, me.across_core())
        )
    for copy in begun:
        copy.wait()
    run.arrive(*landed_q)
    part = WQ.at[pair]
    from_z = {"q": [run.remote(part, part, me.along_z(k)) for k in range(1, n_z)]}
    run.remote(part, part, me.across_x())
    from_z["o"] = [run.remote(wo, WO.at[mine], me.along_z(k)) for k in range(1, n_z)]
    from_x = [run.remote(wo, WO.at[mine], me.across_x())]
    run.remote(wo, WO.at[mine], me.across_core())
    last.append(run.local(wo, WO.at[mine]))
    for copy in begun_u:
        copy.wait()
    run.arrive(*landed_u)
    part = WU.at[pair]
    from_z["u"] = [run.remote(part, part, me.along_z(k)) for k in range(1, n_z)]
    run.remote(part, part, me.across_x())
    own = wd.at[at(me.y * unit, unit, 16)]
    into = WD.at[at(me.chip * unit, unit, 16)]
    from_z["d"] = [run.remote(own, into, me.along_z(k)) for k in range(1, n_z)]
    run.remote(own, into, me.across_x())
    last.append(run.local(own, into))
    keep_c, over_c = spread(cot, CQ)
    last.append(keep_c)

    for k in range(1, n_z):
        z = me.z_before(k)
        run.arrive(from_z["q"][k - 1])
        part = WQ.at[pair_of(z)]
        run.remote(part, part, me.across_x())
    pass_on(over_x, XQ)
    for k in range(1, n_z):
        z = me.z_before(k)
        run.arrive(from_z["o"][k - 1])
        part = WO.at[at(((z * 2 + me.x) * 2 + me.core) * rows, rows, 16)]
        from_x.append(run.remote(part, part, me.across_x()))
        run.remote(part, part, me.across_core())
    for k in range(1, n_z):
        z = me.z_before(k)
        run.arrive(from_z["u"][k - 1])
        part = WU.at[pair_of(z)]
        run.remote(part, part, me.across_x())
    for k in range(1, n_z):
        z = me.z_before(k)
        run.arrive(from_z["d"][k - 1])
        part = WD.at[at((z * 2 + me.x) * unit, unit, 16)]
        run.remote(part, part, me.across_x())
    pass_on(over_c, CQ)
    for k in range(n_z):
        z = me.z_before(k)
        run.arrive(from_x[k])
        part = WO.at[at(((z * 2 + 1 - me.x) * 2 + me.core) * rows, rows, 16)]
        run.remote(part, part, me.across_core())
    run.finish()
    for copy in last:
        copy.wait()


def gather_all(n_z, wq, wo, wu, wd, tok, cot, lens):
    width, low = wq.shape[0] * 4 * n_z, jnp.bfloat16
    quarter_ff = wu.shape[1] // 4
    shapes = [
        jax.ShapeDtypeStruct((width, wq.shape[1] // 4), low),
        jax.ShapeDtypeStruct((width, width), low),
        jax.ShapeDtypeStruct((width, quarter_ff), low),
        jax.ShapeDtypeStruct((quarter_ff, width), low),
        jax.ShapeDtypeStruct((4,) + tok.shape, low),
        jax.ShapeDtypeStruct((4,) + tok.shape, low),
        jax.ShapeDtypeStruct((2,) + lens.shape, lens.dtype),
    ]
    return communicate(
        functools.partial(gather_kernel, n_z),
        shapes,
        (wq, wo, wu, wd, tok, cot, lens),
        [HBM] * 7,
        [HBM] * 7,
        (96, 24),
        call_id=1,
    )


def quad_columns_kernel(n_z, src, dst, send, recv, near):
    me = Place(n_z)
    run = Copies(send, recv, near)
    rows, cols = src.shape
    parts = 4
    step = rows // parts
    meet([me.across_core(), me.across_y()])

    def place(quarter, i):
        return dst.at[i * step : (i + 1) * step, at(quarter * cols, cols, 128)]

    over = []
    for i in range(parts):
        over.append(
            run.remote(src.at[i * step : (i + 1) * step], place(me.quarter, i), me.across_y())
        )
    keep = run.local(src, dst.at[:, at(me.quarter * cols, cols, 128)])
    run.remote(src, dst.at[:, at(me.quarter * cols, cols, 128)], me.across_core())
    for i in range(parts):
        run.arrive(over[i])
        part = place(2 * me.core + 1 - me.y, i)
        run.remote(part, part, me.across_core())
    run.finish()
    keep.wait()


def quad_columns(n_z, src):
    return communicate(
        functools.partial(quad_columns_kernel, n_z),
        jax.ShapeDtypeStruct((src.shape[0], 4 * src.shape[1]), src.dtype),
        (src,),
        HBM,
        [HBM],
        (12, 1),
        call_id=2,
    )


def quad_blocks_kernel(n_z, src, dst, send, recv, near):
    me = Place(n_z)
    run = Copies(send, recv, near)
    rows = src.shape[0]
    parts = 4
    step = rows // parts
    meet([me.across_core(), me.across_y()])
    over = []
    for i in range(parts):
        cut = slice(i * step, (i + 1) * step)
        over.append(run.remote(src.at[cut], dst.at[me.quarter, cut], me.across_y()))
    keep = run.local(src, dst.at[me.quarter])
    run.remote(src, dst.at[me.quarter], me.across_core())
    for i in range(parts):
        run.arrive(over[i])
        part = dst.at[2 * me.core + 1 - me.y, i * step : (i + 1) * step]
        run.remote(part, part, me.across_core())
    run.finish()
    keep.wait()


def quad_blocks(n_z, src):
    return communicate(
        functools.partial(quad_blocks_kernel, n_z),
        jax.ShapeDtypeStruct((4,) + src.shape, src.dtype),
        (src,),
        HBM,
        [HBM],
        (12, 1),
        call_id=3,
    )


def add(*values):
    total = values[0].astype(jnp.float32)
    for value in values[1:]:
        total = total + value.astype(jnp.float32)
    return total


def reduce_kernel(n_z, n_quad, n_chip, *refs):
    me = Place(n_z)
    n_in = n_quad + n_chip
    ins, outs, rest = refs[:n_in], refs[n_in : 2 * n_in], refs[2 * n_in :]
    scratch, (send, recv, near) = rest[:-3], rest[-3:]
    run = Copies(send, recv, near)
    devices = [me.across_core(), me.across_y()]
    if n_chip:
        devices += [me.across_x()] + [me.along_z(k) for k in range(1, n_z)]
    meet(devices)
    quad_scratch = [scratch[3 * i : 3 * i + 3] for i in range(n_quad)]
    chip_scratch = [scratch[3 * n_quad + 3 * i : 3 * n_quad + 3 * i + 3] for i in range(n_chip)]
    order = [1 - me.y, me.y]

    def quad_start(i):
        near_recv = quad_scratch[i][0]
        return [
            run.remote(ins[i].at[2 * (1 - me.core) + y], near_recv.at[y], me.across_core()) for y in order
        ]

    def chip_start(i):
        far_recv = chip_scratch[i][0]
        sent = []
        for k in range(1, n_z + 1):
            z = me.z_after(k)
            sent.append(
                run.remote(ins[n_quad + i].at[z * 2 + 1 - me.x], far_recv.at[z], me.across_x())
            )
        return sent

    near_sent = [quad_start(i) for i in range(n_quad)]
    x_sent = [chip_start(i) for i in range(n_chip)]
    y_sent = []
    for i in range(n_quad):
        near_recv, over_send, over_recv = quad_scratch[i]
        run.arrive(near_sent[i][0])
        over_send[...] = add(ins[i][2 * me.core + 1 - me.y], near_recv[1 - me.y]).astype(jnp.bfloat16)
        y_sent.append(run.remote(over_send, over_recv, me.across_y()))
    z_sent = []
    for k in range(1, n_z + 1):
        z = me.z_after(k)
        for i in range(n_chip):
            far_recv, z_send, z_recv = chip_scratch[i]
            run.arrive(x_sent[i][k - 1])
            z_send[z] = add(ins[n_quad + i][z * 2 + me.x], far_recv[z]).astype(jnp.bfloat16)
            if k < n_z:
                z_sent.append(run.remote(z_send.at[z], z_recv.at[k - 1], me.along_z(k)))
    for i in range(n_quad):
        near_recv, over_send, over_recv = quad_scratch[i]
        run.arrive(near_sent[i][1], y_sent[i])
        outs[i][...] = add(ins[i][2 * me.core + me.y], near_recv[me.y], over_recv[...])
    run.arrive(*z_sent)
    for i in range(n_chip):
        far_recv, z_send, z_recv = chip_scratch[i]
        outs[n_quad + i][...] = add(z_send[me.z], *[z_recv[k] for k in range(n_z - 1)]).astype(
            jnp.bfloat16
        )
    run.finish()


def reduce_all(n_z, quads, chips, call_id):
    scratch, shapes = [], []
    for value in quads:
        block = value.shape[1:]
        scratch += [
            pltpu.VMEM((2,) + block, jnp.bfloat16),
            pltpu.VMEM(block, jnp.bfloat16),
            pltpu.VMEM(block, jnp.bfloat16),
        ]
        shapes.append(jax.ShapeDtypeStruct(block, jnp.float32))
    for value in chips:
        block = value.shape[1:]
        scratch += [
            pltpu.VMEM((n_z,) + block, jnp.bfloat16),
            pltpu.VMEM((n_z,) + block, jnp.bfloat16),
            pltpu.VMEM((n_z - 1,) + block, jnp.bfloat16),
        ]
        shapes.append(jax.ShapeDtypeStruct(block, jnp.bfloat16))
    n = len(quads) + len(chips)
    return communicate(
        functools.partial(reduce_kernel, n_z, len(quads), len(chips)),
        shapes,
        tuple(quads) + tuple(chips),
        [VMEM] * n,
        [VMEM] * n,
        (3 * len(quads) + (2 * n_z - 1) * len(chips) + 1, 1),
        scratch,
        call_id=call_id,
    )


def share_kernel(n_z, n_parts, src, dst, send, recv, near):
    me = Place(n_z)
    run = Copies(send, recv, near)
    step = src.shape[0] // n_parts
    half = step // 2
    meet(
        [me.across_core(), me.across_x(), me.across_y()] + [me.along_z(k) for k in range(1, n_z)]
    )

    def slot(z, x, y):
        return ((z * 2 + x) * 2 + me.core) * 2 + y

    own = slot(me.z, me.x, me.y)
    keep = run.local(src, dst.at[own])
    run.remote(src, dst.at[own], me.across_core())
    spans = [
        (slice(p * step, p * step + half), slice(p * step + half, (p + 1) * step), slice(p * step, (p + 1) * step))
        for p in range(n_parts)
    ]
    from_z = {}
    for p, (_, _, whole) in enumerate(spans):
        for k in range(1, n_z):
            from_z[k, p] = run.remote(src.at[whole], dst.at[own, whole], me.along_z(k))
    level = {}

    def fan(k, p):
        first, second, whole = spans[p]
        here = dst.at[slot(me.z_before(k), me.x, me.y)]
        there = here if k else src
        level["xa", k, p] = run.remote(there.at[first], here.at[first], me.across_x())
        level["yb", k, p] = run.remote(there.at[second], here.at[second], me.across_y())
        level["ya", k, p] = run.remote(there.at[first], here.at[first], me.across_y())
        level["xb", k, p] = run.remote(there.at[second], here.at[second], me.across_x())
        if k:
            run.remote(here.at[whole], here.at[whole], me.across_core())

    def relay(k, p):
        first, second, _ = spans[p]
        z = me.z_before(k)
        run.arrive(level["xa", k, p])
        part = dst.at[slot(z, 1 - me.x, me.y), first]
        level["late a", k, p] = run.remote(part, part, me.across_y())
        run.arrive(level["yb", k, p])
        part = dst.at[slot(z, me.x, 1 - me.y), second]
        level["late b", k, p] = run.remote(part, part, me.across_x())

    def hand_over(k, p):
        whole = spans[p][2]
        z = me.z_before(k)
        run.arrive(level["xb", k, p])
        part = dst.at[slot(z, 1 - me.x, me.y), whole]
        run.remote(part, part, me.across_core())
        run.arrive(level["ya", k, p])
        part = dst.at[slot(z, me.x, 1 - me.y), whole]
        run.remote(part, part, me.across_core())

    def hand_last(k, p):
        run.arrive(level["late a", k, p], level["late b", k, p])
        part = dst.at[slot(me.z_before(k), 1 - me.x, 1 - me.y), spans[p][2]]
        run.remote(part, part, me.across_core())

    steps = [(k, p) for k in range(n_z) for p in range(n_parts)]
    for i in range(len(steps) + 3):
        if i < len(steps):
            k, p = steps[i]
            if k:
                run.arrive(from_z[k, p])
            fan(k, p)
        if 1 <= i < len(steps) + 1:
            relay(*steps[i - 1])
        if 2 <= i < len(steps) + 2:
            hand_over(*steps[i - 2])
        if 3 <= i < len(steps) + 3:
            hand_last(*steps[i - 3])
    run.finish()
    keep.wait()


def share_all(n_z, src, n_parts, call_id):
    return communicate(
        functools.partial(share_kernel, n_z, n_parts),
        jax.ShapeDtypeStruct((8 * n_z,) + src.shape, src.dtype),
        (src,),
        HBM,
        [HBM],
        (n_parts * (n_z * 10 + n_z) + 1, 1),
        call_id=call_id,
    )


def allowed_and_bias(first, rows, count, ends, slope):
    row = first + lax.broadcasted_iota(jnp.int32, (rows, 1), 0)
    col = lax.broadcasted_iota(jnp.int32, (1, count), 1)
    begin = jnp.zeros((rows, 1), jnp.int32)
    for end in ends:
        begin = jnp.where(row >= end, end, begin)
    allowed = (col >= begin) & (col <= row)
    bias = slope * (col - first).astype(jnp.float32)
    return allowed, bias


NEVER = -1000000000.0


def attend_kernel(slopes, ends, q, k, v, o, lse):
    group, head = pl.program_id(0), pl.program_id(1)
    count, size = q.shape
    rows = min(256, count)
    slope = slopes[head]
    stops = [ends[group, i] for i in range(ends.shape[1] - 1)]
    for first in range(0, count, rows):
        here = slice(first, first + rows)
        seen = first + rows
        allowed, bias = allowed_and_bias(first, rows, seen, stops, slope)
        s = times_transposed(q[here], k[:seen]) * size**-0.5 + bias
        s = jnp.where(allowed, s, NEVER)
        top = jnp.max(s, axis=-1, keepdims=True)
        w = jnp.exp(s - top)
        total = jnp.sum(w, axis=-1, keepdims=True)
        p = (w * (1.0 / total)).astype(jnp.bfloat16)
        o[here] = jnp.dot(p, v[:seen], preferred_element_type=jnp.float32).astype(jnp.bfloat16)
        lse[here] = top + jnp.log(total)


def attend_back_kernel(slopes, ends, q, k, v, o, lse, do, dq, dk, dv, sum_k, sum_v):
    group, head = pl.program_id(0), pl.program_id(1)
    count, size = q.shape
    rows = min(256, count)
    slope = slopes[head]
    scale = size**-0.5
    stops = [ends[group, i] for i in range(ends.shape[1] - 1)]
    sum_k[...] = jnp.zeros_like(sum_k)
    sum_v[...] = jnp.zeros_like(sum_v)
    for first in range(0, count, rows):
        here = slice(first, first + rows)
        seen = first + rows
        allowed, bias = allowed_and_bias(first, rows, seen, stops, slope)
        s = times_transposed(q[here], k[:seen]) * scale + bias
        p = jnp.exp(jnp.where(allowed, s, NEVER) - lse[here])
        grad = do[here]
        dots = jnp.sum(grad.astype(jnp.float32) * o[here].astype(jnp.float32), axis=-1, keepdims=True)
        sum_v[:seen] += inner_rows(p.astype(jnp.bfloat16), grad)
        ds = (p * (times_transposed(grad, v[:seen]) - dots)).astype(jnp.bfloat16)
        dq[here] = (jnp.dot(ds, k[:seen], preferred_element_type=jnp.float32) * scale).astype(jnp.bfloat16)
        sum_k[:seen] += inner_rows(ds, q[here])
    dk[...] = (sum_k[...] * scale).astype(jnp.bfloat16)
    dv[...] = sum_v[...].astype(jnp.bfloat16)


def head_spec(count, size, offset):
    return pl.BlockSpec((count, size), lambda g, h: (g, offset + h))


def attention(qkv, slopes, ends, count, size):
    groups, heads = qkv.shape[0] // count, qkv.shape[1] // size // 3
    return pl.pallas_call(
        attend_kernel,
        grid=(groups, heads),
        in_specs=[SMEM, SMEM] + [head_spec(count, size, heads * i) for i in range(3)],
        out_specs=[head_spec(count, size, 0), pl.BlockSpec((None, None, count, 1), lambda g, h: (g, h, 0, 0))],
        out_shape=[
            jax.ShapeDtypeStruct((qkv.shape[0], heads * size), jnp.bfloat16),
            jax.ShapeDtypeStruct((groups, heads, count, 1), jnp.float32),
        ],
        compiler_params=pltpu.CompilerParams(vmem_limit_bytes=48 << 20),
    )(slopes, ends, qkv, qkv, qkv)


def attention_back(qkv, o, lse, do, slopes, ends, count, size):
    groups, heads = qkv.shape[0] // count, qkv.shape[1] // size // 3
    own = head_spec(count, size, 0)
    shape = jax.ShapeDtypeStruct((qkv.shape[0], heads * size), jnp.bfloat16)
    return pl.pallas_call(
        attend_back_kernel,
        grid=(groups, heads),
        in_specs=[SMEM, SMEM]
        + [head_spec(count, size, heads * i) for i in range(3)]
        + [own, pl.BlockSpec((None, None, count, 1), lambda g, h: (g, h, 0, 0)), own],
        out_specs=[own] * 3,
        out_shape=[shape] * 3,
        scratch_shapes=[pltpu.VMEM((count, size), jnp.float32)] * 2,
        compiler_params=pltpu.CompilerParams(vmem_limit_bytes=48 << 20),
    )(slopes, ends, qkv, qkv, qkv, o, lse, do)


def on_quad(
    tokens,
    lengths,
    attn_gain,
    attn_shift,
    w_qkv,
    w_out,
    ffn_gain,
    ffn_shift,
    w_up,
    b_up,
    w_down,
    b_down,
    cotangent,
):
    low = jnp.bfloat16
    local, width = tokens.shape
    n_dp = lax.axis_size("dp")
    n_z, chips = n_dp // 4, n_dp // 2
    size = width // HEADS
    heads = HEADS // 4
    count = 2 * local
    me = Place(n_z)
    lens = jnp.zeros((8, 128), jnp.int32).at[:1, : lengths.shape[1]].set(lengths)
    WQ, WO, WU, WD, XQ, CQ, LQ = gather_all(n_z, w_qkv, w_out, w_up, w_down, tokens, cotangent, lens)
    ends = jnp.cumsum(LQ[:, 0, : lengths.shape[1]], axis=1, dtype=jnp.int32)
    slopes = jnp.exp2(-(me.quarter * heads + jnp.arange(heads, dtype=jnp.int32) + 1).astype(jnp.float32))

    h1 = norm_forward(XQ.reshape(4 * local, width).astype(jnp.float32), attn_gain, attn_shift)[0].astype(low)
    qkv = jnp.dot(h1, WQ, preferred_element_type=jnp.float32).astype(low)
    o, lse = attention(qkv, slopes, ends, count, size)
    joined = quad_columns(n_z, o)
    middle = XQ.reshape(4 * local, width).astype(jnp.float32) + jnp.dot(
        joined, WO, preferred_element_type=jnp.float32
    )
    h2 = norm_forward(middle, ffn_gain, ffn_shift)[0].astype(low)
    middle = lax.dynamic_slice_in_dim(middle, me.quarter * local, local)
    _, unit_mid, factor_mid = norm_forward(middle, ffn_gain, ffn_shift)

    unit = w_up.shape[1] // chips // 4
    bias = lax.dynamic_index_in_dim(b_up.reshape(chips, 4, unit), me.quarter, 1, keepdims=False).reshape(-1)
    c = CQ.reshape(4 * local, width)
    pre = jnp.dot(h2, WU, preferred_element_type=jnp.float32) + bias
    act, pull = jax.vjp(smooth_act, pre)
    active = act.astype(low)
    grad_pre = pull(times_transposed(c, WD))[0]
    grad_pre_low = grad_pre.astype(low)
    part_out = jnp.dot(active, WD, preferred_element_type=jnp.float32).astype(low)
    part_h2 = times_transposed(grad_pre_low, WU).astype(low)
    part_down = inner_rows(active, c).astype(low)
    part_up = inner_rows(h2, grad_pre_low).astype(low)
    grad_b_up = jnp.sum(grad_pre, axis=0)
    sum_h2, sum_out, sum_down, sum_up = reduce_all(
        n_z,
        [part_h2.reshape(4, local, width), part_out.reshape(4, local, width)],
        [part_down.reshape(chips, -1, width), part_up.reshape(chips, -1, part_up.shape[1])],
        4,
    )
    block_out = (middle + sum_out + b_down).astype(low)
    grad_out = cotangent.astype(jnp.float32)
    grad_mid_norm, grad_ffn_gain, grad_ffn_shift = norm_backward(sum_h2, unit_mid, factor_mid, ffn_gain)
    grad_middle = grad_out + grad_mid_norm
    branch = quad_blocks(n_z, grad_middle.astype(low)).reshape(4 * local, width)
    mine = lax.dynamic_slice_in_dim(WO, me.quarter * heads * size, heads * size)
    part_w_out = inner_rows(o, branch).astype(low)
    do = times_transposed(branch, mine).astype(low)
    dqkv = jnp.concatenate(attention_back(qkv, o, lse, do, slopes, ends, count, size), axis=1)
    part_qkv = inner_rows(h1, dqkv).astype(low)
    part_h1 = times_transposed(dqkv, WQ).astype(low)
    sum_h1, sum_qkv, sum_w_out = reduce_all(
        n_z,
        [part_h1.reshape(4, local, width)],
        [part_qkv.reshape(chips, -1, part_qkv.shape[1]), part_w_out.reshape(chips, -1, width)],
        5,
    )
    _, unit_in, factor_in = norm_forward(tokens.astype(jnp.float32), attn_gain, attn_shift)
    grad_in_norm, grad_attn_gain, grad_attn_shift = norm_backward(sum_h1, unit_in, factor_in, attn_gain)
    grad_tokens = (grad_middle + grad_in_norm).astype(low)

    rows = sum_qkv.shape[0]
    few = sum_w_out.shape[0]
    across = rows // few
    side = jnp.concatenate([sum_w_out[:, i * (width // across) : (i + 1) * (width // across)] for i in range(across)])
    slab = jnp.concatenate([sum_down, sum_up, jnp.concatenate([sum_qkv, side], axis=1)])
    shared = share_all(n_z, slab, 3, 6).reshape(chips, 4, 3, rows, width)
    f32 = jnp.float32
    grad_w_down = shared[:, :, 0].reshape(-1, width).astype(f32)
    up = shared[:, :, 1].reshape(chips, 4, rows, chips, unit)
    grad_w_up = jnp.transpose(up, (0, 2, 3, 1, 4)).reshape(width, -1).astype(f32)
    three = shared[:, :, 2, :, : 3 * heads * size].reshape(chips, 4, rows, 3, heads * size)
    grad_w_qkv = jnp.transpose(three, (0, 2, 3, 1, 4)).reshape(width, -1).astype(f32)
    side = shared[:, :, 2, :, 3 * heads * size :].reshape(chips, 4, across, few, width // across)
    grad_w_out = jnp.transpose(side, (1, 0, 3, 2, 4)).reshape(width, width).astype(f32)

    spread = jnp.zeros((chips, 4, unit), f32)
    spread = lax.dynamic_update_slice(spread, grad_b_up.reshape(chips, 1, unit), (0, me.quarter, 0))
    small = jnp.concatenate(
        [
            spread.reshape(-1),
            grad_attn_gain,
            grad_attn_shift,
            grad_ffn_gain,
            grad_ffn_shift,
            jnp.sum(grad_out, axis=0),
        ]
    )
    small = lax.psum(small, ("dp", "seq"))
    ff = w_up.shape[1]
    vectors = [small[ff + i * width : ff + (i + 1) * width] for i in range(5)]
    return (
        block_out,
        grad_tokens,
        vectors[0],
        vectors[1],
        grad_w_qkv,
        grad_w_out,
        vectors[2],
        vectors[3],
        grad_w_up,
        small[:ff],
        grad_w_down,
        vectors[4],
    )


def solution(mesh):
    n_dp, n_seq = mesh.shape["dp"], mesh.shape["seq"]
    quad = n_seq == 2 and n_dp % 4 == 0 and n_dp >= 8 and n_dp <= 16
    return jax.shard_map(
        on_quad if quad else on_device,
        mesh=mesh,
        in_specs=(
            P(("dp", "seq"), None),
            P("dp", None),
            P(),
            P(),
            P("dp", None),
            P("dp", None),
            P(),
            P(),
            P("dp", None),
            P(),
            P("dp", None),
            P(),
            P(("dp", "seq"), None),
        ),
        out_specs=(
            P(("dp", "seq"), None),
            P(("dp", "seq"), None),
            P(),
            P(),
            P(),
            P(),
            P(),
            P(),
            P(),
            P(),
            P(),
            P(),
        ),
        check_vma=False,
    )
```

```python
import functools

import jax
import jax.numpy as jnp
from jax import lax
from jax.experimental import pallas as pl
from jax.experimental.pallas import tpu as pltpu
from jax.sharding import PartitionSpec as P

HEADS = 8


EPS = 1e-05
NEVER = -1000000000.0


def inner_rows(left, right):
    return lax.dot_general(
        left, right, (((0,), (0,)), ((), ())), preferred_element_type=jnp.float32
    )


def times_transposed(left, right):
    return lax.dot_general(
        left, right, (((1,), (1,)), ((), ())), preferred_element_type=jnp.float32
    )


def smooth_act(values):
    return jax.nn.gelu(values, approximate=True)


def norm_forward(values, gain, shift):
    mean = jnp.mean(values, axis=-1, keepdims=True)
    centred = values - mean
    variance = jnp.mean(centred * centred, axis=-1, keepdims=True)
    factor = lax.rsqrt(variance + EPS)
    normed = centred * factor
    return (normed * gain + shift, normed, factor)


def norm_backward(grad_out, normed, factor, gain):
    grad_normed = grad_out * gain
    centre_term = jnp.mean(grad_normed, axis=-1, keepdims=True)
    along_term = jnp.mean(grad_normed * normed, axis=-1, keepdims=True)
    grad_in = factor * (grad_normed - centre_term - normed * along_term)
    return (grad_in, jnp.sum(grad_out * normed, axis=0), jnp.sum(grad_out, axis=0))


def item_ids(item_lengths, count):
    item_ends = jnp.cumsum(item_lengths, dtype=jnp.int32)
    places = jnp.arange(count, dtype=jnp.int32)
    hits = (places[:, None] >= item_ends[None, :]).astype(jnp.int32)
    return jnp.sum(hits, axis=1, dtype=jnp.int32)


def block_scores(query_block, keys, start, item_of, slopes):
    rows = query_block.shape[0]
    count = keys.shape[0]
    scale = query_block.shape[-1] ** (-0.5)
    raw = jnp.einsum("qhd,khd->hqk", query_block, keys, preferred_element_type=jnp.float32)
    row_places = start + jnp.arange(rows, dtype=jnp.int32)
    col_places = jnp.arange(count, dtype=jnp.int32)
    distance = (row_places[:, None] - col_places[None, :]).astype(jnp.float32)
    row_items = lax.dynamic_slice_in_dim(item_of, start, rows)
    allowed = (row_items[:, None] == item_of[None, :]) & (
        col_places[None, :] <= row_places[:, None]
    )
    scores = raw * scale - slopes[:, None, None] * distance[None]
    return jnp.where(allowed[None], scores, jnp.float32(-1000000000.0))


def attend(heads_qkv, item_of, slopes):
    count = heads_qkv.shape[0]
    rows = min(512, count)
    queries = heads_qkv[:, 0]
    keys = heads_qkv[:, 1]
    values = heads_qkv[:, 2]

    def one_block(index):
        start = index * rows
        query_block = lax.dynamic_slice_in_dim(queries, start, rows)
        scores = block_scores(query_block, keys, start, item_of, slopes)
        top = jnp.max(scores, axis=-1, keepdims=True)
        weights = jnp.exp(scores - top)
        total = jnp.sum(weights, axis=-1, keepdims=True)
        probs = (weights / total).astype(jnp.bfloat16)
        mixed = jnp.einsum("hqk,khd->qhd", probs, values, preferred_element_type=jnp.float32)
        return (mixed.astype(jnp.bfloat16), (top + jnp.log(total))[..., 0])

    mixed, log_norm = lax.map(one_block, jnp.arange(count // rows, dtype=jnp.int32))
    return (mixed.reshape(count, mixed.shape[2], mixed.shape[3]), log_norm)


def attend_back(heads_qkv, heads_out, grad_heads, log_norm, item_of, slopes):
    count = heads_qkv.shape[0]
    rows = min(512, count)
    queries = heads_qkv[:, 0]
    keys = heads_qkv[:, 1]
    values = heads_qkv[:, 2]
    scale = queries.shape[-1] ** (-0.5)
    row_dots = jnp.sum(grad_heads.astype(jnp.float32) * heads_out.astype(jnp.float32), axis=-1)

    def one_block(carry, index):
        grad_keys, grad_values = carry
        start = index * rows
        query_block = lax.dynamic_slice_in_dim(queries, start, rows)
        grad_block = lax.dynamic_slice_in_dim(grad_heads, start, rows)
        dots = lax.dynamic_slice_in_dim(row_dots, start, rows)
        scores = block_scores(query_block, keys, start, item_of, slopes)
        probs = jnp.exp(scores - log_norm[index][:, :, None])
        probs_low = probs.astype(jnp.bfloat16)
        grad_values = grad_values + jnp.einsum(
            "hqk,qhd->khd", probs_low, grad_block, preferred_element_type=jnp.float32
        )
        grad_probs = jnp.einsum(
            "qhd,khd->hqk", grad_block, values, preferred_element_type=jnp.float32
        )
        grad_scores = (probs * (grad_probs - jnp.transpose(dots)[:, :, None])).astype(jnp.bfloat16)
        grad_query = (
            jnp.einsum("hqk,khd->qhd", grad_scores, keys, preferred_element_type=jnp.float32)
            * scale
        )
        grad_keys = (
            grad_keys
            + jnp.einsum(
                "hqk,qhd->khd", grad_scores, query_block, preferred_element_type=jnp.float32
            )
            * scale
        )
        return ((grad_keys, grad_values), grad_query)

    empty = jnp.zeros(keys.shape, jnp.float32)
    (grad_keys, grad_values), grad_query = lax.scan(
        one_block, (empty, empty), jnp.arange(count // rows, dtype=jnp.int32)
    )
    grad_query = grad_query.reshape(keys.shape)
    return jnp.stack([grad_query, grad_keys, grad_values], axis=1).astype(jnp.bfloat16)


def on_device(
    tokens,
    lengths,
    attn_gain,
    attn_shift,
    w_qkv,
    w_out,
    ffn_gain,
    ffn_shift,
    w_up,
    b_up,
    w_down,
    b_down,
    cotangent,
):
    w_qkv, w_out, w_up, w_down = (
        lax.all_gather(w_qkv, "dp", axis=0, tiled=True),
        lax.all_gather(w_out, "dp", axis=0, tiled=True),
        lax.all_gather(w_up, "dp", axis=0, tiled=True),
        lax.all_gather(w_down, "dp", axis=0, tiled=True),
    )
    local, width = tokens.shape
    groups = lax.axis_size("seq")
    per_head = width // HEADS
    local_heads = HEADS // groups
    count = local * groups
    item_of = item_ids(lengths[0], count)
    first_head = lax.axis_index("seq") * local_heads
    exponents = (first_head + jnp.arange(local_heads, dtype=jnp.int32) + 1).astype(jnp.float32)
    slopes = jnp.exp2(-exponents)
    inputs = tokens.astype(jnp.float32)
    normed_in, unit_in, factor_in = norm_forward(inputs, attn_gain, attn_shift)
    first_in = normed_in.astype(jnp.bfloat16)
    projected = jnp.dot(first_in, w_qkv, preferred_element_type=jnp.float32).astype(jnp.bfloat16)
    projected = projected.reshape(local, 3, HEADS, per_head)
    heads_qkv = lax.all_to_all(projected, "seq", split_axis=2, concat_axis=0, tiled=True)
    heads_out, log_norm = attend(heads_qkv, item_of, slopes)
    joined = lax.all_to_all(heads_out, "seq", split_axis=0, concat_axis=1, tiled=True).reshape(
        local, width
    )
    middle = inputs + jnp.dot(joined, w_out, preferred_element_type=jnp.float32)
    normed_mid, unit_mid, factor_mid = norm_forward(middle, ffn_gain, ffn_shift)
    second_in = normed_mid.astype(jnp.bfloat16)
    pre_act = jnp.dot(second_in, w_up, preferred_element_type=jnp.float32) + b_up
    act_value, act_pull = jax.vjp(smooth_act, pre_act)
    active = act_value.astype(jnp.bfloat16)
    block_out = (
        middle + jnp.dot(active, w_down, preferred_element_type=jnp.float32) + b_down
    ).astype(jnp.bfloat16)
    grad_out = cotangent.astype(jnp.float32)
    grad_b_down = jnp.sum(grad_out, axis=0)
    grad_w_down = inner_rows(active, cotangent)
    grad_active = times_transposed(cotangent, w_down)
    grad_pre = act_pull(grad_active)[0]
    grad_b_up = jnp.sum(grad_pre, axis=0)
    grad_pre_low = grad_pre.astype(jnp.bfloat16)
    grad_w_up = inner_rows(second_in, grad_pre_low)
    grad_second = times_transposed(grad_pre_low, w_up)
    grad_mid_norm, grad_ffn_gain, grad_ffn_shift = norm_backward(
        grad_second, unit_mid, factor_mid, ffn_gain
    )
    grad_middle = grad_out + grad_mid_norm
    grad_branch = grad_middle.astype(jnp.bfloat16)
    grad_w_out = inner_rows(joined, grad_branch)
    grad_joined = (
        times_transposed(grad_branch, w_out).astype(jnp.bfloat16).reshape(local, HEADS, per_head)
    )
    grad_heads = lax.all_to_all(grad_joined, "seq", split_axis=1, concat_axis=0, tiled=True)
    grad_qkv_heads = attend_back(heads_qkv, heads_out, grad_heads, log_norm, item_of, slopes)
    grad_projected = lax.all_to_all(
        grad_qkv_heads, "seq", split_axis=0, concat_axis=2, tiled=True
    ).reshape(local, 3 * width)
    grad_w_qkv = inner_rows(first_in, grad_projected)
    grad_first = times_transposed(grad_projected, w_qkv)
    grad_in_norm, grad_attn_gain, grad_attn_shift = norm_backward(
        grad_first, unit_in, factor_in, attn_gain
    )
    grad_tokens = (grad_middle + grad_in_norm).astype(jnp.bfloat16)
    all_part = (
        lax.psum_scatter(
            grad_attn_gain.astype(jnp.bfloat16), "dp", scatter_dimension=0, tiled=True
        ).astype(jnp.float32),
        lax.psum_scatter(
            grad_attn_shift.astype(jnp.bfloat16), "dp", scatter_dimension=0, tiled=True
        ).astype(jnp.float32),
        lax.psum_scatter(
            grad_w_qkv.astype(jnp.bfloat16), "dp", scatter_dimension=0, tiled=True
        ).astype(jnp.float32),
        lax.psum_scatter(
            grad_w_out.astype(jnp.bfloat16), "dp", scatter_dimension=0, tiled=True
        ).astype(jnp.float32),
        lax.psum_scatter(
            grad_ffn_gain.astype(jnp.bfloat16), "dp", scatter_dimension=0, tiled=True
        ).astype(jnp.float32),
        lax.psum_scatter(
            grad_ffn_shift.astype(jnp.bfloat16), "dp", scatter_dimension=0, tiled=True
        ).astype(jnp.float32),
        lax.psum_scatter(
            grad_w_up.astype(jnp.bfloat16), "dp", scatter_dimension=0, tiled=True
        ).astype(jnp.float32),
        lax.psum_scatter(
            grad_b_up.astype(jnp.bfloat16), "dp", scatter_dimension=0, tiled=True
        ).astype(jnp.float32),
        lax.psum_scatter(
            grad_w_down.astype(jnp.bfloat16), "dp", scatter_dimension=0, tiled=True
        ).astype(jnp.float32),
        lax.psum_scatter(
            grad_b_down.astype(jnp.bfloat16), "dp", scatter_dimension=0, tiled=True
        ).astype(jnp.float32),
    )
    all_part = (
        lax.psum(all_part[0].astype(jnp.bfloat16), "seq").astype(jnp.float32),
        lax.psum(all_part[1].astype(jnp.bfloat16), "seq").astype(jnp.float32),
        lax.psum(all_part[2].astype(jnp.bfloat16), "seq").astype(jnp.float32),
        lax.psum(all_part[3].astype(jnp.bfloat16), "seq").astype(jnp.float32),
        lax.psum(all_part[4].astype(jnp.bfloat16), "seq").astype(jnp.float32),
        lax.psum(all_part[5].astype(jnp.bfloat16), "seq").astype(jnp.float32),
        lax.psum(all_part[6].astype(jnp.bfloat16), "seq").astype(jnp.float32),
        lax.psum(all_part[7].astype(jnp.bfloat16), "seq").astype(jnp.float32),
        lax.psum(all_part[8].astype(jnp.bfloat16), "seq").astype(jnp.float32),
        lax.psum(all_part[9].astype(jnp.bfloat16), "seq").astype(jnp.float32),
    )
    summed = (
        lax.all_gather(all_part[0].astype(jnp.bfloat16), "dp", axis=0, tiled=True).astype(
            jnp.float32
        ),
        lax.all_gather(all_part[1].astype(jnp.bfloat16), "dp", axis=0, tiled=True).astype(
            jnp.float32
        ),
        lax.all_gather(all_part[2].astype(jnp.bfloat16), "dp", axis=0, tiled=True).astype(
            jnp.float32
        ),
        lax.all_gather(all_part[3].astype(jnp.bfloat16), "dp", axis=0, tiled=True).astype(
            jnp.float32
        ),
        lax.all_gather(all_part[4].astype(jnp.bfloat16), "dp", axis=0, tiled=True).astype(
            jnp.float32
        ),
        lax.all_gather(all_part[5].astype(jnp.bfloat16), "dp", axis=0, tiled=True).astype(
            jnp.float32
        ),
        lax.all_gather(all_part[6].astype(jnp.bfloat16), "dp", axis=0, tiled=True).astype(
            jnp.float32
        ),
        lax.all_gather(all_part[7].astype(jnp.bfloat16), "dp", axis=0, tiled=True).astype(
            jnp.float32
        ),
        lax.all_gather(all_part[8].astype(jnp.bfloat16), "dp", axis=0, tiled=True).astype(
            jnp.float32
        ),
        lax.all_gather(all_part[9].astype(jnp.bfloat16), "dp", axis=0, tiled=True).astype(
            jnp.float32
        ),
    )
    return (
        block_out,
        grad_tokens,
        summed[0],
        summed[1],
        summed[2],
        summed[3],
        summed[4],
        summed[5],
        summed[6],
        summed[7],
        summed[8],
        summed[9],
    )


MESH = pl.DeviceIdType.MESH


class Place:
    def __init__(self, n_z):
        dp = lax.axis_index("dp")
        self.n_z = n_z
        self.dp = dp
        self.y = lax.axis_index("seq")
        self.core = dp % 2
        self.chip = dp // 2
        self.x = self.chip % 2
        self.z = self.chip // 2
        self.quarter = 2 * self.core + self.y

    def device(self, z=None, x=None, core=None, y=None):
        z = self.z if z is None else z
        x = self.x if x is None else x
        core = self.core if core is None else core
        y = self.y if y is None else y
        return ((z * 2 + x) * 2 + core, y)

    def across_core(self):
        return self.device(core=1 - self.core)

    def across_x(self):
        return self.device(x=1 - self.x)

    def across_y(self):
        return self.device(y=1 - self.y)

    def z_after(self, k):
        return (self.z + k) % self.n_z

    def z_before(self, k):
        return (self.z + self.n_z - k) % self.n_z

    def along_z(self, k):
        return self.device(z=self.z_after(k))


class Copy:
    def __init__(self, copy, sends, lands):
        self.copy, self.sends, self.lands, self.landed = copy, sends, lands, False

    def guarded(self, condition, action):
        if condition is None:
            action()
        else:
            pl.when(condition)(action)


class Copies:
    def __init__(self, send, recv, near):
        self.send, self.recv, self.near = send, recv, near
        self.all, self.n, self.m, self.local_open = [], 0, 0, []

    def remote(self, src, dst, device, sends=None, lands=None):
        copy = Copy(
            pltpu.make_async_remote_copy(
                src_ref=src,
                dst_ref=dst,
                send_sem=self.send.at[self.n],
                recv_sem=self.recv.at[self.n],
                device_id=device,
                device_id_type=MESH,
            ),
            sends,
            lands,
        )
        self.n += 1
        copy.guarded(sends, copy.copy.start)
        self.all.append(copy)
        return copy

    def local(self, src, dst):
        copy = pltpu.make_async_copy(src, dst, self.near.at[self.m])
        self.m += 1
        copy.start()
        return copy

    def later(self, src, dst):
        self.local_open.append(self.local(src, dst))

    def arrive(self, *copies):
        for copy in copies:
            if not copy.landed:
                copy.guarded(copy.lands, copy.copy.wait_recv)
                copy.landed = True

    def finish(self):
        self.arrive(*self.all)
        for copy in self.all:
            copy.guarded(copy.sends, copy.copy.wait_send)
        for copy in self.local_open:
            copy.wait()


class Line:
    def __init__(self, me, run, own, view):
        self.me, self.run, self.view = me, run, view
        n, z = me.n_z, me.z
        self.up = [run.remote(own, view(z), me.device(z=z + 1), z < n - 1, z > 0)]
        self.down = [run.remote(own, view(z), me.device(z=z - 1), z > 0, z < n - 1)]

    def step(self, t, then):
        me, run, n, z = self.me, self.run, self.me.n_z, self.me.z
        if t >= n:
            return
        run.arrive(self.up[t - 1])
        if t < n - 1:
            part = self.view(z - t)
            self.up.append(run.remote(part, part, me.device(z=z + 1), (z >= t) & (z < n - 1), z > t))
        then(z - t, z >= t)
        run.arrive(self.down[t - 1])
        if t < n - 1:
            part = self.view(z + t)
            self.down.append(
                run.remote(part, part, me.device(z=z - 1), (z < n - t) & (z > 0), z < n - t - 1)
            )
        then(z + t, z < n - t)


def meet(devices):
    barrier = pltpu.get_barrier_semaphore()
    for device in devices:
        pl.semaphore_signal(barrier, inc=1, device_id=device, device_id_type=MESH)
    pl.semaphore_wait(barrier, len(devices))


def at(start, size, unit):
    return pl.ds(pl.multiple_of(start, unit), size)


def communicate(kernel, out_shapes, ins, out_specs, in_specs, counts, scratch=(), call_id=0, limit=None):
    return pl.pallas_call(
        kernel,
        out_shape=out_shapes,
        in_specs=in_specs,
        out_specs=out_specs,
        scratch_shapes=list(scratch)
        + [
            pltpu.SemaphoreType.DMA((counts[0],)),
            pltpu.SemaphoreType.DMA((counts[0],)),
            pltpu.SemaphoreType.DMA((counts[1],)),
        ],
        compiler_params=pltpu.CompilerParams(
            collective_id=call_id, has_side_effects=True, vmem_limit_bytes=limit or (56 << 20)
        ),
    )(*ins)


HBM = pl.BlockSpec(memory_space=pltpu.HBM)
VMEM = pl.BlockSpec(memory_space=pltpu.VMEM)
SMEM = pl.BlockSpec(memory_space=pltpu.SMEM)


def allowed_and_bias(first, rows, count, ends, slope):
    row = first + lax.broadcasted_iota(jnp.int32, (rows, 1), 0)
    col = lax.broadcasted_iota(jnp.int32, (1, count), 1)
    begin = jnp.zeros((rows, 1), jnp.int32)
    for end in ends:
        begin = jnp.where(row >= end, end, begin)
    allowed = (col >= begin) & (col <= row)
    bias = slope * (col - first).astype(jnp.float32)
    return allowed, bias


def norm_rows(values, gain, shift):
    mean = jnp.mean(values, axis=-1, keepdims=True)
    centred = values - mean
    variance = jnp.mean(centred * centred, axis=-1, keepdims=True)
    return centred * lax.rsqrt(variance + EPS) * gain + shift


def norm_block(src, dst, gain, shift, step=64):
    @pl.loop(0, src.shape[0], step=step)
    def _(i):
        rows = at(i, step, step)
        dst[rows, :] = norm_rows(src[rows, :].astype(jnp.float32), gain[...], shift[...]).astype(dst.dtype)


def front_kernel(
    n_z,
    n_items,
    wq,
    wo,
    wu,
    wd,
    tok,
    cot,
    lens,
    attn_gain,
    attn_shift,
    ffn_gain,
    ffn_shift,
    WQ,
    WOQ,
    WU,
    WD,
    CQ,
    H1,
    QKV,
    O,
    LSE,
    H2,
    MID,
    LQ,
    q_all,
    o_all,
    x_all,
    h1,
    qkv,
    mixed,
    lse,
    h2,
    middle,
    ends,
    send,
    recv,
    near,
):
    me = Place(n_z)
    run = Copies(send, recv, near)
    quarter, other = me.quarter, 2 * (1 - me.core) + me.y
    rows = wq.shape[0]
    third = wq.shape[1] // 3
    cut = third // 4
    chips = 2 * n_z
    span = wu.shape[1] // chips
    unit = span // 4
    local = tok.shape[0]
    count = 2 * local
    half = local // 2
    size = third // HEADS
    heads = HEADS // 4
    meet(
        [me.across_core(), me.across_x(), me.across_y()] + [me.along_z(k) for k in range(1, n_z)]
    )
    mine = at(me.dp * rows, rows, 16)

    into = [q_all.at[mine, p * cut : (p + 1) * cut] for p in range(3)]
    near_q = [run.local(wq.at[:, at(p * third + quarter * cut, cut, 128)], into[p]) for p in range(3)]
    core_q = [
        run.remote(wq.at[:, at(p * third + other * cut, cut, 128)], into[p], me.across_core())
        for p in range(3)
    ]
    keep_x = run.local(tok, x_all.at[quarter])
    keep_lens = run.local(lens, LQ.at[me.core])
    core_lens = run.remote(lens, LQ.at[me.core], me.across_core())

    def halves(h):
        return slice(h * half, (h + 1) * half)

    over_x = [
        run.remote(tok.at[halves(h)], x_all.at[quarter, halves(h)], me.across_y()) for h in range(2)
    ]
    core_x = run.remote(tok, x_all.at[quarter], me.across_core())
    into = [WU.at[mine, s * unit : (s + 1) * unit] for s in range(chips)]
    near_u = [run.local(wu.at[:, at(s * span + quarter * unit, unit, 128)], into[s]) for s in range(chips)]
    core_u = [
        run.remote(wu.at[:, at(s * span + other * unit, unit, 128)], into[s], me.across_core())
        for s in range(chips)
    ]

    def pairs_of(array):
        return lambda z, x=me.x: array.at[at((z * 2 + x) * 2 * rows, 2 * rows, 16)]

    def shard_of(z, x=me.x):
        return o_all.at[at(((z * 2 + x) * 2 + me.core) * rows, rows, 16)]

    def units_of(z, x=me.x):
        return WD.at[at((z * 2 + x) * unit, unit, 16)]

    from_x = {"q": [], "o": [], "u": [], "d": []}
    share_o = []

    def across(name, view):
        def then(z, came):
            part = view(z)
            from_x[name].append((run.remote(part, part, me.across_x(), came, came), z, came))
            if name == "o":
                share_o.append(run.remote(part, part, me.across_core(), came, came))

        return then

    for copy in near_q:
        copy.wait()
    run.arrive(*core_q)
    view_q, view_u = pairs_of(q_all), pairs_of(WU)
    line_q = Line(me, run, view_q(me.z), view_q)
    across("q", view_q)(me.z, None)
    line_o = Line(me, run, wo, shard_of)
    from_x["o"].append((run.remote(wo, shard_of(me.z), me.across_x()), me.z, None))
    share_o.append(run.remote(wo, shard_of(me.z), me.across_core()))
    keep_o = run.local(wo, shard_of(me.z))
    keep_x.wait()
    norm_block(x_all.at[quarter], h1.at[quarter], attn_gain, attn_shift)
    for copy in near_u:
        copy.wait()
    run.arrive(*core_u)
    line_u = Line(me, run, view_u(me.z), view_u)
    across("u", view_u)(me.z, None)
    own = wd.at[at(me.y * unit, unit, 16)]
    line_d = Line(me, run, own, units_of)
    from_x["d"].append((run.remote(own, units_of(me.z), me.across_x()), me.z, None))
    run.later(own, units_of(me.z))
    run.later(cot, CQ.at[quarter])
    run.remote(cot, CQ.at[quarter], me.across_core())
    run.arrive(core_x)
    norm_block(x_all.at[other], h1.at[other], attn_gain, attn_shift)
    line_q.step(1, across("q", view_q))
    beside = 2 * me.core + 1 - me.y
    far = 2 * (1 - me.core) + 1 - me.y
    far_x = []
    for h in range(2):
        run.arrive(over_x[h])
        part = x_all.at[beside, halves(h)]
        far_x.append(run.remote(part, part, me.across_core()))
        norm_block(x_all.at[beside, halves(h)], h1.at[beside, halves(h)], attn_gain, attn_shift)
        line_q.step(2 + h, across("q", view_q))
    over_c = [run.remote(cot.at[halves(0)], CQ.at[quarter, halves(0)], me.across_y())]
    for h in range(2):
        run.arrive(far_x[h])
        norm_block(x_all.at[far, halves(h)], h1.at[far, halves(h)], attn_gain, attn_shift)
    line_o.step(1, across("o", shard_of))
    run.later(h1, H1)
    for copy, _, _ in from_x["q"]:
        run.arrive(copy)
    run.later(q_all, WQ)

    @pl.loop(0, 4 * local, step=256)
    def _(i):
        block = at(i, 256, 256)
        qkv[block, :] = jnp.dot(
            h1[i // local, at(i % local, 256, 256), :], q_all[...], preferred_element_type=jnp.float32
        ).astype(jnp.bfloat16)

    run.later(qkv, QKV)
    keep_lens.wait()
    run.arrive(core_lens)
    fetch = run.local(LQ, ends)
    fetch.wait()

    def heads_at(owner, head):
        return at(owner * heads * size + head * size, size, 128)

    over_o, near_o = [], []
    pumps = [
        lambda: line_o.step(2, across("o", shard_of)),
        lambda: line_o.step(3, across("o", shard_of)),
        lambda: line_u.step(1, across("u", view_u)),
        lambda: line_u.step(2, across("u", view_u)),
    ]
    for g in range(2):
        stops = []
        total = 0
        for item in range(n_items - 1):
            total = total + ends[g, 0, item]
            stops.append(total)
        for head in range(heads):
            slope = jnp.exp2(-(jnp.zeros((1, 1), jnp.float32) + (quarter * heads + head + 1)))
            column = heads_at(quarter, head)
            for first in range(0, count, 256):
                start, seen = g * count, first + 256
                here = slice(start + first, start + seen)
                allowed, bias = allowed_and_bias(first, 256, seen, stops, slope)
                keys = qkv[start : start + seen, (heads + head) * size : (heads + head + 1) * size]
                s = times_transposed(qkv[here, head * size : (head + 1) * size], keys) * size**-0.5 + bias
                s = jnp.where(allowed, s, NEVER)
                top = jnp.max(s, axis=-1, keepdims=True)
                w = jnp.exp(s - top)
                sum_w = jnp.sum(w, axis=-1, keepdims=True)
                p = (w * (1.0 / sum_w)).astype(jnp.bfloat16)
                values = qkv[start : start + seen, (2 * heads + head) * size : (2 * heads + head + 1) * size]
                mixed[here, column] = jnp.dot(p, values, preferred_element_type=jnp.float32).astype(
                    jnp.bfloat16
                )
                lse[g, head, first:seen] = top + jnp.log(sum_w)
            part = mixed.at[g * count : (g + 1) * count, column]
            over_o.append(run.remote(part, part, me.across_y()))
            near_o.append(run.remote(part, part, me.across_core()))
            pumps[g * heads + head]()
    run.later(mixed.at[:, at(quarter * heads * size, heads * size, 128)], O)
    run.later(lse, LSE)
    over_c.append(run.remote(cot.at[halves(1)], CQ.at[quarter, halves(1)], me.across_y()))
    run.arrive(over_c[0])
    part = CQ.at[beside, halves(0)]
    run.remote(part, part, me.across_core())
    far_o = []
    for copy, z, came in from_x["o"]:
        run.arrive(copy)
        part = shard_of(z, 1 - me.x)
        far_o.append(run.remote(part, part, me.across_core(), came, came))
    line_u.step(3, across("u", view_u))
    passed = []
    for g in range(2):
        for head in range(heads):
            run.arrive(over_o[g * heads + head])
            part = mixed.at[g * count : (g + 1) * count, heads_at(beside, head)]
            passed.append(run.remote(part, part, me.across_core()))
    line_d.step(1, across("d", units_of))
    keep_o.wait()
    run.arrive(*share_o, *far_o)
    run.later(o_all.at[at(quarter * heads * size, heads * size, 16)], WOQ)
    for g in range(2):
        run.arrive(*near_o[g * heads : (g + 1) * heads], *passed[g * heads : (g + 1) * heads])

        @pl.loop(0, count, step=256)
        def _(i):
            block = at(g * count + i, 256, 256)
            owner, inner = 2 * g + i // local, at(i % local, 256, 256)
            x1 = x_all[owner, inner, :].astype(jnp.float32) + jnp.dot(
                mixed[block, :], o_all[...], preferred_element_type=jnp.float32
            )
            h2[block, :] = norm_rows(x1, ffn_gain[...], ffn_shift[...]).astype(jnp.bfloat16)

            @pl.when(owner == quarter)
            def _():
                middle[inner, :] = x1

        line_d.step(2 + g, across("d", units_of))
    run.later(h2, H2)
    run.later(middle, MID)
    run.arrive(over_c[1])
    part = CQ.at[beside, halves(1)]
    run.remote(part, part, me.across_core())
    run.finish()


def front(n_z, n_items, wq, wo, wu, wd, tok, cot, lens, gains):
    width, low, f32 = wq.shape[0] * 4 * n_z, jnp.bfloat16, jnp.float32
    quarter_ff = wu.shape[1] // 4
    local = tok.shape[0]
    heads, size = HEADS // 4, width // HEADS
    shape = jax.ShapeDtypeStruct
    shapes = [
        shape((width, wq.shape[1] // 4), low),
        shape((width // 4, width), low),
        shape((width, quarter_ff), low),
        shape((quarter_ff, width), low),
        shape((4, local, width), low),
        shape((4, local, width), low),
        shape((4 * local, 3 * width // 4), low),
        shape((4 * local, width // 4), low),
        shape((2, heads, 2 * local, 1), f32),
        shape((4 * local, width), low),
        shape((local, width), f32),
        shape((2,) + lens.shape, lens.dtype),
    ]
    scratch = [
        pltpu.VMEM((width, wq.shape[1] // 4), low),
        pltpu.VMEM((width, width), low),
        pltpu.VMEM((4, local, width), low),
        pltpu.VMEM((4, local, width), low),
        pltpu.VMEM((4 * local, 3 * width // 4), low),
        pltpu.VMEM((4 * local, width), low),
        pltpu.VMEM((2, heads, 2 * local, 1), f32),
        pltpu.VMEM((4 * local, width), low),
        pltpu.VMEM((local, width), f32),
        pltpu.SMEM((2,) + lens.shape, lens.dtype),
    ]
    return communicate(
        functools.partial(front_kernel, n_z, n_items),
        shapes,
        (wq, wo, wu, wd, tok, cot, lens) + tuple(gains),
        [HBM] * 12,
        [HBM] * 7 + [VMEM] * 4,
        (128, 32),
        scratch,
        call_id=1,
    )


def add(*values):
    total = values[0].astype(jnp.float32)
    for value in values[1:]:
        total = total + value.astype(jnp.float32)
    return total


class Share:
    def __init__(self, me, run, src, dst):
        self.me, self.run, self.src, self.dst = me, run, src, dst

    def slot(self, z, x, y):
        return ((z * 2 + x) * 2 + self.me.core) * 2 + y

    def steps(self, cut):
        me, run, src, dst, slot = self.me, self.run, self.src, self.dst, self.slot
        low, middle, high = cut
        first, second, whole = slice(low, middle), slice(middle, high), slice(low, high)
        own = dst.at[slot(me.z, me.x, me.y)]
        run.later(src.at[whole], own.at[whole])
        from_z = [run.remote(src.at[whole], own.at[whole], me.along_z(k)) for k in range(1, me.n_z)]
        xa, xb, ya, yb, late_a, late_b = [], [], [], [], [], []

        def fan(k):
            here = dst.at[slot(me.z_before(k), me.x, me.y)]
            if k:
                run.arrive(from_z[k - 1])
            there = here if k else src
            xa.append(run.remote(there.at[first], here.at[first], me.across_x()))
            yb.append(run.remote(there.at[second], here.at[second], me.across_y()))
            ya.append(run.remote(there.at[first], here.at[first], me.across_y()))
            xb.append(run.remote(there.at[second], here.at[second], me.across_x()))
            run.remote(there.at[whole], here.at[whole], me.across_core())

        def relay(k):
            z = me.z_before(k)
            run.arrive(xa[k])
            part = dst.at[slot(z, 1 - me.x, me.y), first]
            late_a.append(run.remote(part, part, me.across_y()))
            run.arrive(yb[k])
            part = dst.at[slot(z, me.x, 1 - me.y), second]
            late_b.append(run.remote(part, part, me.across_x()))

        def hand_over(k):
            z = me.z_before(k)
            run.arrive(xb[k])
            part = dst.at[slot(z, 1 - me.x, me.y), whole]
            run.remote(part, part, me.across_core())
            run.arrive(ya[k])
            part = dst.at[slot(z, me.x, 1 - me.y), whole]
            run.remote(part, part, me.across_core())

        def hand_last(k):
            run.arrive(late_a[k], late_b[k])
            part = dst.at[slot(me.z_before(k), 1 - me.x, 1 - me.y), whole]
            run.remote(part, part, me.across_core())

        for i in range(me.n_z + 3):
            for lag, action in enumerate((fan, relay, hand_over, hand_last)):
                if 0 <= i - lag < me.n_z:
                    action(i - lag)
            yield


class ChipSum:
    def __init__(self, me, run, src, own, far, over):
        self.me, self.run, self.own, self.far, self.over = me, run, own, far, over
        self.sent = []
        for k in range(1, me.n_z + 1):
            z = me.z_after(k)
            self.sent.append(run.remote(src.at[z * 2 + 1 - me.x], far.at[z], me.across_x()))

    def steps(self, place):
        me, run = self.me, self.run
        along = []
        for k in range(1, me.n_z + 1):
            z = me.z_after(k)
            run.arrive(self.sent[k - 1])
            part = self.own(z)
            part[...] = add(part[...], self.far[z]).astype(jnp.bfloat16)
            if k < me.n_z:
                along.append(run.remote(part, self.over.at[k - 1], me.along_z(k)))
            yield
        run.arrive(*along)
        place(add(self.own(me.z)[...], *[self.over[k] for k in range(me.n_z - 1)]))
        yield


class QuadSum:
    def __init__(self, me, run, src, own, near, over):
        self.me, self.run, self.own, self.near, self.over = me, run, own, near, over
        self.src = src
        self.first = self.give(1 - me.y)
        self.second = self.give(me.y)

    def give(self, y):
        me = self.me
        return self.run.remote(self.src.at[2 * (1 - me.core) + y], self.near.at[y], me.across_core())

    def cross(self, step=128):
        me, own, near = self.me, self.own, self.near
        self.run.arrive(self.first)

        @pl.loop(0, self.over.shape[0], step=step)
        def _(i):
            rows = at(i, step, step)
            own[1 - me.y, rows, :] = add(own[1 - me.y, rows, :], near[1 - me.y, rows, :]).astype(jnp.bfloat16)

        self.over_y = self.run.remote(own.at[1 - me.y], self.over, me.across_y())

    def landed(self):
        self.run.arrive(self.second, self.over_y)

    def rows(self, rows):
        y = self.me.y
        return add(self.own[y, rows, :], self.near[y, rows, :], self.over[rows, :])


def head_back(qkv, o, lse, do, dqkv, sum_k, sum_v, g, head, heads, size, count, stops, slope):
    scale = size**-0.5
    start = g * count
    sum_k[...] = jnp.zeros_like(sum_k)
    sum_v[...] = jnp.zeros_like(sum_v)

    def columns(part):
        return slice((part * heads + head) * size, (part * heads + head + 1) * size)

    mine = columns(0)
    for first in range(0, count, 256):
        seen = first + 256
        here, past = slice(start + first, start + seen), slice(start, start + seen)
        allowed, bias = allowed_and_bias(first, 256, seen, stops, slope)
        query, keys = qkv[here, mine], qkv[past, columns(1)]
        s = times_transposed(query, keys) * scale + bias
        p = jnp.exp(jnp.where(allowed, s, NEVER) - lse[g, head, first:seen])
        grad = do[here, mine]
        dots = jnp.sum(grad.astype(jnp.float32) * o[here, mine].astype(jnp.float32), axis=-1, keepdims=True)
        sum_v[:seen] += inner_rows(p.astype(jnp.bfloat16), grad)
        ds = (p * (times_transposed(grad, qkv[past, columns(2)]) - dots)).astype(jnp.bfloat16)
        dqkv[here, mine] = (jnp.dot(ds, keys, preferred_element_type=jnp.float32) * scale).astype(jnp.bfloat16)
        sum_k[:seen] += inner_rows(ds, query)
    dqkv[start : start + count, columns(1)] = (sum_k[...] * scale).astype(jnp.bfloat16)
    dqkv[start : start + count, columns(2)] = sum_v[...].astype(jnp.bfloat16)


def norm_parts(values):
    mean = jnp.mean(values, axis=-1, keepdims=True)
    centred = values - mean
    variance = jnp.mean(centred * centred, axis=-1, keepdims=True)
    factor = lax.rsqrt(variance + EPS)
    return centred * factor, factor


def norm_back_rows(grad, unit, factor, gain):
    scaled = grad * gain
    centre = jnp.mean(scaled, axis=-1, keepdims=True)
    along = jnp.mean(scaled * unit, axis=-1, keepdims=True)
    return factor * (scaled - centre - unit * along)


def back_kernel(
    n_z,
    n_items,
    part_h2,
    part_out,
    part_down,
    part_up,
    MID,
    cot_in,
    tok_in,
    H1,
    QKV,
    O,
    LSE,
    WQ,
    WOQ,
    LQ,
    grad_b_up,
    attn_gain,
    ffn_gain,
    b_down,
    BLOCK_OUT,
    GRAD_TOKENS,
    SHARED,
    own_h2,
    near_h2,
    over_h2,
    own_out,
    near_out,
    over_out,
    own_down,
    far_down,
    over_down,
    own_up,
    far_up,
    over_up,
    middle,
    cot,
    tok,
    h1,
    qkv,
    o,
    lse,
    w_q,
    w_o,
    ends,
    grad_mid,
    branch,
    do,
    dqkv,
    sum_k,
    sum_v,
    acc_o,
    grad_q,
    far_q,
    over_q,
    grad_o,
    far_o,
    over_o,
    part_h1,
    near_h1,
    over_h1,
    small,
    slab,
    out_rows,
    send,
    recv,
    near,
):
    me = Place(n_z)
    run = Copies(send, recv, near)
    quarter = me.quarter
    other, beside, far = 2 * (1 - me.core) + me.y, 2 * me.core + 1 - me.y, 2 * (1 - me.core) + 1 - me.y
    low, f32 = jnp.bfloat16, jnp.float32
    chips = 2 * n_z
    local, width = tok_in.shape
    count, half = 2 * local, local // 2
    size = width // HEADS
    heads = HEADS // 4
    rows = part_down.shape[1]
    few = grad_o.shape[1]
    meet(
        [me.across_core(), me.across_x(), me.across_y()] + [me.along_z(k) for k in range(1, n_z)]
    )
    group = pl.ds(2 * me.core, 2)
    sum_h2 = QuadSum(me, run, part_h2, own_h2, near_h2, over_h2)
    load_h2 = run.local(part_h2.at[group], own_h2)
    down = ChipSum(me, run, part_down, lambda z: own_down.at[z], far_down, over_down)
    load_down = [run.local(part_down.at[z * 2 + me.x], own_down.at[z]) for z in range(n_z)]
    load_mid = [run.local(MID, middle), run.local(cot_in, cot)]
    up = ChipSum(me, run, part_up, lambda z: own_up.at[z], far_up, over_up)
    load_up = [run.local(part_up.at[z * 2 + me.x], own_up.at[z]) for z in range(n_z)]
    sum_out = QuadSum(me, run, part_out, own_out, near_out, over_out)
    load_out = run.local(part_out.at[group], own_out)
    load_heads = [
        run.local(a, b) for a, b in ((WOQ, w_o), (O, o), (QKV, qkv), (LSE, lse), (H1, h1), (WQ, w_q), (tok_in, tok), (LQ, ends))
    ]
    small[...] = jnp.zeros_like(small)
    small[5:6] = grad_b_up[...]
    acc_o[...] = jnp.zeros_like(acc_o)

    share = Share(me, run, slab, SHARED)

    def to_slab(start, columns=slice(None)):
        def place(value):
            slab[start : start + value.shape[0], columns] = value.astype(low)

        return place

    def place_o(value):
        step = width // (rows // few)
        for i in range(rows // few):
            slab[2 * rows + i * few : 2 * rows + (i + 1) * few, width - step :] = value[
                :, i * step : (i + 1) * step
            ].astype(low)

    def chain(total, place, cut):
        yield from total.steps(place)
        yield from share.steps(cut)

    run_down = chain(down, to_slab(0), (0, rows // 2, rows))
    run_up = chain(up, to_slab(rows), (rows, rows + rows // 2, 2 * rows))

    def pump(thread, times=1):
        for _ in range(times):
            next(thread, None)

    load_h2.wait()
    sum_h2.cross()
    for copy in load_down:
        copy.wait()
    pump(run_down, 4)
    for copy in load_mid:
        copy.wait()
    sum_h2.landed()

    @pl.loop(0, local, step=64)
    def _(i):
        here = at(i, 64, 64)
        unit, factor = norm_parts(middle[here, :])
        grad, c = sum_h2.rows(here), cot[here, :].astype(f32)
        total = c + norm_back_rows(grad, unit, factor, ffn_gain[...])
        grad_mid[here, :] = total
        branch[quarter, here, :] = total.astype(low)
        small[2:3] += jnp.sum(grad * unit, axis=0, keepdims=True)
        small[3:4] += jnp.sum(grad, axis=0, keepdims=True)
        small[4:5] += jnp.sum(c, axis=0, keepdims=True)

    own = branch.at[quarter]
    core_b = run.remote(own, own, me.across_core())
    over_b = []
    for h in range(2):
        part = branch.at[quarter, h * half : (h + 1) * half]
        over_b.append(run.remote(part, part, me.across_y()))
    for copy in load_up:
        copy.wait()
    pump(run_up)
    pump(run_down)
    pump(run_up)
    pump(run_down)
    for copy in load_heads:
        copy.wait()

    def project_back(block, start, size_b):
        @pl.loop(0, size_b, step=256)
        def _(i):
            here = at(start + i, 256, 256)
            there = at(block * local + start + i, 256, 256)
            values = branch[block, here, :]
            do[there, :] = times_transposed(values, w_o[...]).astype(low)
            acc_o[...] += inner_rows(o[there, :], values)

    project_back(quarter, 0, local)
    run.arrive(core_b)
    project_back(other, 0, local)
    pump(run_up)
    pump(run_down)
    pump(run_up)
    far_b = []
    for h in range(2):
        run.arrive(over_b[h])
        part = branch.at[beside, h * half : (h + 1) * half]
        far_b.append(run.remote(part, part, me.across_core()))
        project_back(beside, h * half, half)
        pump(run_down)
    pump(run_up)
    for h in range(2):
        run.arrive(far_b[h])
        project_back(far, h * half, half)
    load_out.wait()
    sum_out.cross()
    grad_o[...] = acc_o[...].reshape(chips, few, width).astype(low)
    total_o = ChipSum(me, run, grad_o, lambda z: grad_o.at[z * 2 + me.x], far_o, over_o)
    pump(run_up)
    for g in range(2):
        stops = []
        end = 0
        for item in range(n_items - 1):
            end = end + ends[g, 0, item]
            stops.append(end)
        for head in range(heads):
            slope = jnp.exp2(-(jnp.zeros((1, 1), f32) + (quarter * heads + head + 1)))
            head_back(qkv, o, lse, do, dqkv, sum_k, sum_v, g, head, heads, size, count, stops, slope)
            pump(run_down)
            pump(run_up)

    @pl.loop(0, chips // 2)
    def _(i):
        columns = at(i * 2 * rows, 2 * rows, 128)
        grad_q[pl.ds(2 * i, 2)] = (
            inner_rows(h1[:, columns], dqkv[...]).reshape(2, rows, dqkv.shape[1]).astype(low)
        )

    total_q = ChipSum(me, run, grad_q, lambda z: grad_q.at[z * 2 + me.x], far_q, over_q)

    def project_in(block):
        @pl.loop(0, local, step=256)
        def _(i):
            part_h1[block, at(i, 256, 256), :] = times_transposed(
                dqkv[at(block * local + i, 256, 256), :], w_q[...]
            ).astype(low)

    project_in(far)
    sum_h1 = QuadSum.__new__(QuadSum)
    sum_h1.me, sum_h1.run, sum_h1.src = me, run, part_h1
    sum_h1.own, sum_h1.near, sum_h1.over = part_h1.at[group], near_h1, over_h1
    sum_h1.first = sum_h1.give(1 - me.y)
    project_in(other)
    sum_h1.second = sum_h1.give(me.y)
    project_in(beside)
    sum_h1.cross()
    project_in(quarter)
    pump(run_down)
    pump(run_up)
    run_q = total_q.steps(to_slab(2 * rows, slice(0, dqkv.shape[1])))
    run_o = total_o.steps(place_o)
    pump(run_o, 4)
    pump(run_q, 4)
    pump(run_up, 3)
    pump(run_down, 12)
    sum_out.landed()

    @pl.loop(0, local, step=64)
    def _(i):
        here = at(i, 64, 64)
        out_rows[here, :] = (middle[here, :] + sum_out.rows(here) + b_down[...]).astype(low)

    run.later(out_rows, BLOCK_OUT)
    sum_h1.landed()

    @pl.loop(0, local, step=64)
    def _(i):
        here = at(i, 64, 64)
        unit, factor = norm_parts(tok[here, :].astype(f32))
        grad = sum_h1.rows(here)
        cot[here, :] = (grad_mid[here, :] + norm_back_rows(grad, unit, factor, attn_gain[...])).astype(low)
        small[0:1] += jnp.sum(grad * unit, axis=0, keepdims=True)
        small[1:2] += jnp.sum(grad, axis=0, keepdims=True)

    run.later(cot, GRAD_TOKENS)
    slab[3 * rows :, :] = small[...].astype(low)
    pump(run_o, 2)
    pump(run_q, 2)
    last = share.steps((2 * rows, 2 * rows + rows // 2, slab.shape[0]))
    pump(run_up, 12)
    pump(last, 12)
    run.finish()


def back(n_z, n_items, parts, mid, cot, tok, saved, lq, grad_b_up, attn_gain, ffn_gain, b_down):
    low, f32 = jnp.bfloat16, jnp.float32
    local, width = tok.shape
    chips = 2 * n_z
    heads, size = HEADS // 4, width // HEADS
    rows, ff = parts[2].shape[1:]
    few = width // 4 // chips
    cols = saved[1].shape[1]
    shape = jax.ShapeDtypeStruct
    block, piece = (local, width), (rows, ff)
    deep = 3 * rows + 16
    v = pltpu.VMEM
    scratch = (
        [v((2,) + block, low), v((2,) + block, low), v(block, low)] * 2
        + [v((n_z,) + piece, low), v((n_z,) + piece, low), v((n_z - 1,) + piece, low)] * 2
        + [v(block, f32), v(block, low), v(block, low)]
        + [v(value.shape, value.dtype) for value in saved]
        + [pltpu.SMEM(lq.shape, lq.dtype)]
        + [v(block, f32), v((4,) + block, low), v((4 * local, heads * size), low), v((4 * local, cols), low)]
        + [v((2 * local, size), f32)] * 2
        + [v((heads * size, width), f32)]
        + [v((chips, rows, cols), low), v((n_z, rows, cols), low), v((n_z - 1, rows, cols), low)]
        + [v((chips, few, width), low), v((n_z, few, width), low), v((n_z - 1, few, width), low)]
        + [v((4,) + block, low), v((2,) + block, low), v(block, low)]
        + [v((16, width), f32), v((deep, width), low), v(block, low)]
    )
    return communicate(
        functools.partial(back_kernel, n_z, n_items),
        [shape(block, low), shape(block, low), shape((4 * chips, deep, width), low)],
        tuple(parts) + (mid, cot, tok) + tuple(saved) + (lq, grad_b_up, attn_gain, ffn_gain, b_down),
        [HBM] * 3,
        [HBM] * (len(parts) + 3 + len(saved) + 1) + [VMEM] * 4,
        (200, 48),
        scratch,
        call_id=2,
        limit=62 << 20,
    )


def unfold_kernel(rows, head_cols, few, shared, down, up, qkv, out, small, bias):
    f32 = jnp.float32
    width = shared.shape[-1]
    chips = up.shape[1] // width * 2
    unit = width // chips
    third = qkv.shape[1] // 3

    @pl.when(pl.program_id(0) == 0)
    def _():
        small[...] = jnp.zeros_like(small)
        bias[...] = jnp.zeros_like(bias)

    for q in range(4):
        down[q * rows : (q + 1) * rows] = shared[q, :rows].astype(f32)
        for s in range(chips):
            start = (s * 4 + q) * unit
            up[:, start : start + unit] = shared[q, rows : 2 * rows, s * unit : (s + 1) * unit].astype(f32)
        for i in range(3):
            start = i * third + q * head_cols
            qkv[:, start : start + head_cols] = shared[
                q, 2 * rows : 3 * rows, i * head_cols : (i + 1) * head_cols
            ].astype(f32)
        tail = 3 * head_cols
        step = width - tail
        for i in range(rows // few):
            out[q, :, i * step : (i + 1) * step] = shared[
                q, 2 * rows + i * few : 2 * rows + (i + 1) * few, tail:
            ].astype(f32)
        extra = shared[q, 3 * rows :].astype(f32)
        small[...] += extra
        bias[q : q + 1] += extra[5:6]


def unfold(shared, rows, few, ff):
    devices, deep, width = shared.shape
    chips = devices // 4
    f32 = jnp.float32
    head_cols = width // 4
    return pl.pallas_call(
        functools.partial(unfold_kernel, rows, head_cols, few),
        grid=(chips,),
        in_specs=[pl.BlockSpec((4, deep, width), lambda s: (s, 0, 0))],
        out_specs=[
            pl.BlockSpec((4 * rows, width), lambda s: (s, 0)),
            pl.BlockSpec((rows, ff), lambda s: (s, 0)),
            pl.BlockSpec((rows, 3 * width), lambda s: (s, 0)),
            pl.BlockSpec((4, None, few, width), lambda s: (0, s, 0, 0)),
            pl.BlockSpec((deep - 3 * rows, width), lambda s: (0, 0)),
            pl.BlockSpec((4, width), lambda s: (0, 0)),
        ],
        out_shape=[
            jax.ShapeDtypeStruct((ff, width), f32),
            jax.ShapeDtypeStruct((width, ff), f32),
            jax.ShapeDtypeStruct((width, 3 * width), f32),
            jax.ShapeDtypeStruct((4, chips, few, width), f32),
            jax.ShapeDtypeStruct((deep - 3 * rows, width), f32),
            jax.ShapeDtypeStruct((4, width), f32),
        ],
        compiler_params=pltpu.CompilerParams(vmem_limit_bytes=56 << 20),
    )(shared)


def on_quad(
    tokens,
    lengths,
    attn_gain,
    attn_shift,
    w_qkv,
    w_out,
    ffn_gain,
    ffn_shift,
    w_up,
    b_up,
    w_down,
    b_down,
    cotangent,
):
    low = jnp.bfloat16
    local, width = tokens.shape
    n_dp = lax.axis_size("dp")
    n_z, chips = n_dp // 4, n_dp // 2
    size = width // HEADS
    heads = HEADS // 4
    count = 2 * local
    me = Place(n_z)
    lens = jnp.zeros((8, 128), jnp.int32).at[:1, : lengths.shape[1]].set(lengths)
    gains = [value.reshape(1, width) for value in (attn_gain, attn_shift, ffn_gain, ffn_shift)]
    WQ, WOQ, WU, WD, CQ, h1, qkv, o, lse, h2, middle, LQ = front(
        n_z, lengths.shape[1], w_qkv, w_out, w_up, w_down, tokens, cotangent, lens, gains
    )
    unit = w_up.shape[1] // chips // 4
    bias = lax.dynamic_index_in_dim(b_up.reshape(chips, 4, unit), me.quarter, 1, keepdims=False).reshape(-1)
    c = CQ.reshape(4 * local, width)
    pre = jnp.dot(h2, WU, preferred_element_type=jnp.float32) + bias
    act, pull = jax.vjp(smooth_act, pre)
    active = act.astype(low)
    grad_pre = pull(times_transposed(c, WD))[0]
    grad_pre_low = grad_pre.astype(low)
    part_out = jnp.dot(active, WD, preferred_element_type=jnp.float32).astype(low)
    part_h2 = times_transposed(grad_pre_low, WU).astype(low)
    part_down = inner_rows(active, c).astype(low)
    part_up = inner_rows(h2, grad_pre_low).astype(low)
    grad_b_up = jnp.sum(grad_pre, axis=0)
    parts = [
        part_h2.reshape(4, local, width),
        part_out.reshape(4, local, width),
        part_down.reshape(chips, -1, width),
        part_up.reshape(chips, -1, part_up.shape[1]),
    ]
    block_out, grad_tokens, shared = back(
        n_z,
        lengths.shape[1],
        parts,
        middle,
        cotangent,
        tokens,
        [h1.reshape(4 * local, width), qkv, o, lse, WQ, WOQ],
        LQ,
        grad_b_up.reshape(1, width),
        gains[0],
        gains[2],
        b_down.reshape(1, width),
    )
    rows, few = parts[2].shape[1], width // 4 // chips
    ff = w_up.shape[1]
    grad_w_down, grad_w_up, grad_w_qkv, grad_w_out, vectors, bias = unfold(shared, rows, few, ff)
    return (
        block_out,
        grad_tokens,
        vectors[0],
        vectors[1],
        grad_w_qkv,
        grad_w_out.reshape(width, width),
        vectors[2],
        vectors[3],
        grad_w_up,
        jnp.transpose(bias.reshape(4, chips, unit), (1, 0, 2)).reshape(ff),
        grad_w_down,
        vectors[4],
    )


def solution(mesh):
    n_dp, n_seq = mesh.shape["dp"], mesh.shape["seq"]
    quad = n_seq == 2 and n_dp % 4 == 0 and n_dp >= 8 and n_dp <= 16
    return jax.shard_map(
        on_quad if quad else on_device,
        mesh=mesh,
        in_specs=(
            P(("dp", "seq"), None),
            P("dp", None),
            P(),
            P(),
            P("dp", None),
            P("dp", None),
            P(),
            P(),
            P("dp", None),
            P(),
            P("dp", None),
            P(),
            P(("dp", "seq"), None),
        ),
        out_specs=(
            P(("dp", "seq"), None),
            P(("dp", "seq"), None),
            P(),
            P(),
            P(),
            P(),
            P(),
            P(),
            P(),
            P(),
            P(),
            P(),
        ),
        check_vma=False,
    )
```

```python
import functools

import jax
import jax.numpy as jnp
from jax import lax
from jax.experimental import pallas as pl
from jax.experimental.pallas import tpu as pltpu
from jax.sharding import PartitionSpec as P

HEADS = 8


EPS = 1e-05
NEVER = -1000000000.0


def inner_rows(left, right):
    return lax.dot_general(
        left, right, (((0,), (0,)), ((), ())), preferred_element_type=jnp.float32
    )


def times_transposed(left, right):
    return lax.dot_general(
        left, right, (((1,), (1,)), ((), ())), preferred_element_type=jnp.float32
    )


def smooth_act(values):
    return jax.nn.gelu(values, approximate=True)


def norm_forward(values, gain, shift):
    mean = jnp.mean(values, axis=-1, keepdims=True)
    centred = values - mean
    variance = jnp.mean(centred * centred, axis=-1, keepdims=True)
    factor = lax.rsqrt(variance + EPS)
    normed = centred * factor
    return (normed * gain + shift, normed, factor)


def norm_backward(grad_out, normed, factor, gain):
    grad_normed = grad_out * gain
    centre_term = jnp.mean(grad_normed, axis=-1, keepdims=True)
    along_term = jnp.mean(grad_normed * normed, axis=-1, keepdims=True)
    grad_in = factor * (grad_normed - centre_term - normed * along_term)
    return (grad_in, jnp.sum(grad_out * normed, axis=0), jnp.sum(grad_out, axis=0))


def item_ids(item_lengths, count):
    item_ends = jnp.cumsum(item_lengths, dtype=jnp.int32)
    places = jnp.arange(count, dtype=jnp.int32)
    hits = (places[:, None] >= item_ends[None, :]).astype(jnp.int32)
    return jnp.sum(hits, axis=1, dtype=jnp.int32)


def block_scores(query_block, keys, start, item_of, slopes):
    rows = query_block.shape[0]
    count = keys.shape[0]
    scale = query_block.shape[-1] ** (-0.5)
    raw = jnp.einsum("qhd,khd->hqk", query_block, keys, preferred_element_type=jnp.float32)
    row_places = start + jnp.arange(rows, dtype=jnp.int32)
    col_places = jnp.arange(count, dtype=jnp.int32)
    distance = (row_places[:, None] - col_places[None, :]).astype(jnp.float32)
    row_items = lax.dynamic_slice_in_dim(item_of, start, rows)
    allowed = (row_items[:, None] == item_of[None, :]) & (
        col_places[None, :] <= row_places[:, None]
    )
    scores = raw * scale - slopes[:, None, None] * distance[None]
    return jnp.where(allowed[None], scores, jnp.float32(-1000000000.0))


def attend(heads_qkv, item_of, slopes):
    count = heads_qkv.shape[0]
    rows = min(512, count)
    queries = heads_qkv[:, 0]
    keys = heads_qkv[:, 1]
    values = heads_qkv[:, 2]

    def one_block(index):
        start = index * rows
        query_block = lax.dynamic_slice_in_dim(queries, start, rows)
        scores = block_scores(query_block, keys, start, item_of, slopes)
        top = jnp.max(scores, axis=-1, keepdims=True)
        weights = jnp.exp(scores - top)
        total = jnp.sum(weights, axis=-1, keepdims=True)
        probs = (weights / total).astype(jnp.bfloat16)
        mixed = jnp.einsum("hqk,khd->qhd", probs, values, preferred_element_type=jnp.float32)
        return (mixed.astype(jnp.bfloat16), (top + jnp.log(total))[..., 0])

    mixed, log_norm = lax.map(one_block, jnp.arange(count // rows, dtype=jnp.int32))
    return (mixed.reshape(count, mixed.shape[2], mixed.shape[3]), log_norm)


def attend_back(heads_qkv, heads_out, grad_heads, log_norm, item_of, slopes):
    count = heads_qkv.shape[0]
    rows = min(512, count)
    queries = heads_qkv[:, 0]
    keys = heads_qkv[:, 1]
    values = heads_qkv[:, 2]
    scale = queries.shape[-1] ** (-0.5)
    row_dots = jnp.sum(grad_heads.astype(jnp.float32) * heads_out.astype(jnp.float32), axis=-1)

    def one_block(carry, index):
        grad_keys, grad_values = carry
        start = index * rows
        query_block = lax.dynamic_slice_in_dim(queries, start, rows)
        grad_block = lax.dynamic_slice_in_dim(grad_heads, start, rows)
        dots = lax.dynamic_slice_in_dim(row_dots, start, rows)
        scores = block_scores(query_block, keys, start, item_of, slopes)
        probs = jnp.exp(scores - log_norm[index][:, :, None])
        probs_low = probs.astype(jnp.bfloat16)
        grad_values = grad_values + jnp.einsum(
            "hqk,qhd->khd", probs_low, grad_block, preferred_element_type=jnp.float32
        )
        grad_probs = jnp.einsum(
            "qhd,khd->hqk", grad_block, values, preferred_element_type=jnp.float32
        )
        grad_scores = (probs * (grad_probs - jnp.transpose(dots)[:, :, None])).astype(jnp.bfloat16)
        grad_query = (
            jnp.einsum("hqk,khd->qhd", grad_scores, keys, preferred_element_type=jnp.float32)
            * scale
        )
        grad_keys = (
            grad_keys
            + jnp.einsum(
                "hqk,qhd->khd", grad_scores, query_block, preferred_element_type=jnp.float32
            )
            * scale
        )
        return ((grad_keys, grad_values), grad_query)

    empty = jnp.zeros(keys.shape, jnp.float32)
    (grad_keys, grad_values), grad_query = lax.scan(
        one_block, (empty, empty), jnp.arange(count // rows, dtype=jnp.int32)
    )
    grad_query = grad_query.reshape(keys.shape)
    return jnp.stack([grad_query, grad_keys, grad_values], axis=1).astype(jnp.bfloat16)


def on_device(
    tokens,
    lengths,
    attn_gain,
    attn_shift,
    w_qkv,
    w_out,
    ffn_gain,
    ffn_shift,
    w_up,
    b_up,
    w_down,
    b_down,
    cotangent,
):
    w_qkv, w_out, w_up, w_down = (
        lax.all_gather(w_qkv, "dp", axis=0, tiled=True),
        lax.all_gather(w_out, "dp", axis=0, tiled=True),
        lax.all_gather(w_up, "dp", axis=0, tiled=True),
        lax.all_gather(w_down, "dp", axis=0, tiled=True),
    )
    local, width = tokens.shape
    groups = lax.axis_size("seq")
    per_head = width // HEADS
    local_heads = HEADS // groups
    count = local * groups
    item_of = item_ids(lengths[0], count)
    first_head = lax.axis_index("seq") * local_heads
    exponents = (first_head + jnp.arange(local_heads, dtype=jnp.int32) + 1).astype(jnp.float32)
    slopes = jnp.exp2(-exponents)
    inputs = tokens.astype(jnp.float32)
    normed_in, unit_in, factor_in = norm_forward(inputs, attn_gain, attn_shift)
    first_in = normed_in.astype(jnp.bfloat16)
    projected = jnp.dot(first_in, w_qkv, preferred_element_type=jnp.float32).astype(jnp.bfloat16)
    projected = projected.reshape(local, 3, HEADS, per_head)
    heads_qkv = lax.all_to_all(projected, "seq", split_axis=2, concat_axis=0, tiled=True)
    heads_out, log_norm = attend(heads_qkv, item_of, slopes)
    joined = lax.all_to_all(heads_out, "seq", split_axis=0, concat_axis=1, tiled=True).reshape(
        local, width
    )
    middle = inputs + jnp.dot(joined, w_out, preferred_element_type=jnp.float32)
    normed_mid, unit_mid, factor_mid = norm_forward(middle, ffn_gain, ffn_shift)
    second_in = normed_mid.astype(jnp.bfloat16)
    pre_act = jnp.dot(second_in, w_up, preferred_element_type=jnp.float32) + b_up
    act_value, act_pull = jax.vjp(smooth_act, pre_act)
    active = act_value.astype(jnp.bfloat16)
    block_out = (
        middle + jnp.dot(active, w_down, preferred_element_type=jnp.float32) + b_down
    ).astype(jnp.bfloat16)
    grad_out = cotangent.astype(jnp.float32)
    grad_b_down = jnp.sum(grad_out, axis=0)
    grad_w_down = inner_rows(active, cotangent)
    grad_active = times_transposed(cotangent, w_down)
    grad_pre = act_pull(grad_active)[0]
    grad_b_up = jnp.sum(grad_pre, axis=0)
    grad_pre_low = grad_pre.astype(jnp.bfloat16)
    grad_w_up = inner_rows(second_in, grad_pre_low)
    grad_second = times_transposed(grad_pre_low, w_up)
    grad_mid_norm, grad_ffn_gain, grad_ffn_shift = norm_backward(
        grad_second, unit_mid, factor_mid, ffn_gain
    )
    grad_middle = grad_out + grad_mid_norm
    grad_branch = grad_middle.astype(jnp.bfloat16)
    grad_w_out = inner_rows(joined, grad_branch)
    grad_joined = (
        times_transposed(grad_branch, w_out).astype(jnp.bfloat16).reshape(local, HEADS, per_head)
    )
    grad_heads = lax.all_to_all(grad_joined, "seq", split_axis=1, concat_axis=0, tiled=True)
    grad_qkv_heads = attend_back(heads_qkv, heads_out, grad_heads, log_norm, item_of, slopes)
    grad_projected = lax.all_to_all(
        grad_qkv_heads, "seq", split_axis=0, concat_axis=2, tiled=True
    ).reshape(local, 3 * width)
    grad_w_qkv = inner_rows(first_in, grad_projected)
    grad_first = times_transposed(grad_projected, w_qkv)
    grad_in_norm, grad_attn_gain, grad_attn_shift = norm_backward(
        grad_first, unit_in, factor_in, attn_gain
    )
    grad_tokens = (grad_middle + grad_in_norm).astype(jnp.bfloat16)
    all_part = (
        lax.psum_scatter(
            grad_attn_gain.astype(jnp.bfloat16), "dp", scatter_dimension=0, tiled=True
        ).astype(jnp.float32),
        lax.psum_scatter(
            grad_attn_shift.astype(jnp.bfloat16), "dp", scatter_dimension=0, tiled=True
        ).astype(jnp.float32),
        lax.psum_scatter(
            grad_w_qkv.astype(jnp.bfloat16), "dp", scatter_dimension=0, tiled=True
        ).astype(jnp.float32),
        lax.psum_scatter(
            grad_w_out.astype(jnp.bfloat16), "dp", scatter_dimension=0, tiled=True
        ).astype(jnp.float32),
        lax.psum_scatter(
            grad_ffn_gain.astype(jnp.bfloat16), "dp", scatter_dimension=0, tiled=True
        ).astype(jnp.float32),
        lax.psum_scatter(
            grad_ffn_shift.astype(jnp.bfloat16), "dp", scatter_dimension=0, tiled=True
        ).astype(jnp.float32),
        lax.psum_scatter(
            grad_w_up.astype(jnp.bfloat16), "dp", scatter_dimension=0, tiled=True
        ).astype(jnp.float32),
        lax.psum_scatter(
            grad_b_up.astype(jnp.bfloat16), "dp", scatter_dimension=0, tiled=True
        ).astype(jnp.float32),
        lax.psum_scatter(
            grad_w_down.astype(jnp.bfloat16), "dp", scatter_dimension=0, tiled=True
        ).astype(jnp.float32),
        lax.psum_scatter(
            grad_b_down.astype(jnp.bfloat16), "dp", scatter_dimension=0, tiled=True
        ).astype(jnp.float32),
    )
    all_part = (
        lax.psum(all_part[0].astype(jnp.bfloat16), "seq").astype(jnp.float32),
        lax.psum(all_part[1].astype(jnp.bfloat16), "seq").astype(jnp.float32),
        lax.psum(all_part[2].astype(jnp.bfloat16), "seq").astype(jnp.float32),
        lax.psum(all_part[3].astype(jnp.bfloat16), "seq").astype(jnp.float32),
        lax.psum(all_part[4].astype(jnp.bfloat16), "seq").astype(jnp.float32),
        lax.psum(all_part[5].astype(jnp.bfloat16), "seq").astype(jnp.float32),
        lax.psum(all_part[6].astype(jnp.bfloat16), "seq").astype(jnp.float32),
        lax.psum(all_part[7].astype(jnp.bfloat16), "seq").astype(jnp.float32),
        lax.psum(all_part[8].astype(jnp.bfloat16), "seq").astype(jnp.float32),
        lax.psum(all_part[9].astype(jnp.bfloat16), "seq").astype(jnp.float32),
    )
    summed = (
        lax.all_gather(all_part[0].astype(jnp.bfloat16), "dp", axis=0, tiled=True).astype(
            jnp.float32
        ),
        lax.all_gather(all_part[1].astype(jnp.bfloat16), "dp", axis=0, tiled=True).astype(
            jnp.float32
        ),
        lax.all_gather(all_part[2].astype(jnp.bfloat16), "dp", axis=0, tiled=True).astype(
            jnp.float32
        ),
        lax.all_gather(all_part[3].astype(jnp.bfloat16), "dp", axis=0, tiled=True).astype(
            jnp.float32
        ),
        lax.all_gather(all_part[4].astype(jnp.bfloat16), "dp", axis=0, tiled=True).astype(
            jnp.float32
        ),
        lax.all_gather(all_part[5].astype(jnp.bfloat16), "dp", axis=0, tiled=True).astype(
            jnp.float32
        ),
        lax.all_gather(all_part[6].astype(jnp.bfloat16), "dp", axis=0, tiled=True).astype(
            jnp.float32
        ),
        lax.all_gather(all_part[7].astype(jnp.bfloat16), "dp", axis=0, tiled=True).astype(
            jnp.float32
        ),
        lax.all_gather(all_part[8].astype(jnp.bfloat16), "dp", axis=0, tiled=True).astype(
            jnp.float32
        ),
        lax.all_gather(all_part[9].astype(jnp.bfloat16), "dp", axis=0, tiled=True).astype(
            jnp.float32
        ),
    )
    return (
        block_out,
        grad_tokens,
        summed[0],
        summed[1],
        summed[2],
        summed[3],
        summed[4],
        summed[5],
        summed[6],
        summed[7],
        summed[8],
        summed[9],
    )


MESH = pl.DeviceIdType.MESH


class Place:
    def __init__(self, n_z):
        dp = lax.axis_index("dp")
        self.n_z = n_z
        self.dp = dp
        self.y = lax.axis_index("seq")
        self.core = dp % 2
        self.chip = dp // 2
        self.x = self.chip % 2
        self.z = self.chip // 2
        self.quarter = 2 * self.core + self.y

    def device(self, z=None, x=None, core=None, y=None):
        z = self.z if z is None else z
        x = self.x if x is None else x
        core = self.core if core is None else core
        y = self.y if y is None else y
        return ((z * 2 + x) * 2 + core, y)

    def across_core(self):
        return self.device(core=1 - self.core)

    def across_x(self):
        return self.device(x=1 - self.x)

    def across_y(self):
        return self.device(y=1 - self.y)

    def z_after(self, k):
        return (self.z + k) % self.n_z

    def z_before(self, k):
        return (self.z + self.n_z - k) % self.n_z

    def along_z(self, k):
        return self.device(z=self.z_after(k))


class Copy:
    def __init__(self, copy, sends, lands):
        self.copy, self.sends, self.lands, self.landed = copy, sends, lands, False

    def guarded(self, condition, action):
        if condition is None:
            action()
        else:
            pl.when(condition)(action)


class Copies:
    def __init__(self, send, recv, near):
        self.send, self.recv, self.near = send, recv, near
        self.all, self.n, self.m, self.local_open = [], 0, 0, []

    def remote(self, src, dst, device, sends=None, lands=None):
        copy = Copy(
            pltpu.make_async_remote_copy(
                src_ref=src,
                dst_ref=dst,
                send_sem=self.send.at[self.n],
                recv_sem=self.recv.at[self.n],
                device_id=device,
                device_id_type=MESH,
            ),
            sends,
            lands,
        )
        self.n += 1
        copy.guarded(sends, copy.copy.start)
        self.all.append(copy)
        return copy

    def local(self, src, dst):
        copy = pltpu.make_async_copy(src, dst, self.near.at[self.m])
        self.m += 1
        copy.start()
        return copy

    def later(self, src, dst):
        self.local_open.append(self.local(src, dst))

    def arrive(self, *copies):
        for copy in copies:
            if not copy.landed:
                copy.guarded(copy.lands, copy.copy.wait_recv)
                copy.landed = True

    def finish(self):
        self.arrive(*self.all)
        for copy in self.all:
            copy.guarded(copy.sends, copy.copy.wait_send)
        for copy in self.local_open:
            copy.wait()


class Line:
    def __init__(self, me, run, own, view):
        self.me, self.run, self.view = me, run, view
        n, z = me.n_z, me.z
        self.up = [run.remote(own, view(z), me.device(z=z + 1), z < n - 1, z > 0)]
        self.down = [run.remote(own, view(z), me.device(z=z - 1), z > 0, z < n - 1)]

    def step(self, t, then):
        me, run, n, z = self.me, self.run, self.me.n_z, self.me.z
        if t >= n:
            return
        run.arrive(self.up[t - 1])
        if t < n - 1:
            part = self.view(z - t)
            self.up.append(run.remote(part, part, me.device(z=z + 1), (z >= t) & (z < n - 1), z > t))
        then(z - t, z >= t)
        run.arrive(self.down[t - 1])
        if t < n - 1:
            part = self.view(z + t)
            self.down.append(
                run.remote(part, part, me.device(z=z - 1), (z < n - t) & (z > 0), z < n - t - 1)
            )
        then(z + t, z < n - t)


def meet(devices):
    barrier = pltpu.get_barrier_semaphore()
    for device in devices:
        pl.semaphore_signal(barrier, inc=1, device_id=device, device_id_type=MESH)
    pl.semaphore_wait(barrier, len(devices))


def at(start, size, unit):
    return pl.ds(pl.multiple_of(start, unit), size)


def communicate(kernel, out_shapes, ins, out_specs, in_specs, counts, scratch=(), call_id=0, limit=None):
    return pl.pallas_call(
        kernel,
        out_shape=out_shapes,
        in_specs=in_specs,
        out_specs=out_specs,
        scratch_shapes=list(scratch)
        + [
            pltpu.SemaphoreType.DMA((counts[0],)),
            pltpu.SemaphoreType.DMA((counts[0],)),
            pltpu.SemaphoreType.DMA((counts[1],)),
        ],
        compiler_params=pltpu.CompilerParams(
            collective_id=call_id, has_side_effects=True, vmem_limit_bytes=limit or (56 << 20)
        ),
    )(*ins)


HBM = pl.BlockSpec(memory_space=pltpu.HBM)
VMEM = pl.BlockSpec(memory_space=pltpu.VMEM)
SMEM = pl.BlockSpec(memory_space=pltpu.SMEM)


def allowed_and_bias(first, rows, count, ends, slope):
    row = first + lax.broadcasted_iota(jnp.int32, (rows, 1), 0)
    col = lax.broadcasted_iota(jnp.int32, (1, count), 1)
    begin = jnp.zeros((rows, 1), jnp.int32)
    for end in ends:
        begin = jnp.where(row >= end, end, begin)
    allowed = (col >= begin) & (col <= row)
    bias = slope * (col - first).astype(jnp.float32)
    return allowed, bias


def norm_rows(values, gain, shift):
    mean = jnp.mean(values, axis=-1, keepdims=True)
    centred = values - mean
    variance = jnp.mean(centred * centred, axis=-1, keepdims=True)
    return centred * lax.rsqrt(variance + EPS) * gain + shift


def norm_block(src, dst, gain, shift, step=64):
    @pl.loop(0, src.shape[0], step=step)
    def _(i):
        rows = at(i, step, step)
        dst[rows, :] = norm_rows(src[rows, :].astype(jnp.float32), gain[...], shift[...]).astype(dst.dtype)


def front_kernel(
    n_z,
    n_items,
    wq,
    wo,
    wu,
    wd,
    tok,
    cot,
    lens,
    attn_gain,
    attn_shift,
    ffn_gain,
    ffn_shift,
    WQ,
    WOQ,
    WU,
    WD,
    CQ,
    H1,
    QKV,
    O,
    LSE,
    H2,
    MID,
    LQ,
    q_all,
    o_all,
    x_all,
    h1,
    qkv,
    mixed,
    lse,
    h2,
    middle,
    ends,
    send,
    recv,
    near,
):
    me = Place(n_z)
    run = Copies(send, recv, near)
    quarter, other = me.quarter, 2 * (1 - me.core) + me.y
    rows = wq.shape[0]
    third = wq.shape[1] // 3
    cut = third // 4
    chips = 2 * n_z
    span = wu.shape[1] // chips
    unit = span // 4
    local = tok.shape[0]
    count = 2 * local
    half = local // 2
    size = third // HEADS
    heads = HEADS // 4
    meet(
        [me.across_core(), me.across_x(), me.across_y()] + [me.along_z(k) for k in range(1, n_z)]
    )
    mine = at(me.dp * rows, rows, 16)

    into = [q_all.at[mine, p * cut : (p + 1) * cut] for p in range(3)]
    near_q = [run.local(wq.at[:, at(p * third + quarter * cut, cut, 128)], into[p]) for p in range(3)]
    core_q = [
        run.remote(wq.at[:, at(p * third + other * cut, cut, 128)], into[p], me.across_core())
        for p in range(3)
    ]
    keep_x = run.local(tok, x_all.at[quarter])
    keep_lens = run.local(lens, LQ.at[me.core])
    core_lens = run.remote(lens, LQ.at[me.core], me.across_core())

    def halves(h):
        return slice(h * half, (h + 1) * half)

    over_x = [
        run.remote(tok.at[halves(h)], x_all.at[quarter, halves(h)], me.across_y()) for h in range(2)
    ]
    core_x = run.remote(tok, x_all.at[quarter], me.across_core())
    into = [WU.at[mine, s * unit : (s + 1) * unit] for s in range(chips)]
    near_u = [run.local(wu.at[:, at(s * span + quarter * unit, unit, 128)], into[s]) for s in range(chips)]
    core_u = [
        run.remote(wu.at[:, at(s * span + other * unit, unit, 128)], into[s], me.across_core())
        for s in range(chips)
    ]

    def pairs_of(array):
        return lambda z, x=me.x: array.at[at((z * 2 + x) * 2 * rows, 2 * rows, 16)]

    def shard_of(z, x=me.x):
        return o_all.at[at(((z * 2 + x) * 2 + me.core) * rows, rows, 16)]

    def units_of(z, x=me.x):
        return WD.at[at((z * 2 + x) * unit, unit, 16)]

    from_x = {"q": [], "o": [], "u": [], "d": []}
    share_o = []

    def across(name, view):
        def then(z, came):
            part = view(z)
            from_x[name].append((run.remote(part, part, me.across_x(), came, came), z, came))
            if name == "o":
                share_o.append(run.remote(part, part, me.across_core(), came, came))

        return then

    for copy in near_q:
        copy.wait()
    run.arrive(*core_q)
    view_q, view_u = pairs_of(q_all), pairs_of(WU)
    line_q = Line(me, run, view_q(me.z), view_q)
    across("q", view_q)(me.z, None)
    line_o = Line(me, run, wo, shard_of)
    from_x["o"].append((run.remote(wo, shard_of(me.z), me.across_x()), me.z, None))
    share_o.append(run.remote(wo, shard_of(me.z), me.across_core()))
    keep_o = run.local(wo, shard_of(me.z))
    keep_x.wait()
    norm_block(x_all.at[quarter], h1.at[quarter], attn_gain, attn_shift)
    for copy in near_u:
        copy.wait()
    run.arrive(*core_u)
    line_u = Line(me, run, view_u(me.z), view_u)
    across("u", view_u)(me.z, None)
    own = wd.at[at(me.y * unit, unit, 16)]
    line_d = Line(me, run, own, units_of)
    from_x["d"].append((run.remote(own, units_of(me.z), me.across_x()), me.z, None))
    run.later(own, units_of(me.z))
    run.later(cot, CQ.at[quarter])
    run.remote(cot, CQ.at[quarter], me.across_core())
    run.arrive(core_x)
    norm_block(x_all.at[other], h1.at[other], attn_gain, attn_shift)
    line_q.step(1, across("q", view_q))
    beside = 2 * me.core + 1 - me.y
    far = 2 * (1 - me.core) + 1 - me.y
    far_x = []
    for h in range(2):
        run.arrive(over_x[h])
        part = x_all.at[beside, halves(h)]
        far_x.append(run.remote(part, part, me.across_core()))
        norm_block(x_all.at[beside, halves(h)], h1.at[beside, halves(h)], attn_gain, attn_shift)
        line_q.step(2 + h, across("q", view_q))
    over_c = [run.remote(cot.at[halves(0)], CQ.at[quarter, halves(0)], me.across_y())]
    for h in range(2):
        run.arrive(far_x[h])
        norm_block(x_all.at[far, halves(h)], h1.at[far, halves(h)], attn_gain, attn_shift)
    line_o.step(1, across("o", shard_of))
    run.later(h1, H1)
    for copy, _, _ in from_x["q"]:
        run.arrive(copy)
    run.later(q_all, WQ)

    @pl.loop(0, 4 * local, step=256)
    def _(i):
        block = at(i, 256, 256)
        qkv[block, :] = jnp.dot(
            h1[i // local, at(i % local, 256, 256), :], q_all[...], preferred_element_type=jnp.float32
        ).astype(jnp.bfloat16)

    run.later(qkv, QKV)
    keep_lens.wait()
    run.arrive(core_lens)
    fetch = run.local(LQ, ends)
    fetch.wait()

    def heads_at(owner, head):
        return at(owner * heads * size + head * size, size, 128)

    over_o, near_o = [], []
    pumps = [
        lambda: line_o.step(2, across("o", shard_of)),
        lambda: line_o.step(3, across("o", shard_of)),
        lambda: line_u.step(1, across("u", view_u)),
        lambda: line_u.step(2, across("u", view_u)),
    ]
    for g in range(2):
        stops = []
        total = 0
        for item in range(n_items - 1):
            total = total + ends[g, 0, item]
            stops.append(total)
        for head in range(heads):
            slope = jnp.exp2(-(jnp.zeros((1, 1), jnp.float32) + (quarter * heads + head + 1)))
            column = heads_at(quarter, head)
            for first in range(0, count, 256):
                start, seen = g * count, first + 256
                here = slice(start + first, start + seen)
                allowed, bias = allowed_and_bias(first, 256, seen, stops, slope)
                keys = qkv[start : start + seen, (heads + head) * size : (heads + head + 1) * size]
                s = times_transposed(qkv[here, head * size : (head + 1) * size], keys) * size**-0.5 + bias
                s = jnp.where(allowed, s, NEVER)
                top = jnp.max(s, axis=-1, keepdims=True)
                w = jnp.exp(s - top)
                sum_w = jnp.sum(w, axis=-1, keepdims=True)
                p = (w * (1.0 / sum_w)).astype(jnp.bfloat16)
                values = qkv[start : start + seen, (2 * heads + head) * size : (2 * heads + head + 1) * size]
                mixed[here, column] = jnp.dot(p, values, preferred_element_type=jnp.float32).astype(
                    jnp.bfloat16
                )
                lse[g, head, first:seen] = top + jnp.log(sum_w)
            part = mixed.at[g * count : (g + 1) * count, column]
            over_o.append(run.remote(part, part, me.across_y()))
            near_o.append(run.remote(part, part, me.across_core()))
            pumps[g * heads + head]()
    run.later(mixed.at[:, at(quarter * heads * size, heads * size, 128)], O)
    run.later(lse, LSE)
    over_c.append(run.remote(cot.at[halves(1)], CQ.at[quarter, halves(1)], me.across_y()))
    run.arrive(over_c[0])
    part = CQ.at[beside, halves(0)]
    run.remote(part, part, me.across_core())
    far_o = []
    for copy, z, came in from_x["o"]:
        run.arrive(copy)
        part = shard_of(z, 1 - me.x)
        far_o.append(run.remote(part, part, me.across_core(), came, came))
    line_u.step(3, across("u", view_u))
    passed = []
    for g in range(2):
        for head in range(heads):
            run.arrive(over_o[g * heads + head])
            part = mixed.at[g * count : (g + 1) * count, heads_at(beside, head)]
            passed.append(run.remote(part, part, me.across_core()))
    line_d.step(1, across("d", units_of))
    keep_o.wait()
    run.arrive(*share_o, *far_o)
    run.later(o_all.at[at(quarter * heads * size, heads * size, 16)], WOQ)
    for g in range(2):
        run.arrive(*near_o[g * heads : (g + 1) * heads], *passed[g * heads : (g + 1) * heads])

        @pl.loop(0, count, step=256)
        def _(i):
            block = at(g * count + i, 256, 256)
            owner, inner = 2 * g + i // local, at(i % local, 256, 256)
            x1 = x_all[owner, inner, :].astype(jnp.float32) + jnp.dot(
                mixed[block, :], o_all[...], preferred_element_type=jnp.float32
            )
            h2[block, :] = norm_rows(x1, ffn_gain[...], ffn_shift[...]).astype(jnp.bfloat16)

            @pl.when(owner == quarter)
            def _():
                middle[inner, :] = x1

        line_d.step(2 + g, across("d", units_of))
    run.later(h2, H2)
    run.later(middle, MID)
    run.arrive(over_c[1])
    part = CQ.at[beside, halves(1)]
    run.remote(part, part, me.across_core())
    run.finish()


def front(n_z, n_items, wq, wo, wu, wd, tok, cot, lens, gains):
    width, low, f32 = wq.shape[0] * 4 * n_z, jnp.bfloat16, jnp.float32
    quarter_ff = wu.shape[1] // 4
    local = tok.shape[0]
    heads, size = HEADS // 4, width // HEADS
    shape = jax.ShapeDtypeStruct
    shapes = [
        shape((width, wq.shape[1] // 4), low),
        shape((width // 4, width), low),
        shape((width, quarter_ff), low),
        shape((quarter_ff, width), low),
        shape((4, local, width), low),
        shape((4, local, width), low),
        shape((4 * local, 3 * width // 4), low),
        shape((4 * local, width // 4), low),
        shape((2, heads, 2 * local, 1), f32),
        shape((4 * local, width), low),
        shape((local, width), f32),
        shape((2,) + lens.shape, lens.dtype),
    ]
    scratch = [
        pltpu.VMEM((width, wq.shape[1] // 4), low),
        pltpu.VMEM((width, width), low),
        pltpu.VMEM((4, local, width), low),
        pltpu.VMEM((4, local, width), low),
        pltpu.VMEM((4 * local, 3 * width // 4), low),
        pltpu.VMEM((4 * local, width), low),
        pltpu.VMEM((2, heads, 2 * local, 1), f32),
        pltpu.VMEM((4 * local, width), low),
        pltpu.VMEM((local, width), f32),
        pltpu.SMEM((2,) + lens.shape, lens.dtype),
    ]
    return communicate(
        functools.partial(front_kernel, n_z, n_items),
        shapes,
        (wq, wo, wu, wd, tok, cot, lens) + tuple(gains),
        [HBM] * 12,
        [HBM] * 7 + [VMEM] * 4,
        (128, 32),
        scratch,
        call_id=1,
    )


def add(*values):
    total = values[0].astype(jnp.float32)
    for value in values[1:]:
        total = total + value.astype(jnp.float32)
    return total


class Share:
    def __init__(self, me, run, src, dst):
        self.me, self.run, self.src, self.dst = me, run, src, dst

    def slot(self, z, x, y):
        return ((z * 2 + x) * 2 + self.me.core) * 2 + y

    def steps(self, cut):
        me, run, src, dst, slot = self.me, self.run, self.src, self.dst, self.slot
        low, middle, high = cut
        first, second, whole = slice(low, middle), slice(middle, high), slice(low, high)
        own = dst.at[slot(me.z, me.x, me.y)]
        run.later(src.at[whole], own.at[whole])
        from_z = [run.remote(src.at[whole], own.at[whole], me.along_z(k)) for k in range(1, me.n_z)]
        xa, xb, ya, yb, late_a, late_b = [], [], [], [], [], []

        def fan(k):
            here = dst.at[slot(me.z_before(k), me.x, me.y)]
            if k:
                run.arrive(from_z[k - 1])
            there = here if k else src
            xa.append(run.remote(there.at[first], here.at[first], me.across_x()))
            yb.append(run.remote(there.at[second], here.at[second], me.across_y()))
            ya.append(run.remote(there.at[first], here.at[first], me.across_y()))
            xb.append(run.remote(there.at[second], here.at[second], me.across_x()))
            run.remote(there.at[whole], here.at[whole], me.across_core())

        def relay(k):
            z = me.z_before(k)
            run.arrive(xa[k])
            part = dst.at[slot(z, 1 - me.x, me.y), first]
            late_a.append(run.remote(part, part, me.across_y()))
            run.arrive(yb[k])
            part = dst.at[slot(z, me.x, 1 - me.y), second]
            late_b.append(run.remote(part, part, me.across_x()))

        def hand_over(k):
            z = me.z_before(k)
            run.arrive(xb[k])
            part = dst.at[slot(z, 1 - me.x, me.y), whole]
            run.remote(part, part, me.across_core())
            run.arrive(ya[k])
            part = dst.at[slot(z, me.x, 1 - me.y), whole]
            run.remote(part, part, me.across_core())

        def hand_last(k):
            run.arrive(late_a[k], late_b[k])
            part = dst.at[slot(me.z_before(k), 1 - me.x, 1 - me.y), whole]
            run.remote(part, part, me.across_core())

        for i in range(me.n_z + 3):
            for lag, action in enumerate((fan, relay, hand_over, hand_last)):
                if 0 <= i - lag < me.n_z:
                    action(i - lag)
            yield


class ChipSum:
    def __init__(self, me, run, src, own, far, over):
        self.me, self.run, self.src, self.own, self.far, self.over = me, run, src, own, far, over
        self.sent = []

    def send(self, times=1):
        for _ in range(times):
            z = self.me.z_after(len(self.sent) + 1)
            piece = self.src.at[z * 2 + 1 - self.me.x]
            self.sent.append(self.run.remote(piece, self.far.at[z], self.me.across_x()))

    def steps(self, place, then=None):
        me, run = self.me, self.run
        along = []
        for k in range(1, me.n_z + 1):
            z = me.z_after(k)
            run.arrive(self.sent[k - 1])
            if then is not None:
                then()
            part = self.own(z)
            part[...] = add(part[...], self.far[z]).astype(jnp.bfloat16)
            if k < me.n_z:
                along.append(run.remote(part, self.over.at[k - 1], me.along_z(k)))
            yield
        run.arrive(*along)
        place(add(self.own(me.z)[...], *[self.over[k] for k in range(me.n_z - 1)]))
        yield


class QuadSum:
    def __init__(self, me, run, src, own, near, over):
        self.me, self.run, self.own, self.near, self.over = me, run, own, near, over
        self.src, self.given = src, []

    def start(self, y):
        me = self.me
        self.given.append(self.run.remote(self.src.at[2 * (1 - me.core) + y], self.near.at[y], me.across_core()))

    def cross(self, step=128):
        me, own, near = self.me, self.own, self.near
        self.run.arrive(self.given[0])

        @pl.loop(0, self.over.shape[0], step=step)
        def _(i):
            rows = at(i, step, step)
            own[1 - me.y, rows, :] = add(own[1 - me.y, rows, :], near[1 - me.y, rows, :]).astype(jnp.bfloat16)

        self.over_y = self.run.remote(own.at[1 - me.y], self.over, me.across_y())

    def landed(self):
        self.run.arrive(self.given[1], self.over_y)

    def rows(self, rows):
        y = self.me.y
        return add(self.own[y, rows, :], self.near[y, rows, :], self.over[rows, :])


def head_back(qkv, o, lse, do, dqkv, sum_k, sum_v, g, head, heads, size, count, stops, slope):
    scale = size**-0.5
    start = g * count
    sum_k[...] = jnp.zeros_like(sum_k)
    sum_v[...] = jnp.zeros_like(sum_v)

    def columns(part):
        return slice((part * heads + head) * size, (part * heads + head + 1) * size)

    mine = columns(0)
    for first in range(0, count, 256):
        seen = first + 256
        here, past = slice(start + first, start + seen), slice(start, start + seen)
        allowed, bias = allowed_and_bias(first, 256, seen, stops, slope)
        query, keys = qkv[here, mine], qkv[past, columns(1)]
        s = times_transposed(query, keys) * scale + bias
        p = jnp.exp(jnp.where(allowed, s, NEVER) - lse[g, head, first:seen])
        grad = do[here, mine]
        dots = jnp.sum(grad.astype(jnp.float32) * o[here, mine].astype(jnp.float32), axis=-1, keepdims=True)
        sum_v[:seen] += inner_rows(p.astype(jnp.bfloat16), grad)
        ds = (p * (times_transposed(grad, qkv[past, columns(2)]) - dots)).astype(jnp.bfloat16)
        dqkv[here, mine] = (jnp.dot(ds, keys, preferred_element_type=jnp.float32) * scale).astype(jnp.bfloat16)
        sum_k[:seen] += inner_rows(ds, query)
    dqkv[start : start + count, columns(1)] = (sum_k[...] * scale).astype(jnp.bfloat16)
    dqkv[start : start + count, columns(2)] = sum_v[...].astype(jnp.bfloat16)


def norm_parts(values):
    mean = jnp.mean(values, axis=-1, keepdims=True)
    centred = values - mean
    variance = jnp.mean(centred * centred, axis=-1, keepdims=True)
    factor = lax.rsqrt(variance + EPS)
    return centred * factor, factor


def norm_back_rows(grad, unit, factor, gain):
    scaled = grad * gain
    centre = jnp.mean(scaled, axis=-1, keepdims=True)
    along = jnp.mean(scaled * unit, axis=-1, keepdims=True)
    return factor * (scaled - centre - unit * along)


def gelu_and_slope(u):
    root, cube = 0.7978845608028654, 0.044715
    square = u * u
    t = jnp.tanh(root * u * (1.0 + cube * square))
    half = 0.5 * (1.0 + t)
    return u * half, half + 0.5 * u * (1.0 - t * t) * (root * (1.0 + 3.0 * cube * square))


def back_kernel(
    n_z,
    n_items,
    H2,
    C,
    WU,
    WD,
    MID,
    cot_in,
    tok_in,
    H1,
    QKV,
    O,
    LSE,
    WQ,
    WOQ,
    LQ,
    b_up,
    attn_gain,
    ffn_gain,
    b_down,
    BLOCK_OUT,
    GRAD_TOKENS,
    SHARED,
    rows_c,
    rows_h2,
    rows_a,
    rows_du,
    mat_u,
    mat_d,
    part_h2,
    near_h2,
    over_h2,
    part_out,
    near_out,
    over_out,
    grad_d,
    far_d,
    over_d,
    grad_u,
    far_u,
    over_u,
    middle,
    cot,
    lse,
    ends,
    branch,
    sum_k,
    sum_v,
    acc_o,
    grad_q,
    far_q,
    over_q,
    grad_o,
    far_o,
    over_o,
    small,
    slab,
    send,
    recv,
    near,
):
    me = Place(n_z)
    run = Copies(send, recv, near)
    quarter = me.quarter
    other, beside, far = 2 * (1 - me.core) + me.y, 2 * me.core + 1 - me.y, 2 * (1 - me.core) + 1 - me.y
    low, f32 = jnp.bfloat16, jnp.float32
    chips = 2 * n_z
    local, width = tok_in.shape
    count, half = 2 * local, local // 2
    size = width // HEADS
    heads = HEADS // 4
    rows = grad_d.shape[1]
    few = grad_o.shape[1]
    cols = 3 * heads * size
    meet(
        [me.across_core(), me.across_x(), me.across_y()] + [me.along_z(k) for k in range(1, n_z)]
    )
    load_up = [run.local(a, b) for a, b in ((H2, rows_h2), (WU, mat_u))]
    load_down = [run.local(a, b) for a, b in ((C, rows_c), (WD, mat_d))]
    load_mid = [run.local(MID, middle), run.local(cot_in, cot)]
    load_few = [run.local(a, b) for a, b in ((LSE, lse), (LQ, ends))]
    small[...] = jnp.zeros_like(small)
    acc_o[...] = jnp.zeros_like(acc_o)
    group = pl.ds(2 * me.core, 2)
    sum_h2 = QuadSum(me, run, part_h2, part_h2.at[group], near_h2, over_h2)
    sum_out = QuadSum(me, run, part_out, part_out.at[group], near_out, over_out)
    down = ChipSum(me, run, grad_d, lambda z: grad_d.at[z * 2 + me.x], far_d, over_d)
    up = ChipSum(me, run, grad_u, lambda z: grad_u.at[z * 2 + me.x], far_u, over_u)

    def feed(block):
        @pl.loop(0, local, step=256)
        def _(i):
            here, there = at(i, 256, 256), at(block * local + i, 256, 256)
            values, grads = rows_h2[there, :], rows_c[there, :]
            for j in range(0, width, 256):
                part = slice(j, j + 256)
                u = jnp.dot(values, mat_u[:, part], preferred_element_type=f32) + b_up[:, part]
                bent, slope = gelu_and_slope(u)
                rows_a[there, part] = bent.astype(low)
                du = times_transposed(grads, mat_d[part, :]) * slope
                rows_du[block, here, part] = du.astype(low)
                small[5:6, part] += jnp.sum(du, axis=0, keepdims=True)
            part_h2[block, here, :] = times_transposed(rows_du[block, here, :], mat_u[...]).astype(low)

    def feed_out(block):
        @pl.loop(0, local, step=256)
        def _(i):
            here, there = at(i, 256, 256), at(block * local + i, 256, 256)
            part_out[block, here, :] = jnp.dot(rows_a[there, :], mat_d[...], preferred_element_type=f32).astype(low)

    def weight_grad(into, left, right):
        @pl.loop(0, chips // 2)
        def _(i):
            columns = at(i * 2 * rows, 2 * rows, 128)
            total = inner_rows(left(columns, 0), right(0))
            for block in range(1, 4):
                total = total + inner_rows(left(columns, block), right(block))
            into[pl.ds(2 * i, 2)] = total.reshape(2, rows, total.shape[1]).astype(low)

    def block_rows(block):
        return slice(block * local, (block + 1) * local)

    share = Share(me, run, slab, SHARED)

    def to_slab(start, columns=slice(None)):
        def place(value):
            slab[start : start + value.shape[0], columns] = value.astype(low)

        return place

    def place_o(value):
        step = width // (rows // few)
        for i in range(rows // few):
            slab[2 * rows + i * few : 2 * rows + (i + 1) * few, width - step :] = value[
                :, i * step : (i + 1) * step
            ].astype(low)

    def chain(total, place, cut, then=None):
        yield from total.steps(place, then)
        yield from share.steps(cut)

    part = 3 * rows // 8
    run_down = chain(down, to_slab(0), (0, part, rows), up.send)
    run_up = chain(up, to_slab(rows), (rows, rows + part, 2 * rows))

    def pump(thread, times=1):
        for _ in range(times):
            next(thread, None)

    for copy in load_up + load_down:
        copy.wait()
    feed(far)
    sum_h2.start(1 - me.y)
    feed(other)
    sum_h2.start(me.y)
    feed(beside)
    sum_h2.cross()
    feed(quarter)
    weight_grad(grad_d, lambda columns, b: rows_a[block_rows(b), columns], lambda b: rows_c[block_rows(b), :])
    down.send(n_z)
    weight_grad(grad_u, lambda columns, b: rows_h2[block_rows(b), columns], lambda b: rows_du[b])
    pump(run_down, 2)
    feed_out(far)
    sum_out.start(1 - me.y)
    feed_out(other)
    sum_out.start(me.y)
    feed_out(beside)
    feed_out(quarter)
    qkv, o = rows_c.at[:, :cols], rows_c.at[:, cols:]
    dqkv, do = rows_h2.at[:, :cols], rows_h2.at[:, cols:]
    h1, part_h1 = rows_a, rows_du
    w_q, w_o = mat_u.at[:, :cols], mat_d.at[: heads * size]
    load_heads = [run.local(a, b) for a, b in ((WOQ, w_o), (O, o), (QKV, qkv), (H1, h1), (WQ, w_q))]
    pump(run_down, 2)
    for copy in load_mid:
        copy.wait()
    sum_h2.landed()

    @pl.loop(0, local, step=64)
    def _(i):
        here = at(i, 64, 64)
        unit, factor = norm_parts(middle[here, :])
        grad, c = sum_h2.rows(here), cot[here, :].astype(f32)
        total = c + norm_back_rows(grad, unit, factor, ffn_gain[...])
        branch[quarter, here, :] = total.astype(low)
        small[2:3] += jnp.sum(grad * unit, axis=0, keepdims=True)
        small[3:4] += jnp.sum(grad, axis=0, keepdims=True)
        small[4:5] += jnp.sum(c, axis=0, keepdims=True)

    load_few.append(run.local(tok_in, cot))
    own = branch.at[quarter]
    core_b = run.remote(own, own, me.across_core())
    over_b = []
    for h in range(2):
        part = branch.at[quarter, h * half : (h + 1) * half]
        over_b.append(run.remote(part, part, me.across_y()))
    pump(run_up)
    pump(run_down)
    pump(run_up)
    pump(run_down)
    for copy in load_heads + load_few:
        copy.wait()

    def project_back(block, start, size_b):
        @pl.loop(0, size_b, step=256)
        def _(i):
            here = at(start + i, 256, 256)
            there = at(block * local + start + i, 256, 256)
            values = branch[block, here, :]
            do[there, :] = times_transposed(values, w_o[...]).astype(low)
            acc_o[...] += inner_rows(o[there, :], values)

    project_back(quarter, 0, local)
    run.arrive(core_b)
    project_back(other, 0, local)
    pump(run_up)
    pump(run_down)
    pump(run_up)
    far_b = []
    for h in range(2):
        run.arrive(over_b[h])
        part = branch.at[beside, h * half : (h + 1) * half]
        far_b.append(run.remote(part, part, me.across_core()))
        project_back(beside, h * half, half)
        pump(run_down)
    pump(run_up)
    for h in range(2):
        run.arrive(far_b[h])
        project_back(far, h * half, half)
    sum_out.cross()
    grad_o[...] = acc_o[...].reshape(chips, few, width).astype(low)
    total_o = ChipSum(me, run, grad_o, lambda z: grad_o.at[z * 2 + me.x], far_o, over_o)
    total_o.send(n_z)
    pump(run_up)
    for g in range(2):
        stops = []
        end = 0
        for item in range(n_items - 1):
            end = end + ends[g, 0, item]
            stops.append(end)
        for head in range(heads):
            slope = jnp.exp2(-(jnp.zeros((1, 1), f32) + (quarter * heads + head + 1)))
            head_back(qkv, o, lse, do, dqkv, sum_k, sum_v, g, head, heads, size, count, stops, slope)
            pump(run_down)
            pump(run_up)

    weight_grad(grad_q, lambda columns, b: h1[block_rows(b), columns], lambda b: dqkv[block_rows(b), :])
    total_q = ChipSum(me, run, grad_q, lambda z: grad_q.at[z * 2 + me.x], far_q, over_q)
    total_q.send(n_z)

    def project_in(block):
        @pl.loop(0, local, step=256)
        def _(i):
            part_h1[block, at(i, 256, 256), :] = times_transposed(
                dqkv[at(block * local + i, 256, 256), :], w_q[...]
            ).astype(low)

    project_in(far)
    sum_h1 = QuadSum(me, run, part_h1, part_h1.at[group], near_h2, over_h2)
    sum_h1.start(1 - me.y)
    project_in(other)
    sum_h1.start(me.y)
    project_in(beside)
    sum_h1.cross()
    project_in(quarter)
    pump(run_down)
    pump(run_up)
    run_q = total_q.steps(to_slab(2 * rows, slice(0, cols)))
    run_o = total_o.steps(place_o)
    pump(run_o, 4)
    pump(run_q, 4)
    pump(run_up, 3)
    pump(run_down, 12)
    sum_out.landed()

    @pl.loop(0, local, step=64)
    def _(i):
        here = at(i, 64, 64)
        part_out[quarter, here, :] = (middle[here, :] + sum_out.rows(here) + b_down[...]).astype(low)

    run.later(part_out.at[quarter], BLOCK_OUT)
    sum_h1.landed()

    @pl.loop(0, local, step=64)
    def _(i):
        here = at(i, 64, 64)
        unit, factor = norm_parts(cot[here, :].astype(f32))
        grad = sum_h1.rows(here)
        base = branch[quarter, here, :].astype(f32)
        cot[here, :] = (base + norm_back_rows(grad, unit, factor, attn_gain[...])).astype(low)
        small[0:1] += jnp.sum(grad * unit, axis=0, keepdims=True)
        small[1:2] += jnp.sum(grad, axis=0, keepdims=True)

    run.later(cot, GRAD_TOKENS)
    slab[3 * rows :, :] = small[...].astype(low)
    pump(run_o, 2)
    pump(run_q, 2)
    halfway = 2 * rows + rows // 2
    last = [
        share.steps((2 * rows, 2 * rows + 16, halfway)),
        share.steps((halfway, halfway + 32, slab.shape[0])),
    ]
    pump(run_up, 12)
    for _ in range(n_z + 3):
        for thread in last:
            pump(thread)
    run.finish()


def back(n_z, n_items, feed, mid, cot, tok, saved, lq, b_up, attn_gain, ffn_gain, b_down):
    low, f32 = jnp.bfloat16, jnp.float32
    local, width = tok.shape
    chips = 2 * n_z
    heads, size = HEADS // 4, width // HEADS
    rows, few = width // chips, width // 4 // chips
    cols = 3 * heads * size
    shape = jax.ShapeDtypeStruct
    block, four, flat = (local, width), (4, local, width), (4 * local, width)
    deep = 3 * rows + 16
    v = pltpu.VMEM

    def sums(piece):
        return [v((chips,) + piece, low), v((n_z,) + piece, low), v((n_z - 1,) + piece, low)]

    scratch = (
        [v(flat, low)] * 3
        + [v(four, low)]
        + [v((width, width), low)] * 2
        + [v(four, low), v((2,) + block, low), v(block, low)] * 2
        + sums((rows, width)) * 2
        + [v(block, f32), v(block, low), v(saved[3].shape, f32), pltpu.SMEM(lq.shape, lq.dtype)]
        + [v(four, low)]
        + [v((2 * local, size), f32)] * 2
        + [v((heads * size, width), f32)]
        + sums((rows, cols))
        + sums((few, width))
        + [v((16, width), f32), v((deep, width), low)]
    )
    return communicate(
        functools.partial(back_kernel, n_z, n_items),
        [shape(block, low), shape(block, low), shape((4 * chips, deep, width), low)],
        tuple(feed) + (mid, cot, tok) + tuple(saved) + (lq, b_up, attn_gain, ffn_gain, b_down),
        [HBM] * 3,
        [HBM] * (len(feed) + 3 + len(saved) + 1) + [VMEM] * 4,
        (240, 48),
        scratch,
        call_id=2,
        limit=63 << 20,
    )


def unfold_kernel(rows, head_cols, few, shared, down, up, qkv, out, small, bias):
    f32 = jnp.float32
    width = shared.shape[-1]
    chips = up.shape[1] // width * 2
    unit = width // chips
    third = qkv.shape[1] // 3

    @pl.when(pl.program_id(0) == 0)
    def _():
        small[...] = jnp.zeros_like(small)
        bias[...] = jnp.zeros_like(bias)

    for q in range(4):
        down[q * rows : (q + 1) * rows] = shared[q, :rows].astype(f32)
        for s in range(chips):
            start = (s * 4 + q) * unit
            up[:, start : start + unit] = shared[q, rows : 2 * rows, s * unit : (s + 1) * unit].astype(f32)
        for i in range(3):
            start = i * third + q * head_cols
            qkv[:, start : start + head_cols] = shared[
                q, 2 * rows : 3 * rows, i * head_cols : (i + 1) * head_cols
            ].astype(f32)
        tail = 3 * head_cols
        step = width - tail
        for i in range(rows // few):
            out[q, :, i * step : (i + 1) * step] = shared[
                q, 2 * rows + i * few : 2 * rows + (i + 1) * few, tail:
            ].astype(f32)
        extra = shared[q, 3 * rows :].astype(f32)
        small[...] += extra
        bias[q : q + 1] += extra[5:6]


def unfold(shared, rows, few, ff):
    devices, deep, width = shared.shape
    chips = devices // 4
    f32 = jnp.float32
    head_cols = width // 4
    return pl.pallas_call(
        functools.partial(unfold_kernel, rows, head_cols, few),
        grid=(chips,),
        in_specs=[pl.BlockSpec((4, deep, width), lambda s: (s, 0, 0))],
        out_specs=[
            pl.BlockSpec((4 * rows, width), lambda s: (s, 0)),
            pl.BlockSpec((rows, ff), lambda s: (s, 0)),
            pl.BlockSpec((rows, 3 * width), lambda s: (s, 0)),
            pl.BlockSpec((4, None, few, width), lambda s: (0, s, 0, 0)),
            pl.BlockSpec((deep - 3 * rows, width), lambda s: (0, 0)),
            pl.BlockSpec((4, width), lambda s: (0, 0)),
        ],
        out_shape=[
            jax.ShapeDtypeStruct((ff, width), f32),
            jax.ShapeDtypeStruct((width, ff), f32),
            jax.ShapeDtypeStruct((width, 3 * width), f32),
            jax.ShapeDtypeStruct((4, chips, few, width), f32),
            jax.ShapeDtypeStruct((deep - 3 * rows, width), f32),
            jax.ShapeDtypeStruct((4, width), f32),
        ],
        compiler_params=pltpu.CompilerParams(vmem_limit_bytes=56 << 20),
    )(shared)


def on_quad(
    tokens,
    lengths,
    attn_gain,
    attn_shift,
    w_qkv,
    w_out,
    ffn_gain,
    ffn_shift,
    w_up,
    b_up,
    w_down,
    b_down,
    cotangent,
):
    low = jnp.bfloat16
    local, width = tokens.shape
    n_dp = lax.axis_size("dp")
    n_z, chips = n_dp // 4, n_dp // 2
    size = width // HEADS
    heads = HEADS // 4
    count = 2 * local
    me = Place(n_z)
    lens = jnp.zeros((8, 128), jnp.int32).at[:1, : lengths.shape[1]].set(lengths)
    gains = [value.reshape(1, width) for value in (attn_gain, attn_shift, ffn_gain, ffn_shift)]
    WQ, WOQ, WU, WD, CQ, h1, qkv, o, lse, h2, middle, LQ = front(
        n_z, lengths.shape[1], w_qkv, w_out, w_up, w_down, tokens, cotangent, lens, gains
    )
    unit = w_up.shape[1] // chips // 4
    bias = lax.dynamic_index_in_dim(b_up.reshape(chips, 4, unit), me.quarter, 1, keepdims=False).reshape(-1)
    block_out, grad_tokens, shared = back(
        n_z,
        lengths.shape[1],
        [h2, CQ.reshape(4 * local, width), WU, WD],
        middle,
        cotangent,
        tokens,
        [h1.reshape(4 * local, width), qkv, o, lse, WQ, WOQ],
        LQ,
        bias.reshape(1, width),
        gains[0],
        gains[2],
        b_down.reshape(1, width),
    )
    rows, few = width // chips, width // 4 // chips
    ff = w_up.shape[1]
    grad_w_down, grad_w_up, grad_w_qkv, grad_w_out, vectors, bias = unfold(shared, rows, few, ff)
    return (
        block_out,
        grad_tokens,
        vectors[0],
        vectors[1],
        grad_w_qkv,
        grad_w_out.reshape(width, width),
        vectors[2],
        vectors[3],
        grad_w_up,
        jnp.transpose(bias.reshape(4, chips, unit), (1, 0, 2)).reshape(ff),
        grad_w_down,
        vectors[4],
    )


def solution(mesh):
    n_dp, n_seq = mesh.shape["dp"], mesh.shape["seq"]
    quad = n_seq == 2 and n_dp % 4 == 0 and n_dp >= 8 and n_dp <= 16
    return jax.shard_map(
        on_quad if quad else on_device,
        mesh=mesh,
        in_specs=(
            P(("dp", "seq"), None),
            P("dp", None),
            P(),
            P(),
            P("dp", None),
            P("dp", None),
            P(),
            P(),
            P("dp", None),
            P(),
            P("dp", None),
            P(),
            P(("dp", "seq"), None),
        ),
        out_specs=(
            P(("dp", "seq"), None),
            P(("dp", "seq"), None),
            P(),
            P(),
            P(),
            P(),
            P(),
            P(),
            P(),
            P(),
            P(),
            P(),
        ),
        check_vma=False,
    )
```

```python
import functools

import jax
import jax.numpy as jnp
from jax import lax
from jax.experimental import pallas as pl
from jax.experimental.pallas import tpu as pltpu
from jax.sharding import PartitionSpec as P

HEADS = 8


EPS = 1e-05
NEVER = -1000000000.0


def inner_rows(left, right):
    return lax.dot_general(
        left, right, (((0,), (0,)), ((), ())), preferred_element_type=jnp.float32
    )


def times_transposed(left, right):
    return lax.dot_general(
        left, right, (((1,), (1,)), ((), ())), preferred_element_type=jnp.float32
    )


def smooth_act(values):
    return jax.nn.gelu(values, approximate=True)


def norm_forward(values, gain, shift):
    mean = jnp.mean(values, axis=-1, keepdims=True)
    centred = values - mean
    variance = jnp.mean(centred * centred, axis=-1, keepdims=True)
    factor = lax.rsqrt(variance + EPS)
    normed = centred * factor
    return (normed * gain + shift, normed, factor)


def norm_backward(grad_out, normed, factor, gain):
    grad_normed = grad_out * gain
    centre_term = jnp.mean(grad_normed, axis=-1, keepdims=True)
    along_term = jnp.mean(grad_normed * normed, axis=-1, keepdims=True)
    grad_in = factor * (grad_normed - centre_term - normed * along_term)
    return (grad_in, jnp.sum(grad_out * normed, axis=0), jnp.sum(grad_out, axis=0))


def item_ids(item_lengths, count):
    item_ends = jnp.cumsum(item_lengths, dtype=jnp.int32)
    places = jnp.arange(count, dtype=jnp.int32)
    hits = (places[:, None] >= item_ends[None, :]).astype(jnp.int32)
    return jnp.sum(hits, axis=1, dtype=jnp.int32)


def block_scores(query_block, keys, start, item_of, slopes):
    rows = query_block.shape[0]
    count = keys.shape[0]
    scale = query_block.shape[-1] ** (-0.5)
    raw = jnp.einsum("qhd,khd->hqk", query_block, keys, preferred_element_type=jnp.float32)
    row_places = start + jnp.arange(rows, dtype=jnp.int32)
    col_places = jnp.arange(count, dtype=jnp.int32)
    distance = (row_places[:, None] - col_places[None, :]).astype(jnp.float32)
    row_items = lax.dynamic_slice_in_dim(item_of, start, rows)
    allowed = (row_items[:, None] == item_of[None, :]) & (
        col_places[None, :] <= row_places[:, None]
    )
    scores = raw * scale - slopes[:, None, None] * distance[None]
    return jnp.where(allowed[None], scores, jnp.float32(-1000000000.0))


def attend(heads_qkv, item_of, slopes):
    count = heads_qkv.shape[0]
    rows = min(512, count)
    queries = heads_qkv[:, 0]
    keys = heads_qkv[:, 1]
    values = heads_qkv[:, 2]

    def one_block(index):
        start = index * rows
        query_block = lax.dynamic_slice_in_dim(queries, start, rows)
        scores = block_scores(query_block, keys, start, item_of, slopes)
        top = jnp.max(scores, axis=-1, keepdims=True)
        weights = jnp.exp(scores - top)
        total = jnp.sum(weights, axis=-1, keepdims=True)
        probs = (weights / total).astype(jnp.bfloat16)
        mixed = jnp.einsum("hqk,khd->qhd", probs, values, preferred_element_type=jnp.float32)
        return (mixed.astype(jnp.bfloat16), (top + jnp.log(total))[..., 0])

    mixed, log_norm = lax.map(one_block, jnp.arange(count // rows, dtype=jnp.int32))
    return (mixed.reshape(count, mixed.shape[2], mixed.shape[3]), log_norm)


def attend_back(heads_qkv, heads_out, grad_heads, log_norm, item_of, slopes):
    count = heads_qkv.shape[0]
    rows = min(512, count)
    queries = heads_qkv[:, 0]
    keys = heads_qkv[:, 1]
    values = heads_qkv[:, 2]
    scale = queries.shape[-1] ** (-0.5)
    row_dots = jnp.sum(grad_heads.astype(jnp.float32) * heads_out.astype(jnp.float32), axis=-1)

    def one_block(carry, index):
        grad_keys, grad_values = carry
        start = index * rows
        query_block = lax.dynamic_slice_in_dim(queries, start, rows)
        grad_block = lax.dynamic_slice_in_dim(grad_heads, start, rows)
        dots = lax.dynamic_slice_in_dim(row_dots, start, rows)
        scores = block_scores(query_block, keys, start, item_of, slopes)
        probs = jnp.exp(scores - log_norm[index][:, :, None])
        probs_low = probs.astype(jnp.bfloat16)
        grad_values = grad_values + jnp.einsum(
            "hqk,qhd->khd", probs_low, grad_block, preferred_element_type=jnp.float32
        )
        grad_probs = jnp.einsum(
            "qhd,khd->hqk", grad_block, values, preferred_element_type=jnp.float32
        )
        grad_scores = (probs * (grad_probs - jnp.transpose(dots)[:, :, None])).astype(jnp.bfloat16)
        grad_query = (
            jnp.einsum("hqk,khd->qhd", grad_scores, keys, preferred_element_type=jnp.float32)
            * scale
        )
        grad_keys = (
            grad_keys
            + jnp.einsum(
                "hqk,qhd->khd", grad_scores, query_block, preferred_element_type=jnp.float32
            )
            * scale
        )
        return ((grad_keys, grad_values), grad_query)

    empty = jnp.zeros(keys.shape, jnp.float32)
    (grad_keys, grad_values), grad_query = lax.scan(
        one_block, (empty, empty), jnp.arange(count // rows, dtype=jnp.int32)
    )
    grad_query = grad_query.reshape(keys.shape)
    return jnp.stack([grad_query, grad_keys, grad_values], axis=1).astype(jnp.bfloat16)


def on_device(
    tokens,
    lengths,
    attn_gain,
    attn_shift,
    w_qkv,
    w_out,
    ffn_gain,
    ffn_shift,
    w_up,
    b_up,
    w_down,
    b_down,
    cotangent,
):
    w_qkv, w_out, w_up, w_down = (
        lax.all_gather(w_qkv, "dp", axis=0, tiled=True),
        lax.all_gather(w_out, "dp", axis=0, tiled=True),
        lax.all_gather(w_up, "dp", axis=0, tiled=True),
        lax.all_gather(w_down, "dp", axis=0, tiled=True),
    )
    local, width = tokens.shape
    groups = lax.axis_size("seq")
    per_head = width // HEADS
    local_heads = HEADS // groups
    count = local * groups
    item_of = item_ids(lengths[0], count)
    first_head = lax.axis_index("seq") * local_heads
    exponents = (first_head + jnp.arange(local_heads, dtype=jnp.int32) + 1).astype(jnp.float32)
    slopes = jnp.exp2(-exponents)
    inputs = tokens.astype(jnp.float32)
    normed_in, unit_in, factor_in = norm_forward(inputs, attn_gain, attn_shift)
    first_in = normed_in.astype(jnp.bfloat16)
    projected = jnp.dot(first_in, w_qkv, preferred_element_type=jnp.float32).astype(jnp.bfloat16)
    projected = projected.reshape(local, 3, HEADS, per_head)
    heads_qkv = lax.all_to_all(projected, "seq", split_axis=2, concat_axis=0, tiled=True)
    heads_out, log_norm = attend(heads_qkv, item_of, slopes)
    joined = lax.all_to_all(heads_out, "seq", split_axis=0, concat_axis=1, tiled=True).reshape(
        local, width
    )
    middle = inputs + jnp.dot(joined, w_out, preferred_element_type=jnp.float32)
    normed_mid, unit_mid, factor_mid = norm_forward(middle, ffn_gain, ffn_shift)
    second_in = normed_mid.astype(jnp.bfloat16)
    pre_act = jnp.dot(second_in, w_up, preferred_element_type=jnp.float32) + b_up
    act_value, act_pull = jax.vjp(smooth_act, pre_act)
    active = act_value.astype(jnp.bfloat16)
    block_out = (
        middle + jnp.dot(active, w_down, preferred_element_type=jnp.float32) + b_down
    ).astype(jnp.bfloat16)
    grad_out = cotangent.astype(jnp.float32)
    grad_b_down = jnp.sum(grad_out, axis=0)
    grad_w_down = inner_rows(active, cotangent)
    grad_active = times_transposed(cotangent, w_down)
    grad_pre = act_pull(grad_active)[0]
    grad_b_up = jnp.sum(grad_pre, axis=0)
    grad_pre_low = grad_pre.astype(jnp.bfloat16)
    grad_w_up = inner_rows(second_in, grad_pre_low)
    grad_second = times_transposed(grad_pre_low, w_up)
    grad_mid_norm, grad_ffn_gain, grad_ffn_shift = norm_backward(
        grad_second, unit_mid, factor_mid, ffn_gain
    )
    grad_middle = grad_out + grad_mid_norm
    grad_branch = grad_middle.astype(jnp.bfloat16)
    grad_w_out = inner_rows(joined, grad_branch)
    grad_joined = (
        times_transposed(grad_branch, w_out).astype(jnp.bfloat16).reshape(local, HEADS, per_head)
    )
    grad_heads = lax.all_to_all(grad_joined, "seq", split_axis=1, concat_axis=0, tiled=True)
    grad_qkv_heads = attend_back(heads_qkv, heads_out, grad_heads, log_norm, item_of, slopes)
    grad_projected = lax.all_to_all(
        grad_qkv_heads, "seq", split_axis=0, concat_axis=2, tiled=True
    ).reshape(local, 3 * width)
    grad_w_qkv = inner_rows(first_in, grad_projected)
    grad_first = times_transposed(grad_projected, w_qkv)
    grad_in_norm, grad_attn_gain, grad_attn_shift = norm_backward(
        grad_first, unit_in, factor_in, attn_gain
    )
    grad_tokens = (grad_middle + grad_in_norm).astype(jnp.bfloat16)
    all_part = (
        lax.psum_scatter(
            grad_attn_gain.astype(jnp.bfloat16), "dp", scatter_dimension=0, tiled=True
        ).astype(jnp.float32),
        lax.psum_scatter(
            grad_attn_shift.astype(jnp.bfloat16), "dp", scatter_dimension=0, tiled=True
        ).astype(jnp.float32),
        lax.psum_scatter(
            grad_w_qkv.astype(jnp.bfloat16), "dp", scatter_dimension=0, tiled=True
        ).astype(jnp.float32),
        lax.psum_scatter(
            grad_w_out.astype(jnp.bfloat16), "dp", scatter_dimension=0, tiled=True
        ).astype(jnp.float32),
        lax.psum_scatter(
            grad_ffn_gain.astype(jnp.bfloat16), "dp", scatter_dimension=0, tiled=True
        ).astype(jnp.float32),
        lax.psum_scatter(
            grad_ffn_shift.astype(jnp.bfloat16), "dp", scatter_dimension=0, tiled=True
        ).astype(jnp.float32),
        lax.psum_scatter(
            grad_w_up.astype(jnp.bfloat16), "dp", scatter_dimension=0, tiled=True
        ).astype(jnp.float32),
        lax.psum_scatter(
            grad_b_up.astype(jnp.bfloat16), "dp", scatter_dimension=0, tiled=True
        ).astype(jnp.float32),
        lax.psum_scatter(
            grad_w_down.astype(jnp.bfloat16), "dp", scatter_dimension=0, tiled=True
        ).astype(jnp.float32),
        lax.psum_scatter(
            grad_b_down.astype(jnp.bfloat16), "dp", scatter_dimension=0, tiled=True
        ).astype(jnp.float32),
    )
    all_part = (
        lax.psum(all_part[0].astype(jnp.bfloat16), "seq").astype(jnp.float32),
        lax.psum(all_part[1].astype(jnp.bfloat16), "seq").astype(jnp.float32),
        lax.psum(all_part[2].astype(jnp.bfloat16), "seq").astype(jnp.float32),
        lax.psum(all_part[3].astype(jnp.bfloat16), "seq").astype(jnp.float32),
        lax.psum(all_part[4].astype(jnp.bfloat16), "seq").astype(jnp.float32),
        lax.psum(all_part[5].astype(jnp.bfloat16), "seq").astype(jnp.float32),
        lax.psum(all_part[6].astype(jnp.bfloat16), "seq").astype(jnp.float32),
        lax.psum(all_part[7].astype(jnp.bfloat16), "seq").astype(jnp.float32),
        lax.psum(all_part[8].astype(jnp.bfloat16), "seq").astype(jnp.float32),
        lax.psum(all_part[9].astype(jnp.bfloat16), "seq").astype(jnp.float32),
    )
    summed = (
        lax.all_gather(all_part[0].astype(jnp.bfloat16), "dp", axis=0, tiled=True).astype(
            jnp.float32
        ),
        lax.all_gather(all_part[1].astype(jnp.bfloat16), "dp", axis=0, tiled=True).astype(
            jnp.float32
        ),
        lax.all_gather(all_part[2].astype(jnp.bfloat16), "dp", axis=0, tiled=True).astype(
            jnp.float32
        ),
        lax.all_gather(all_part[3].astype(jnp.bfloat16), "dp", axis=0, tiled=True).astype(
            jnp.float32
        ),
        lax.all_gather(all_part[4].astype(jnp.bfloat16), "dp", axis=0, tiled=True).astype(
            jnp.float32
        ),
        lax.all_gather(all_part[5].astype(jnp.bfloat16), "dp", axis=0, tiled=True).astype(
            jnp.float32
        ),
        lax.all_gather(all_part[6].astype(jnp.bfloat16), "dp", axis=0, tiled=True).astype(
            jnp.float32
        ),
        lax.all_gather(all_part[7].astype(jnp.bfloat16), "dp", axis=0, tiled=True).astype(
            jnp.float32
        ),
        lax.all_gather(all_part[8].astype(jnp.bfloat16), "dp", axis=0, tiled=True).astype(
            jnp.float32
        ),
        lax.all_gather(all_part[9].astype(jnp.bfloat16), "dp", axis=0, tiled=True).astype(
            jnp.float32
        ),
    )
    return (
        block_out,
        grad_tokens,
        summed[0],
        summed[1],
        summed[2],
        summed[3],
        summed[4],
        summed[5],
        summed[6],
        summed[7],
        summed[8],
        summed[9],
    )


MESH = pl.DeviceIdType.MESH


class Place:
    def __init__(self, n_z):
        dp = lax.axis_index("dp")
        self.n_z = n_z
        self.dp = dp
        self.y = lax.axis_index("seq")
        self.core = dp % 2
        self.chip = dp // 2
        self.x = self.chip % 2
        self.z = self.chip // 2
        self.quarter = 2 * self.core + self.y

    def device(self, z=None, x=None, core=None, y=None):
        z = self.z if z is None else z
        x = self.x if x is None else x
        core = self.core if core is None else core
        y = self.y if y is None else y
        return ((z * 2 + x) * 2 + core, y)

    def across_core(self):
        return self.device(core=1 - self.core)

    def across_x(self):
        return self.device(x=1 - self.x)

    def across_y(self):
        return self.device(y=1 - self.y)

    def z_after(self, k):
        return (self.z + k) % self.n_z

    def z_before(self, k):
        return (self.z + self.n_z - k) % self.n_z

    def along_z(self, k):
        return self.device(z=self.z_after(k))


class Copy:
    def __init__(self, copy, sends, lands):
        self.copy, self.sends, self.lands, self.landed = copy, sends, lands, False

    def guarded(self, condition, action):
        if condition is None:
            action()
        else:
            pl.when(condition)(action)


class Copies:
    def __init__(self, send, recv, near):
        self.send, self.recv, self.near = send, recv, near
        self.all, self.n, self.m, self.local_open = [], 0, 0, []

    def remote(self, src, dst, device, sends=None, lands=None):
        copy = Copy(
            pltpu.make_async_remote_copy(
                src_ref=src,
                dst_ref=dst,
                send_sem=self.send.at[self.n],
                recv_sem=self.recv.at[self.n],
                device_id=device,
                device_id_type=MESH,
            ),
            sends,
            lands,
        )
        self.n += 1
        copy.guarded(sends, copy.copy.start)
        self.all.append(copy)
        return copy

    def local(self, src, dst):
        copy = pltpu.make_async_copy(src, dst, self.near.at[self.m])
        self.m += 1
        copy.start()
        return copy

    def later(self, src, dst):
        self.local_open.append(self.local(src, dst))

    def arrive(self, *copies):
        for copy in copies:
            if not copy.landed:
                copy.guarded(copy.lands, copy.copy.wait_recv)
                copy.landed = True

    def finish(self):
        self.arrive(*self.all)
        for copy in self.all:
            copy.guarded(copy.sends, copy.copy.wait_send)
        for copy in self.local_open:
            copy.wait()


class Line:
    def __init__(self, me, run, own, view):
        self.me, self.run, self.view = me, run, view
        n, z = me.n_z, me.z
        self.up = [run.remote(own, view(z), me.device(z=z + 1), z < n - 1, z > 0)]
        self.down = [run.remote(own, view(z), me.device(z=z - 1), z > 0, z < n - 1)]

    def step(self, t, then):
        me, run, n, z = self.me, self.run, self.me.n_z, self.me.z
        if t >= n:
            return
        run.arrive(self.up[t - 1])
        if t < n - 1:
            part = self.view(z - t)
            self.up.append(run.remote(part, part, me.device(z=z + 1), (z >= t) & (z < n - 1), z > t))
        then(z - t, z >= t)
        run.arrive(self.down[t - 1])
        if t < n - 1:
            part = self.view(z + t)
            self.down.append(
                run.remote(part, part, me.device(z=z - 1), (z < n - t) & (z > 0), z < n - t - 1)
            )
        then(z + t, z < n - t)


def meet(devices):
    barrier = pltpu.get_barrier_semaphore()
    for device in devices:
        pl.semaphore_signal(barrier, inc=1, device_id=device, device_id_type=MESH)
    pl.semaphore_wait(barrier, len(devices))


def at(start, size, unit):
    return pl.ds(pl.multiple_of(start, unit), size)


def communicate(kernel, out_shapes, ins, out_specs, in_specs, counts, scratch=(), call_id=0, limit=None):
    return pl.pallas_call(
        kernel,
        out_shape=out_shapes,
        in_specs=in_specs,
        out_specs=out_specs,
        scratch_shapes=list(scratch)
        + [
            pltpu.SemaphoreType.DMA((counts[0],)),
            pltpu.SemaphoreType.DMA((counts[0],)),
            pltpu.SemaphoreType.DMA((counts[1],)),
        ],
        compiler_params=pltpu.CompilerParams(
            collective_id=call_id, has_side_effects=True, vmem_limit_bytes=limit or (56 << 20)
        ),
    )(*ins)


HBM = pl.BlockSpec(memory_space=pltpu.HBM)
VMEM = pl.BlockSpec(memory_space=pltpu.VMEM)
SMEM = pl.BlockSpec(memory_space=pltpu.SMEM)


def allowed_and_bias(first, rows, count, ends, slope):
    row = first + lax.broadcasted_iota(jnp.int32, (rows, 1), 0)
    col = lax.broadcasted_iota(jnp.int32, (1, count), 1)
    begin = jnp.zeros((rows, 1), jnp.int32)
    for end in ends:
        begin = jnp.where(row >= end, end, begin)
    allowed = (col >= begin) & (col <= row)
    bias = slope * (col - first).astype(jnp.float32)
    return allowed, bias


def norm_rows(values, gain, shift):
    mean = jnp.mean(values, axis=-1, keepdims=True)
    centred = values - mean
    variance = jnp.mean(centred * centred, axis=-1, keepdims=True)
    return centred * lax.rsqrt(variance + EPS) * gain + shift


def norm_block(src, dst, gain, shift, step=64):
    @pl.loop(0, src.shape[0], step=step)
    def _(i):
        rows = at(i, step, step)
        dst[rows, :] = norm_rows(src[rows, :].astype(jnp.float32), gain[...], shift[...]).astype(dst.dtype)


def front_kernel(
    n_z,
    n_items,
    wq,
    wo,
    wu,
    wd,
    tok,
    cot,
    lens,
    attn_gain,
    attn_shift,
    ffn_gain,
    ffn_shift,
    WQ,
    WOQ,
    WU,
    WD,
    CQ,
    H1,
    QKV,
    O,
    LSE,
    H2,
    MID,
    LQ,
    q_all,
    o_all,
    x_all,
    h1,
    qkv,
    mixed,
    lse,
    h2,
    middle,
    ends,
    send,
    recv,
    near,
):
    me = Place(n_z)
    run = Copies(send, recv, near)
    quarter, other = me.quarter, 2 * (1 - me.core) + me.y
    rows = wq.shape[0]
    third = wq.shape[1] // 3
    cut = third // 4
    chips = 2 * n_z
    span = wu.shape[1] // chips
    unit = span // 4
    local = tok.shape[0]
    count = 2 * local
    half = local // 2
    size = third // HEADS
    heads = HEADS // 4
    meet(
        [me.across_core(), me.across_x(), me.across_y()] + [me.along_z(k) for k in range(1, n_z)]
    )
    mine = at(me.dp * rows, rows, 16)

    into = [q_all.at[mine, p * cut : (p + 1) * cut] for p in range(3)]
    near_q = [run.local(wq.at[:, at(p * third + quarter * cut, cut, 128)], into[p]) for p in range(3)]
    core_q = [
        run.remote(wq.at[:, at(p * third + other * cut, cut, 128)], into[p], me.across_core())
        for p in range(3)
    ]
    keep_x = run.local(tok, x_all.at[quarter])
    keep_lens = run.local(lens, LQ.at[me.core])
    core_lens = run.remote(lens, LQ.at[me.core], me.across_core())

    def halves(h):
        return slice(h * half, (h + 1) * half)

    over_x = [
        run.remote(tok.at[halves(h)], x_all.at[quarter, halves(h)], me.across_y()) for h in range(2)
    ]
    core_x = run.remote(tok, x_all.at[quarter], me.across_core())
    into = [WU.at[mine, s * unit : (s + 1) * unit] for s in range(chips)]
    near_u = [run.local(wu.at[:, at(s * span + quarter * unit, unit, 128)], into[s]) for s in range(chips)]
    core_u = [
        run.remote(wu.at[:, at(s * span + other * unit, unit, 128)], into[s], me.across_core())
        for s in range(chips)
    ]

    def pairs_of(array):
        return lambda z, x=me.x: array.at[at((z * 2 + x) * 2 * rows, 2 * rows, 16)]

    def shard_of(z, x=me.x):
        return o_all.at[at(((z * 2 + x) * 2 + me.core) * rows, rows, 16)]

    def units_of(z, x=me.x):
        return WD.at[at((z * 2 + x) * unit, unit, 16)]

    from_x = {"q": [], "o": [], "u": [], "d": []}
    share_o = []

    def across(name, view):
        def then(z, came):
            part = view(z)
            from_x[name].append((run.remote(part, part, me.across_x(), came, came), z, came))
            if name == "o":
                share_o.append(run.remote(part, part, me.across_core(), came, came))

        return then

    for copy in near_q:
        copy.wait()
    run.arrive(*core_q)
    view_q, view_u = pairs_of(q_all), pairs_of(WU)
    line_q = Line(me, run, view_q(me.z), view_q)
    across("q", view_q)(me.z, None)
    keep_o = run.local(wo, shard_of(me.z))
    keep_x.wait()
    norm_block(x_all.at[quarter], h1.at[quarter], attn_gain, attn_shift)
    run.arrive(core_x)
    line_q.step(1, across("q", view_q))
    line_o = Line(me, run, wo, shard_of)
    share_o.append(run.remote(wo, shard_of(me.z), me.across_core()))
    norm_block(x_all.at[other], h1.at[other], attn_gain, attn_shift)
    line_q.step(2, across("q", view_q))
    beside = 2 * me.core + 1 - me.y
    far = 2 * (1 - me.core) + 1 - me.y
    far_x = []
    for h in range(2):
        run.arrive(over_x[h])
        part = x_all.at[beside, halves(h)]
        far_x.append(run.remote(part, part, me.across_core()))
        if h == 0:
            line_q.step(3, across("q", view_q))
            from_x["o"].append((run.remote(wo, shard_of(me.z), me.across_x()), me.z, None))
            line_o.step(1, across("o", shard_of))
            for copy in near_u:
                copy.wait()
            run.arrive(*core_u)
            line_u = Line(me, run, view_u(me.z), view_u)
        norm_block(x_all.at[beside, halves(h)], h1.at[beside, halves(h)], attn_gain, attn_shift)
    over_c = [run.remote(cot.at[halves(0)], CQ.at[quarter, halves(0)], me.across_y())]
    run.later(cot, CQ.at[quarter])
    run.remote(cot, CQ.at[quarter], me.across_core())
    for h in range(2):
        run.arrive(far_x[h])
        norm_block(x_all.at[far, halves(h)], h1.at[far, halves(h)], attn_gain, attn_shift)
    line_o.step(2, across("o", shard_of))
    own = wd.at[at(me.y * unit, unit, 16)]
    across("u", view_u)(me.z, None)
    run.later(h1, H1)
    for copy, _, _ in from_x["q"]:
        run.arrive(copy)
    run.later(q_all, WQ)

    @pl.loop(0, 4 * local, step=256)
    def _(i):
        block = at(i, 256, 256)
        qkv[block, :] = jnp.dot(
            h1[i // local, at(i % local, 256, 256), :], q_all[...], preferred_element_type=jnp.float32
        ).astype(jnp.bfloat16)

    run.later(qkv, QKV)
    keep_lens.wait()
    run.arrive(core_lens)
    fetch = run.local(LQ, ends)
    fetch.wait()

    def heads_at(owner, head):
        return at(owner * heads * size + head * size, size, 128)

    over_o, near_o = [], []
    line_o.step(3, across("o", shard_of))
    line_d = Line(me, run, own, units_of)
    from_x["d"].append((run.remote(own, units_of(me.z), me.across_x()), me.z, None))
    run.later(own, units_of(me.z))
    pumps = [
        lambda: line_u.step(1, across("u", view_u)),
        lambda: line_u.step(2, across("u", view_u)),
        lambda: line_u.step(3, across("u", view_u)),
        lambda: line_d.step(1, across("d", units_of)),
    ]
    for g in range(2):
        stops = []
        total = 0
        for item in range(n_items - 1):
            total = total + ends[g, 0, item]
            stops.append(total)
        for head in range(heads):
            slope = jnp.exp2(-(jnp.zeros((1, 1), jnp.float32) + (quarter * heads + head + 1)))
            column = heads_at(quarter, head)
            for first in range(0, count, 256):
                start, seen = g * count, first + 256
                here = slice(start + first, start + seen)
                allowed, bias = allowed_and_bias(first, 256, seen, stops, slope)
                keys = qkv[start : start + seen, (heads + head) * size : (heads + head + 1) * size]
                s = times_transposed(qkv[here, head * size : (head + 1) * size], keys) * size**-0.5 + bias
                s = jnp.where(allowed, s, NEVER)
                top = jnp.max(s, axis=-1, keepdims=True)
                w = jnp.exp(s - top)
                sum_w = jnp.sum(w, axis=-1, keepdims=True)
                p = (w * (1.0 / sum_w)).astype(jnp.bfloat16)
                values = qkv[start : start + seen, (2 * heads + head) * size : (2 * heads + head + 1) * size]
                mixed[here, column] = jnp.dot(p, values, preferred_element_type=jnp.float32).astype(
                    jnp.bfloat16
                )
                lse[g, head, first:seen] = top + jnp.log(sum_w)
            part = mixed.at[g * count : (g + 1) * count, column]
            over_o.append(run.remote(part, part, me.across_y()))
            near_o.append(run.remote(part, part, me.across_core()))
            pumps[g * heads + head]()
    run.later(mixed.at[:, at(quarter * heads * size, heads * size, 128)], O)
    run.later(lse, LSE)
    over_c.append(run.remote(cot.at[halves(1)], CQ.at[quarter, halves(1)], me.across_y()))
    run.arrive(over_c[0])
    part = CQ.at[beside, halves(0)]
    run.remote(part, part, me.across_core())
    far_o = []
    for copy, z, came in from_x["o"]:
        run.arrive(copy)
        part = shard_of(z, 1 - me.x)
        far_o.append(run.remote(part, part, me.across_core(), came, came))
    passed = []
    for g in range(2):
        for head in range(heads):
            run.arrive(over_o[g * heads + head])
            part = mixed.at[g * count : (g + 1) * count, heads_at(beside, head)]
            passed.append(run.remote(part, part, me.across_core()))
    line_d.step(2, across("d", units_of))
    keep_o.wait()
    run.arrive(*share_o, *far_o)
    run.later(o_all.at[at(quarter * heads * size, heads * size, 16)], WOQ)
    for g in range(2):
        run.arrive(*near_o[g * heads : (g + 1) * heads], *passed[g * heads : (g + 1) * heads])

        @pl.loop(0, count, step=256)
        def _(i):
            block = at(g * count + i, 256, 256)
            owner, inner = 2 * g + i // local, at(i % local, 256, 256)
            x1 = x_all[owner, inner, :].astype(jnp.float32) + jnp.dot(
                mixed[block, :], o_all[...], preferred_element_type=jnp.float32
            )
            h2[block, :] = norm_rows(x1, ffn_gain[...], ffn_shift[...]).astype(jnp.bfloat16)

            @pl.when(owner == quarter)
            def _():
                middle[inner, :] = x1

        line_d.step(3 + g, across("d", units_of))
    run.later(h2, H2)
    run.later(middle, MID)
    run.arrive(over_c[1])
    part = CQ.at[beside, halves(1)]
    run.remote(part, part, me.across_core())
    run.finish()


def front(n_z, n_items, wq, wo, wu, wd, tok, cot, lens, gains):
    width, low, f32 = wq.shape[0] * 4 * n_z, jnp.bfloat16, jnp.float32
    quarter_ff = wu.shape[1] // 4
    local = tok.shape[0]
    heads, size = HEADS // 4, width // HEADS
    shape = jax.ShapeDtypeStruct
    shapes = [
        shape((width, wq.shape[1] // 4), low),
        shape((width // 4, width), low),
        shape((width, quarter_ff), low),
        shape((quarter_ff, width), low),
        shape((4, local, width), low),
        shape((4, local, width), low),
        shape((4 * local, 3 * width // 4), low),
        shape((4 * local, width // 4), low),
        shape((2, heads, 2 * local, 1), f32),
        shape((4 * local, width), low),
        shape((local, width), f32),
        shape((2,) + lens.shape, lens.dtype),
    ]
    scratch = [
        pltpu.VMEM((width, wq.shape[1] // 4), low),
        pltpu.VMEM((width, width), low),
        pltpu.VMEM((4, local, width), low),
        pltpu.VMEM((4, local, width), low),
        pltpu.VMEM((4 * local, 3 * width // 4), low),
        pltpu.VMEM((4 * local, width), low),
        pltpu.VMEM((2, heads, 2 * local, 1), f32),
        pltpu.VMEM((4 * local, width), low),
        pltpu.VMEM((local, width), f32),
        pltpu.SMEM((2,) + lens.shape, lens.dtype),
    ]
    return communicate(
        functools.partial(front_kernel, n_z, n_items),
        shapes,
        (wq, wo, wu, wd, tok, cot, lens) + tuple(gains),
        [HBM] * 12,
        [HBM] * 7 + [VMEM] * 4,
        (128, 32),
        scratch,
        call_id=1,
    )


def add(*values):
    total = values[0].astype(jnp.float32)
    for value in values[1:]:
        total = total + value.astype(jnp.float32)
    return total


class Share:
    def __init__(self, me, run, src, dst):
        self.me, self.run, self.src, self.dst = me, run, src, dst

    def slot(self, z, x, y):
        return ((z * 2 + x) * 2 + self.me.core) * 2 + y

    def steps(self, cut):
        me, run, src, dst, slot = self.me, self.run, self.src, self.dst, self.slot
        low, middle, high = cut
        first, second, whole = slice(low, middle), slice(middle, high), slice(low, high)
        own = dst.at[slot(me.z, me.x, me.y)]
        run.later(src.at[whole], own.at[whole])
        from_z = [run.remote(src.at[whole], own.at[whole], me.along_z(k)) for k in range(1, me.n_z)]
        xa, xb, ya, yb, late_a, late_b = [], [], [], [], [], []

        def fan(k):
            here = dst.at[slot(me.z_before(k), me.x, me.y)]
            if k:
                run.arrive(from_z[k - 1])
            there = here if k else src
            xa.append(run.remote(there.at[first], here.at[first], me.across_x()))
            yb.append(run.remote(there.at[second], here.at[second], me.across_y()))
            ya.append(run.remote(there.at[first], here.at[first], me.across_y()))
            xb.append(run.remote(there.at[second], here.at[second], me.across_x()))
            run.remote(there.at[whole], here.at[whole], me.across_core())

        def relay(k):
            z = me.z_before(k)
            run.arrive(xa[k])
            part = dst.at[slot(z, 1 - me.x, me.y), first]
            late_a.append(run.remote(part, part, me.across_y()))
            run.arrive(yb[k])
            part = dst.at[slot(z, me.x, 1 - me.y), second]
            late_b.append(run.remote(part, part, me.across_x()))

        def hand_over(k):
            z = me.z_before(k)
            run.arrive(xb[k])
            part = dst.at[slot(z, 1 - me.x, me.y), whole]
            run.remote(part, part, me.across_core())
            run.arrive(ya[k])
            part = dst.at[slot(z, me.x, 1 - me.y), whole]
            run.remote(part, part, me.across_core())

        def hand_last(k):
            run.arrive(late_a[k], late_b[k])
            part = dst.at[slot(me.z_before(k), 1 - me.x, 1 - me.y), whole]
            run.remote(part, part, me.across_core())

        for i in range(me.n_z + 3):
            for lag, action in enumerate((fan, relay, hand_over, hand_last)):
                if 0 <= i - lag < me.n_z:
                    action(i - lag)
            yield


    def flat_steps(self, cut):
        me, run, src, dst = self.me, self.run, self.src, self.dst
        whole = slice(*cut)
        own = dst.at[self.slot(me.z, me.x, me.y), whole]
        keep = run.local(src.at[whole], own)
        from_y = run.remote(src.at[whole], own, me.across_y())
        run.remote(src.at[whole], own, me.across_core())
        from_z = []

        def pair(z, x):
            return dst.at[pl.ds(self.slot(z, x, 0), 2), whole]

        def along(part):
            from_z.append([run.remote(part, part, me.along_z(k)) for k in range(1, me.n_z)])

        yield
        keep.wait()
        run.arrive(from_y)
        part = pair(me.z, me.x)
        from_x = run.remote(part, part, me.across_x())
        along(part)
        part = dst.at[self.slot(me.z, me.x, 1 - me.y), whole]
        run.remote(part, part, me.across_core())
        yield
        run.arrive(from_x)
        part = pair(me.z, 1 - me.x)
        along(part)
        run.remote(part, part, me.across_core())
        yield
        for k in range(1, me.n_z):
            for i, x in enumerate((me.x, 1 - me.x)):
                run.arrive(from_z[i][k - 1])
                part = pair(me.z_before(k), x)
                run.remote(part, part, me.across_core())
            yield


class ChipSum:
    def __init__(self, me, run, src, own, far, over):
        self.me, self.run, self.src, self.own, self.far, self.over = me, run, src, own, far, over
        self.sent = []

    def send(self, times=1):
        for _ in range(times):
            z = self.me.z_after(len(self.sent) + 1)
            piece = self.src.at[z * 2 + 1 - self.me.x]
            self.sent.append(self.run.remote(piece, self.far.at[z], self.me.across_x()))

    def steps(self, place, then=None):
        me, run = self.me, self.run
        along = []
        for k in range(1, me.n_z + 1):
            z = me.z_after(k)
            run.arrive(self.sent[k - 1])
            if then is not None:
                then()
            part = self.own(z)
            part[...] = add(part[...], self.far[z]).astype(jnp.bfloat16)
            if k < me.n_z:
                along.append(run.remote(part, self.over.at[k - 1], me.along_z(k)))
            yield
        run.arrive(*along)
        place(add(self.own(me.z)[...], *[self.over[k] for k in range(me.n_z - 1)]))
        yield


class QuadSum:
    def __init__(self, me, run, src, own, near, over):
        self.me, self.run, self.own, self.near, self.over = me, run, own, near, over
        self.src, self.given = src, []

    def start(self, y):
        me = self.me
        self.given.append(self.run.remote(self.src.at[2 * (1 - me.core) + y], self.near.at[y], me.across_core()))

    def cross(self, step=128):
        me, own, near = self.me, self.own, self.near
        self.run.arrive(self.given[0])

        @pl.loop(0, self.over.shape[0], step=step)
        def _(i):
            rows = at(i, step, step)
            own[1 - me.y, rows, :] = add(own[1 - me.y, rows, :], near[1 - me.y, rows, :]).astype(jnp.bfloat16)

        self.over_y = self.run.remote(own.at[1 - me.y], self.over, me.across_y())

    def landed(self):
        self.run.arrive(self.given[1], self.over_y)

    def rows(self, rows):
        y = self.me.y
        return add(self.own[y, rows, :], self.near[y, rows, :], self.over[rows, :])


def head_back(qkv, o, lse, do, dqkv, sum_k, sum_v, g, head, heads, size, count, stops, slope):
    scale = size**-0.5
    start = g * count
    sum_k[...] = jnp.zeros_like(sum_k)
    sum_v[...] = jnp.zeros_like(sum_v)

    def columns(part):
        return slice((part * heads + head) * size, (part * heads + head + 1) * size)

    mine = columns(0)
    for first in range(0, count, 256):
        seen = first + 256
        here, past = slice(start + first, start + seen), slice(start, start + seen)
        allowed, bias = allowed_and_bias(first, 256, seen, stops, slope)
        query, keys = qkv[here, mine], qkv[past, columns(1)]
        s = times_transposed(query, keys) * scale + bias
        p = jnp.exp(jnp.where(allowed, s, NEVER) - lse[g, head, first:seen])
        grad = do[here, mine]
        dots = jnp.sum(grad.astype(jnp.float32) * o[here, mine].astype(jnp.float32), axis=-1, keepdims=True)
        sum_v[:seen] += inner_rows(p.astype(jnp.bfloat16), grad)
        ds = (p * (times_transposed(grad, qkv[past, columns(2)]) - dots)).astype(jnp.bfloat16)
        dqkv[here, mine] = (jnp.dot(ds, keys, preferred_element_type=jnp.float32) * scale).astype(jnp.bfloat16)
        sum_k[:seen] += inner_rows(ds, query)
    dqkv[start : start + count, columns(1)] = (sum_k[...] * scale).astype(jnp.bfloat16)
    dqkv[start : start + count, columns(2)] = sum_v[...].astype(jnp.bfloat16)


def norm_parts(values):
    mean = jnp.mean(values, axis=-1, keepdims=True)
    centred = values - mean
    variance = jnp.mean(centred * centred, axis=-1, keepdims=True)
    factor = lax.rsqrt(variance + EPS)
    return centred * factor, factor


def norm_back_rows(grad, unit, factor, gain):
    scaled = grad * gain
    centre = jnp.mean(scaled, axis=-1, keepdims=True)
    along = jnp.mean(scaled * unit, axis=-1, keepdims=True)
    return factor * (scaled - centre - unit * along)


def gelu_and_slope(u):
    root, cube = 0.7978845608028654, 0.044715
    square = u * u
    t = jnp.tanh(root * u * (1.0 + cube * square))
    half = 0.5 * (1.0 + t)
    return u * half, half + 0.5 * u * (1.0 - t * t) * (root * (1.0 + 3.0 * cube * square))


def back_kernel(
    n_z,
    n_items,
    H2,
    C,
    WU,
    WD,
    MID,
    cot_in,
    tok_in,
    H1,
    QKV,
    O,
    LSE,
    WQ,
    WOQ,
    LQ,
    b_up,
    attn_gain,
    ffn_gain,
    b_down,
    BLOCK_OUT,
    GRAD_TOKENS,
    SHARED,
    rows_c,
    rows_h2,
    rows_a,
    rows_du,
    mat_u,
    mat_d,
    part_h2,
    near_h2,
    over_h2,
    part_out,
    near_out,
    over_out,
    grad_d,
    far_d,
    over_d,
    grad_u,
    far_u,
    over_u,
    middle,
    cot,
    lse,
    ends,
    branch,
    sum_k,
    sum_v,
    acc_o,
    grad_q,
    far_q,
    over_q,
    grad_o,
    far_o,
    over_o,
    small,
    slab,
    send,
    recv,
    near,
):
    me = Place(n_z)
    run = Copies(send, recv, near)
    quarter = me.quarter
    other, beside, far = 2 * (1 - me.core) + me.y, 2 * me.core + 1 - me.y, 2 * (1 - me.core) + 1 - me.y
    low, f32 = jnp.bfloat16, jnp.float32
    chips = 2 * n_z
    local, width = tok_in.shape
    count, half = 2 * local, local // 2
    size = width // HEADS
    heads = HEADS // 4
    rows = grad_d.shape[1]
    few = grad_o.shape[1]
    cols = 3 * heads * size
    meet(
        [me.across_core(), me.across_x(), me.across_y()] + [me.along_z(k) for k in range(1, n_z)]
    )
    load_up = [run.local(a, b) for a, b in ((H2, rows_h2), (WU, mat_u))]
    load_down = [run.local(a, b) for a, b in ((C, rows_c), (WD, mat_d))]
    load_mid = [run.local(MID, middle), run.local(cot_in, cot)]
    load_few = [run.local(a, b) for a, b in ((LSE, lse), (LQ, ends))]
    small[...] = jnp.zeros_like(small)
    acc_o[...] = jnp.zeros_like(acc_o)
    group = pl.ds(2 * me.core, 2)
    sum_h2 = QuadSum(me, run, part_h2, part_h2.at[group], near_h2, over_h2)
    sum_out = QuadSum(me, run, part_out, part_out.at[group], near_out, over_out)
    down = ChipSum(me, run, grad_d, lambda z: grad_d.at[z * 2 + me.x], far_d, over_d)
    up = ChipSum(me, run, grad_u, lambda z: grad_u.at[z * 2 + me.x], far_u, over_u)

    def feed(block):
        @pl.loop(0, local, step=256)
        def _(i):
            here, there = at(i, 256, 256), at(block * local + i, 256, 256)
            values, grads = rows_h2[there, :], rows_c[there, :]
            for j in range(0, width, 256):
                part = slice(j, j + 256)
                u = jnp.dot(values, mat_u[:, part], preferred_element_type=f32) + b_up[:, part]
                bent, slope = gelu_and_slope(u)
                rows_a[there, part] = bent.astype(low)
                du = times_transposed(grads, mat_d[part, :]) * slope
                rows_du[block, here, part] = du.astype(low)
                small[5:6, part] += jnp.sum(du, axis=0, keepdims=True)
            part_h2[block, here, :] = times_transposed(rows_du[block, here, :], mat_u[...]).astype(low)

    def feed_out(block):
        @pl.loop(0, local, step=256)
        def _(i):
            here, there = at(i, 256, 256), at(block * local + i, 256, 256)
            part_out[block, here, :] = jnp.dot(rows_a[there, :], mat_d[...], preferred_element_type=f32).astype(low)

    def weight_grad(into, left, right):
        @pl.loop(0, chips // 2)
        def _(i):
            columns = at(i * 2 * rows, 2 * rows, 128)
            total = inner_rows(left(columns, 0), right(0))
            for block in range(1, 4):
                total = total + inner_rows(left(columns, block), right(block))
            into[pl.ds(2 * i, 2)] = total.reshape(2, rows, total.shape[1]).astype(low)

    def block_rows(block):
        return slice(block * local, (block + 1) * local)

    share = Share(me, run, slab, SHARED)

    def to_slab(start, columns=slice(None)):
        def place(value):
            slab[start : start + value.shape[0], columns] = value.astype(low)

        return place

    base = 2 * rows + few
    kept = rows - few

    def place_q(value):
        slab[base : base + kept, :cols] = value[:kept].astype(low)
        for i in range(3):
            slab[base + i * few : base + (i + 1) * few, cols:] = value[
                kept:, i * heads * size : (i + 1) * heads * size
            ].astype(low)

    def both(start):
        flat = share.flat_steps((start, start + 16))
        for _ in share.steps((start + 16, start + rows // 2, start + rows)):
            next(flat, None)
            yield
        yield from flat

    def chain(total, place, *then):
        yield from total.steps(place)
        for thread in then:
            yield from thread

    run_down = chain(down, to_slab(0), both(0))
    run_up = chain(up, to_slab(rows), both(rows))

    def pump(thread, times=1):
        for _ in range(times):
            next(thread, None)

    for copy in load_up + load_down:
        copy.wait()
    feed(far)
    sum_h2.start(1 - me.y)
    feed(other)
    sum_h2.start(me.y)
    feed(beside)
    sum_h2.cross()
    feed(quarter)
    weight_grad(grad_d, lambda columns, b: rows_a[block_rows(b), columns], lambda b: rows_c[block_rows(b), :])
    down.send(n_z)
    weight_grad(grad_u, lambda columns, b: rows_h2[block_rows(b), columns], lambda b: rows_du[b])
    up.send(n_z)
    pump(run_down)
    feed_out(far)
    sum_out.start(1 - me.y)
    feed_out(other)
    sum_out.start(me.y)
    pump(run_down)
    feed_out(beside)
    feed_out(quarter)
    qkv, o = rows_c.at[:, :cols], rows_c.at[:, cols:]
    dqkv, do = rows_h2.at[:, :cols], rows_h2.at[:, cols:]
    h1, part_h1 = rows_a, rows_du
    w_q, w_o = mat_u.at[:, :cols], mat_d.at[: heads * size]
    load_heads = [run.local(a, b) for a, b in ((WOQ, w_o), (O, o), (QKV, qkv), (H1, h1), (WQ, w_q))]
    for copy in load_mid:
        copy.wait()
    sum_h2.landed()

    @pl.loop(0, local, step=64)
    def _(i):
        here = at(i, 64, 64)
        unit, factor = norm_parts(middle[here, :])
        grad, c = sum_h2.rows(here), cot[here, :].astype(f32)
        total = c + norm_back_rows(grad, unit, factor, ffn_gain[...])
        branch[quarter, here, :] = total.astype(low)
        small[2:3] += jnp.sum(grad * unit, axis=0, keepdims=True)
        small[3:4] += jnp.sum(grad, axis=0, keepdims=True)
        small[4:5] += jnp.sum(c, axis=0, keepdims=True)

    load_few.append(run.local(tok_in, cot))
    own = branch.at[quarter]
    core_b = run.remote(own, own, me.across_core())
    over_b = []
    for h in range(2):
        part = branch.at[quarter, h * half : (h + 1) * half]
        over_b.append(run.remote(part, part, me.across_y()))
    sum_out.cross()
    pump(run_down)
    for copy in load_heads + load_few:
        copy.wait()

    def project_back(block, start, size_b):
        @pl.loop(0, size_b, step=256)
        def _(i):
            here = at(start + i, 256, 256)
            there = at(block * local + start + i, 256, 256)
            values = branch[block, here, :]
            do[there, :] = times_transposed(values, w_o[...]).astype(low)
            acc_o[...] += inner_rows(o[there, :], values)

    project_back(quarter, 0, local)
    run.arrive(core_b)
    pump(run_down)
    project_back(other, 0, local)
    pump(run_up)
    far_b = []
    for h in range(2):
        run.arrive(over_b[h])
        part = branch.at[beside, h * half : (h + 1) * half]
        far_b.append(run.remote(part, part, me.across_core()))
        project_back(beside, h * half, half)
        pump(run_down)
        pump(run_up)
    for h in range(2):
        run.arrive(far_b[h])
        project_back(far, h * half, half)
    grad_o[...] = acc_o[...].reshape(chips, few, width).astype(low)
    total_o = ChipSum(me, run, grad_o, lambda z: grad_o.at[z * 2 + me.x], far_o, over_o)
    total_o.send(n_z)
    between = [[run_down], [run_up], [run_down], [run_up]]
    run_o = chain(total_o, to_slab(2 * rows), share.flat_steps((2 * rows, base)))
    for g in range(2):
        stops = []
        end = 0
        for item in range(n_items - 1):
            end = end + ends[g, 0, item]
            stops.append(end)
        for head in range(heads):
            slope = jnp.exp2(-(jnp.zeros((1, 1), f32) + (quarter * heads + head + 1)))
            head_back(qkv, o, lse, do, dqkv, sum_k, sum_v, g, head, heads, size, count, stops, slope)
            for thread in between[2 * g + head]:
                pump(thread)

    weight_grad(grad_q, lambda columns, b: h1[block_rows(b), columns], lambda b: dqkv[block_rows(b), :])
    total_q = ChipSum(me, run, grad_q, lambda z: grad_q.at[z * 2 + me.x], far_q, over_q)
    total_q.send(n_z)

    def project_in(block):
        @pl.loop(0, local, step=256)
        def _(i):
            part_h1[block, at(i, 256, 256), :] = times_transposed(
                dqkv[at(block * local + i, 256, 256), :], w_q[...]
            ).astype(low)

    project_in(far)
    sum_h1 = QuadSum(me, run, part_h1, part_h1.at[group], near_h2, over_h2)
    sum_h1.start(1 - me.y)
    project_in(other)
    sum_h1.start(me.y)
    project_in(beside)
    sum_h1.cross()
    project_in(quarter)
    run_q = chain(total_q, place_q, share.steps((base, base + 16, base + 48)))
    pump(run_o, 5)
    pump(run_down, 1)
    pump(run_q, 1)
    pump(run_up, 1)
    pump(run_q, 1)
    pump(run_o, 1)
    pump(run_down, 1)
    pump(run_q, 1)
    pump(run_up, 1)
    pump(run_q, 1)
    sum_out.landed()

    @pl.loop(0, local, step=64)
    def _(i):
        here = at(i, 64, 64)
        part_out[quarter, here, :] = (middle[here, :] + sum_out.rows(here) + b_down[...]).astype(low)

    run.later(part_out.at[quarter], BLOCK_OUT)
    pump(run_o, 1)
    pump(run_down, 2)
    pump(run_q, 2)
    pump(run_up, 1)
    sum_h1.landed()

    @pl.loop(0, local, step=64)
    def _(i):
        here = at(i, 64, 64)
        unit, factor = norm_parts(cot[here, :].astype(f32))
        grad = sum_h1.rows(here)
        base = branch[quarter, here, :].astype(f32)
        cot[here, :] = (base + norm_back_rows(grad, unit, factor, attn_gain[...])).astype(low)
        small[0:1] += jnp.sum(grad * unit, axis=0, keepdims=True)
        small[1:2] += jnp.sum(grad, axis=0, keepdims=True)

    run.later(cot, GRAD_TOKENS)
    slab[3 * rows :, :] = small[...].astype(low)
    last = share.steps((base + 48, base + 80, slab.shape[0]))
    threads = [run_q, run_up, run_o, run_down, last]
    for _ in range(12):
        for thread in threads:
            pump(thread)
    run.finish()


def back(n_z, n_items, feed, mid, cot, tok, saved, lq, b_up, attn_gain, ffn_gain, b_down):
    low, f32 = jnp.bfloat16, jnp.float32
    local, width = tok.shape
    chips = 2 * n_z
    heads, size = HEADS // 4, width // HEADS
    rows, few = width // chips, width // 4 // chips
    cols = 3 * heads * size
    shape = jax.ShapeDtypeStruct
    block, four, flat = (local, width), (4, local, width), (4 * local, width)
    deep = 3 * rows + 16
    v = pltpu.VMEM

    def sums(piece):
        return [v((chips,) + piece, low), v((n_z,) + piece, low), v((n_z - 1,) + piece, low)]

    scratch = (
        [v(flat, low)] * 3
        + [v(four, low)]
        + [v((width, width), low)] * 2
        + [v(four, low), v((2,) + block, low), v(block, low)] * 2
        + sums((rows, width)) * 2
        + [v(block, f32), v(block, low), v(saved[3].shape, f32), pltpu.SMEM(lq.shape, lq.dtype)]
        + [v(four, low)]
        + [v((2 * local, size), f32)] * 2
        + [v((heads * size, width), f32)]
        + sums((rows, cols))
        + sums((few, width))
        + [v((16, width), f32), v((deep, width), low)]
    )
    return communicate(
        functools.partial(back_kernel, n_z, n_items),
        [shape(block, low), shape(block, low), shape((4 * chips, deep, width), low)],
        tuple(feed) + (mid, cot, tok) + tuple(saved) + (lq, b_up, attn_gain, ffn_gain, b_down),
        [HBM] * 3,
        [HBM] * (len(feed) + 3 + len(saved) + 1) + [VMEM] * 4,
        (320, 48),
        scratch,
        call_id=2,
        limit=63 << 20,
    )


def unfold_kernel(rows, head_cols, few, shared, down, up, qkv, out, small, bias):
    f32 = jnp.float32
    width = shared.shape[-1]
    chips = up.shape[1] // width * 2
    unit = width // chips
    third = qkv.shape[1] // 3

    @pl.when(pl.program_id(0) == 0)
    def _():
        small[...] = jnp.zeros_like(small)
        bias[...] = jnp.zeros_like(bias)

    for q in range(4):
        down[q * rows : (q + 1) * rows] = shared[q, :rows].astype(f32)
        for s in range(chips):
            start = (s * 4 + q) * unit
            up[:, start : start + unit] = shared[q, rows : 2 * rows, s * unit : (s + 1) * unit].astype(f32)
        base, kept = 2 * rows + few, rows - few
        for i in range(3):
            here = slice(i * third + q * head_cols, i * third + (q + 1) * head_cols)
            qkv[:kept, here] = shared[q, base : base + kept, i * head_cols : (i + 1) * head_cols].astype(f32)
            qkv[kept:, here] = shared[q, base + i * few : base + (i + 1) * few, 3 * head_cols :].astype(f32)
        out[q] = shared[q, 2 * rows : base].astype(f32)
        extra = shared[q, 3 * rows :].astype(f32)
        small[...] += extra
        bias[q : q + 1] += extra[5:6]


def unfold(shared, rows, few, ff):
    devices, deep, width = shared.shape
    chips = devices // 4
    f32 = jnp.float32
    head_cols = width // 4
    return pl.pallas_call(
        functools.partial(unfold_kernel, rows, head_cols, few),
        grid=(chips,),
        in_specs=[pl.BlockSpec((4, deep, width), lambda s: (s, 0, 0))],
        out_specs=[
            pl.BlockSpec((4 * rows, width), lambda s: (s, 0)),
            pl.BlockSpec((rows, ff), lambda s: (s, 0)),
            pl.BlockSpec((rows, 3 * width), lambda s: (s, 0)),
            pl.BlockSpec((4, None, few, width), lambda s: (0, s, 0, 0)),
            pl.BlockSpec((deep - 3 * rows, width), lambda s: (0, 0)),
            pl.BlockSpec((4, width), lambda s: (0, 0)),
        ],
        out_shape=[
            jax.ShapeDtypeStruct((ff, width), f32),
            jax.ShapeDtypeStruct((width, ff), f32),
            jax.ShapeDtypeStruct((width, 3 * width), f32),
            jax.ShapeDtypeStruct((4, chips, few, width), f32),
            jax.ShapeDtypeStruct((deep - 3 * rows, width), f32),
            jax.ShapeDtypeStruct((4, width), f32),
        ],
        compiler_params=pltpu.CompilerParams(vmem_limit_bytes=56 << 20),
    )(shared)


def on_quad(
    tokens,
    lengths,
    attn_gain,
    attn_shift,
    w_qkv,
    w_out,
    ffn_gain,
    ffn_shift,
    w_up,
    b_up,
    w_down,
    b_down,
    cotangent,
):
    low = jnp.bfloat16
    local, width = tokens.shape
    n_dp = lax.axis_size("dp")
    n_z, chips = n_dp // 4, n_dp // 2
    size = width // HEADS
    heads = HEADS // 4
    count = 2 * local
    me = Place(n_z)
    lens = jnp.zeros((8, 128), jnp.int32).at[:1, : lengths.shape[1]].set(lengths)
    gains = [value.reshape(1, width) for value in (attn_gain, attn_shift, ffn_gain, ffn_shift)]
    WQ, WOQ, WU, WD, CQ, h1, qkv, o, lse, h2, middle, LQ = front(
        n_z, lengths.shape[1], w_qkv, w_out, w_up, w_down, tokens, cotangent, lens, gains
    )
    unit = w_up.shape[1] // chips // 4
    bias = lax.dynamic_index_in_dim(b_up.reshape(chips, 4, unit), me.quarter, 1, keepdims=False).reshape(-1)
    block_out, grad_tokens, shared = back(
        n_z,
        lengths.shape[1],
        [h2, CQ.reshape(4 * local, width), WU, WD],
        middle,
        cotangent,
        tokens,
        [h1.reshape(4 * local, width), qkv, o, lse, WQ, WOQ],
        LQ,
        bias.reshape(1, width),
        gains[0],
        gains[2],
        b_down.reshape(1, width),
    )
    rows, few = width // chips, width // 4 // chips
    ff = w_up.shape[1]
    grad_w_down, grad_w_up, grad_w_qkv, grad_w_out, vectors, bias = unfold(shared, rows, few, ff)
    return (
        block_out,
        grad_tokens,
        vectors[0],
        vectors[1],
        grad_w_qkv,
        grad_w_out.reshape(width, width),
        vectors[2],
        vectors[3],
        grad_w_up,
        jnp.transpose(bias.reshape(4, chips, unit), (1, 0, 2)).reshape(ff),
        grad_w_down,
        vectors[4],
    )


def solution(mesh):
    n_dp, n_seq = mesh.shape["dp"], mesh.shape["seq"]
    quad = n_seq == 2 and n_dp % 4 == 0 and n_dp >= 8 and n_dp <= 16
    return jax.shard_map(
        on_quad if quad else on_device,
        mesh=mesh,
        in_specs=(
            P(("dp", "seq"), None),
            P("dp", None),
            P(),
            P(),
            P("dp", None),
            P("dp", None),
            P(),
            P(),
            P("dp", None),
            P(),
            P("dp", None),
            P(),
            P(("dp", "seq"), None),
        ),
        out_specs=(
            P(("dp", "seq"), None),
            P(("dp", "seq"), None),
            P(),
            P(),
            P(),
            P(),
            P(),
            P(),
            P(),
            P(),
            P(),
            P(),
        ),
        check_vma=False,
    )
```

```python
import functools

import jax
import jax.numpy as jnp
from jax import lax
from jax.experimental import pallas as pl
from jax.experimental.pallas import tpu as pltpu
from jax.sharding import PartitionSpec as P

HEADS = 8


EPS = 1e-05
NEVER = -1000000000.0


def inner_rows(left, right):
    return lax.dot_general(
        left, right, (((0,), (0,)), ((), ())), preferred_element_type=jnp.float32
    )


def times_transposed(left, right):
    return lax.dot_general(
        left, right, (((1,), (1,)), ((), ())), preferred_element_type=jnp.float32
    )


def smooth_act(values):
    return jax.nn.gelu(values, approximate=True)


def norm_forward(values, gain, shift):
    mean = jnp.mean(values, axis=-1, keepdims=True)
    centred = values - mean
    variance = jnp.mean(centred * centred, axis=-1, keepdims=True)
    factor = lax.rsqrt(variance + EPS)
    normed = centred * factor
    return (normed * gain + shift, normed, factor)


def norm_backward(grad_out, normed, factor, gain):
    grad_normed = grad_out * gain
    centre_term = jnp.mean(grad_normed, axis=-1, keepdims=True)
    along_term = jnp.mean(grad_normed * normed, axis=-1, keepdims=True)
    grad_in = factor * (grad_normed - centre_term - normed * along_term)
    return (grad_in, jnp.sum(grad_out * normed, axis=0), jnp.sum(grad_out, axis=0))


def item_ids(item_lengths, count):
    item_ends = jnp.cumsum(item_lengths, dtype=jnp.int32)
    places = jnp.arange(count, dtype=jnp.int32)
    hits = (places[:, None] >= item_ends[None, :]).astype(jnp.int32)
    return jnp.sum(hits, axis=1, dtype=jnp.int32)


def block_scores(query_block, keys, start, item_of, slopes):
    rows = query_block.shape[0]
    count = keys.shape[0]
    scale = query_block.shape[-1] ** (-0.5)
    raw = jnp.einsum("qhd,khd->hqk", query_block, keys, preferred_element_type=jnp.float32)
    row_places = start + jnp.arange(rows, dtype=jnp.int32)
    col_places = jnp.arange(count, dtype=jnp.int32)
    distance = (row_places[:, None] - col_places[None, :]).astype(jnp.float32)
    row_items = lax.dynamic_slice_in_dim(item_of, start, rows)
    allowed = (row_items[:, None] == item_of[None, :]) & (
        col_places[None, :] <= row_places[:, None]
    )
    scores = raw * scale - slopes[:, None, None] * distance[None]
    return jnp.where(allowed[None], scores, jnp.float32(-1000000000.0))


def attend(heads_qkv, item_of, slopes):
    count = heads_qkv.shape[0]
    rows = min(512, count)
    queries = heads_qkv[:, 0]
    keys = heads_qkv[:, 1]
    values = heads_qkv[:, 2]

    def one_block(index):
        start = index * rows
        query_block = lax.dynamic_slice_in_dim(queries, start, rows)
        scores = block_scores(query_block, keys, start, item_of, slopes)
        top = jnp.max(scores, axis=-1, keepdims=True)
        weights = jnp.exp(scores - top)
        total = jnp.sum(weights, axis=-1, keepdims=True)
        probs = (weights / total).astype(jnp.bfloat16)
        mixed = jnp.einsum("hqk,khd->qhd", probs, values, preferred_element_type=jnp.float32)
        return (mixed.astype(jnp.bfloat16), (top + jnp.log(total))[..., 0])

    mixed, log_norm = lax.map(one_block, jnp.arange(count // rows, dtype=jnp.int32))
    return (mixed.reshape(count, mixed.shape[2], mixed.shape[3]), log_norm)


def attend_back(heads_qkv, heads_out, grad_heads, log_norm, item_of, slopes):
    count = heads_qkv.shape[0]
    rows = min(512, count)
    queries = heads_qkv[:, 0]
    keys = heads_qkv[:, 1]
    values = heads_qkv[:, 2]
    scale = queries.shape[-1] ** (-0.5)
    row_dots = jnp.sum(grad_heads.astype(jnp.float32) * heads_out.astype(jnp.float32), axis=-1)

    def one_block(carry, index):
        grad_keys, grad_values = carry
        start = index * rows
        query_block = lax.dynamic_slice_in_dim(queries, start, rows)
        grad_block = lax.dynamic_slice_in_dim(grad_heads, start, rows)
        dots = lax.dynamic_slice_in_dim(row_dots, start, rows)
        scores = block_scores(query_block, keys, start, item_of, slopes)
        probs = jnp.exp(scores - log_norm[index][:, :, None])
        probs_low = probs.astype(jnp.bfloat16)
        grad_values = grad_values + jnp.einsum(
            "hqk,qhd->khd", probs_low, grad_block, preferred_element_type=jnp.float32
        )
        grad_probs = jnp.einsum(
            "qhd,khd->hqk", grad_block, values, preferred_element_type=jnp.float32
        )
        grad_scores = (probs * (grad_probs - jnp.transpose(dots)[:, :, None])).astype(jnp.bfloat16)
        grad_query = (
            jnp.einsum("hqk,khd->qhd", grad_scores, keys, preferred_element_type=jnp.float32)
            * scale
        )
        grad_keys = (
            grad_keys
            + jnp.einsum(
                "hqk,qhd->khd", grad_scores, query_block, preferred_element_type=jnp.float32
            )
            * scale
        )
        return ((grad_keys, grad_values), grad_query)

    empty = jnp.zeros(keys.shape, jnp.float32)
    (grad_keys, grad_values), grad_query = lax.scan(
        one_block, (empty, empty), jnp.arange(count // rows, dtype=jnp.int32)
    )
    grad_query = grad_query.reshape(keys.shape)
    return jnp.stack([grad_query, grad_keys, grad_values], axis=1).astype(jnp.bfloat16)


def on_device(
    tokens,
    lengths,
    attn_gain,
    attn_shift,
    w_qkv,
    w_out,
    ffn_gain,
    ffn_shift,
    w_up,
    b_up,
    w_down,
    b_down,
    cotangent,
):
    w_qkv, w_out, w_up, w_down = (
        lax.all_gather(w_qkv, "dp", axis=0, tiled=True),
        lax.all_gather(w_out, "dp", axis=0, tiled=True),
        lax.all_gather(w_up, "dp", axis=0, tiled=True),
        lax.all_gather(w_down, "dp", axis=0, tiled=True),
    )
    local, width = tokens.shape
    groups = lax.axis_size("seq")
    per_head = width // HEADS
    local_heads = HEADS // groups
    count = local * groups
    item_of = item_ids(lengths[0], count)
    first_head = lax.axis_index("seq") * local_heads
    exponents = (first_head + jnp.arange(local_heads, dtype=jnp.int32) + 1).astype(jnp.float32)
    slopes = jnp.exp2(-exponents)
    inputs = tokens.astype(jnp.float32)
    normed_in, unit_in, factor_in = norm_forward(inputs, attn_gain, attn_shift)
    first_in = normed_in.astype(jnp.bfloat16)
    projected = jnp.dot(first_in, w_qkv, preferred_element_type=jnp.float32).astype(jnp.bfloat16)
    projected = projected.reshape(local, 3, HEADS, per_head)
    heads_qkv = lax.all_to_all(projected, "seq", split_axis=2, concat_axis=0, tiled=True)
    heads_out, log_norm = attend(heads_qkv, item_of, slopes)
    joined = lax.all_to_all(heads_out, "seq", split_axis=0, concat_axis=1, tiled=True).reshape(
        local, width
    )
    middle = inputs + jnp.dot(joined, w_out, preferred_element_type=jnp.float32)
    normed_mid, unit_mid, factor_mid = norm_forward(middle, ffn_gain, ffn_shift)
    second_in = normed_mid.astype(jnp.bfloat16)
    pre_act = jnp.dot(second_in, w_up, preferred_element_type=jnp.float32) + b_up
    act_value, act_pull = jax.vjp(smooth_act, pre_act)
    active = act_value.astype(jnp.bfloat16)
    block_out = (
        middle + jnp.dot(active, w_down, preferred_element_type=jnp.float32) + b_down
    ).astype(jnp.bfloat16)
    grad_out = cotangent.astype(jnp.float32)
    grad_b_down = jnp.sum(grad_out, axis=0)
    grad_w_down = inner_rows(active, cotangent)
    grad_active = times_transposed(cotangent, w_down)
    grad_pre = act_pull(grad_active)[0]
    grad_b_up = jnp.sum(grad_pre, axis=0)
    grad_pre_low = grad_pre.astype(jnp.bfloat16)
    grad_w_up = inner_rows(second_in, grad_pre_low)
    grad_second = times_transposed(grad_pre_low, w_up)
    grad_mid_norm, grad_ffn_gain, grad_ffn_shift = norm_backward(
        grad_second, unit_mid, factor_mid, ffn_gain
    )
    grad_middle = grad_out + grad_mid_norm
    grad_branch = grad_middle.astype(jnp.bfloat16)
    grad_w_out = inner_rows(joined, grad_branch)
    grad_joined = (
        times_transposed(grad_branch, w_out).astype(jnp.bfloat16).reshape(local, HEADS, per_head)
    )
    grad_heads = lax.all_to_all(grad_joined, "seq", split_axis=1, concat_axis=0, tiled=True)
    grad_qkv_heads = attend_back(heads_qkv, heads_out, grad_heads, log_norm, item_of, slopes)
    grad_projected = lax.all_to_all(
        grad_qkv_heads, "seq", split_axis=0, concat_axis=2, tiled=True
    ).reshape(local, 3 * width)
    grad_w_qkv = inner_rows(first_in, grad_projected)
    grad_first = times_transposed(grad_projected, w_qkv)
    grad_in_norm, grad_attn_gain, grad_attn_shift = norm_backward(
        grad_first, unit_in, factor_in, attn_gain
    )
    grad_tokens = (grad_middle + grad_in_norm).astype(jnp.bfloat16)
    all_part = (
        lax.psum_scatter(
            grad_attn_gain.astype(jnp.bfloat16), "dp", scatter_dimension=0, tiled=True
        ).astype(jnp.float32),
        lax.psum_scatter(
            grad_attn_shift.astype(jnp.bfloat16), "dp", scatter_dimension=0, tiled=True
        ).astype(jnp.float32),
        lax.psum_scatter(
            grad_w_qkv.astype(jnp.bfloat16), "dp", scatter_dimension=0, tiled=True
        ).astype(jnp.float32),
        lax.psum_scatter(
            grad_w_out.astype(jnp.bfloat16), "dp", scatter_dimension=0, tiled=True
        ).astype(jnp.float32),
        lax.psum_scatter(
            grad_ffn_gain.astype(jnp.bfloat16), "dp", scatter_dimension=0, tiled=True
        ).astype(jnp.float32),
        lax.psum_scatter(
            grad_ffn_shift.astype(jnp.bfloat16), "dp", scatter_dimension=0, tiled=True
        ).astype(jnp.float32),
        lax.psum_scatter(
            grad_w_up.astype(jnp.bfloat16), "dp", scatter_dimension=0, tiled=True
        ).astype(jnp.float32),
        lax.psum_scatter(
            grad_b_up.astype(jnp.bfloat16), "dp", scatter_dimension=0, tiled=True
        ).astype(jnp.float32),
        lax.psum_scatter(
            grad_w_down.astype(jnp.bfloat16), "dp", scatter_dimension=0, tiled=True
        ).astype(jnp.float32),
        lax.psum_scatter(
            grad_b_down.astype(jnp.bfloat16), "dp", scatter_dimension=0, tiled=True
        ).astype(jnp.float32),
    )
    all_part = (
        lax.psum(all_part[0].astype(jnp.bfloat16), "seq").astype(jnp.float32),
        lax.psum(all_part[1].astype(jnp.bfloat16), "seq").astype(jnp.float32),
        lax.psum(all_part[2].astype(jnp.bfloat16), "seq").astype(jnp.float32),
        lax.psum(all_part[3].astype(jnp.bfloat16), "seq").astype(jnp.float32),
        lax.psum(all_part[4].astype(jnp.bfloat16), "seq").astype(jnp.float32),
        lax.psum(all_part[5].astype(jnp.bfloat16), "seq").astype(jnp.float32),
        lax.psum(all_part[6].astype(jnp.bfloat16), "seq").astype(jnp.float32),
        lax.psum(all_part[7].astype(jnp.bfloat16), "seq").astype(jnp.float32),
        lax.psum(all_part[8].astype(jnp.bfloat16), "seq").astype(jnp.float32),
        lax.psum(all_part[9].astype(jnp.bfloat16), "seq").astype(jnp.float32),
    )
    summed = (
        lax.all_gather(all_part[0].astype(jnp.bfloat16), "dp", axis=0, tiled=True).astype(
            jnp.float32
        ),
        lax.all_gather(all_part[1].astype(jnp.bfloat16), "dp", axis=0, tiled=True).astype(
            jnp.float32
        ),
        lax.all_gather(all_part[2].astype(jnp.bfloat16), "dp", axis=0, tiled=True).astype(
            jnp.float32
        ),
        lax.all_gather(all_part[3].astype(jnp.bfloat16), "dp", axis=0, tiled=True).astype(
            jnp.float32
        ),
        lax.all_gather(all_part[4].astype(jnp.bfloat16), "dp", axis=0, tiled=True).astype(
            jnp.float32
        ),
        lax.all_gather(all_part[5].astype(jnp.bfloat16), "dp", axis=0, tiled=True).astype(
            jnp.float32
        ),
        lax.all_gather(all_part[6].astype(jnp.bfloat16), "dp", axis=0, tiled=True).astype(
            jnp.float32
        ),
        lax.all_gather(all_part[7].astype(jnp.bfloat16), "dp", axis=0, tiled=True).astype(
            jnp.float32
        ),
        lax.all_gather(all_part[8].astype(jnp.bfloat16), "dp", axis=0, tiled=True).astype(
            jnp.float32
        ),
        lax.all_gather(all_part[9].astype(jnp.bfloat16), "dp", axis=0, tiled=True).astype(
            jnp.float32
        ),
    )
    return (
        block_out,
        grad_tokens,
        summed[0],
        summed[1],
        summed[2],
        summed[3],
        summed[4],
        summed[5],
        summed[6],
        summed[7],
        summed[8],
        summed[9],
    )


MESH = pl.DeviceIdType.MESH


class Place:
    def __init__(self, n_z):
        dp = lax.axis_index("dp")
        self.n_z = n_z
        self.dp = dp
        self.y = lax.axis_index("seq")
        self.core = dp % 2
        self.chip = dp // 2
        self.x = self.chip % 2
        self.z = self.chip // 2
        self.quarter = 2 * self.core + self.y

    def device(self, z=None, x=None, core=None, y=None):
        z = self.z if z is None else z
        x = self.x if x is None else x
        core = self.core if core is None else core
        y = self.y if y is None else y
        return ((z * 2 + x) * 2 + core, y)

    def across_core(self):
        return self.device(core=1 - self.core)

    def across_x(self):
        return self.device(x=1 - self.x)

    def across_y(self):
        return self.device(y=1 - self.y)

    def z_after(self, k):
        return (self.z + k) % self.n_z

    def z_before(self, k):
        return (self.z + self.n_z - k) % self.n_z

    def along_z(self, k):
        return self.device(z=self.z_after(k))


class Copy:
    def __init__(self, copy, sends, lands):
        self.copy, self.sends, self.lands, self.landed = copy, sends, lands, False

    def guarded(self, condition, action):
        if condition is None:
            action()
        else:
            pl.when(condition)(action)


class Copies:
    def __init__(self, send, recv, near):
        self.send, self.recv, self.near = send, recv, near
        self.all, self.n, self.m, self.local_open = [], 0, 0, []

    def remote(self, src, dst, device, sends=None, lands=None):
        copy = Copy(
            pltpu.make_async_remote_copy(
                src_ref=src,
                dst_ref=dst,
                send_sem=self.send.at[self.n],
                recv_sem=self.recv.at[self.n],
                device_id=device,
                device_id_type=MESH,
            ),
            sends,
            lands,
        )
        self.n += 1
        copy.guarded(sends, copy.copy.start)
        self.all.append(copy)
        return copy

    def local(self, src, dst):
        copy = pltpu.make_async_copy(src, dst, self.near.at[self.m])
        self.m += 1
        copy.start()
        return copy

    def later(self, src, dst):
        self.local_open.append(self.local(src, dst))

    def arrive(self, *copies):
        for copy in copies:
            if not copy.landed:
                copy.guarded(copy.lands, copy.copy.wait_recv)
                copy.landed = True

    def finish(self):
        self.arrive(*self.all)
        for copy in self.all:
            copy.guarded(copy.sends, copy.copy.wait_send)
        for copy in self.local_open:
            copy.wait()


class Line:
    def __init__(self, me, run, own, view):
        self.me, self.run, self.view = me, run, view
        n, z = me.n_z, me.z
        self.up = [run.remote(own, view(z), me.device(z=z + 1), z < n - 1, z > 0)]
        self.down = [run.remote(own, view(z), me.device(z=z - 1), z > 0, z < n - 1)]

    def step(self, t, then):
        me, run, n, z = self.me, self.run, self.me.n_z, self.me.z
        if t >= n:
            return
        run.arrive(self.up[t - 1])
        if t < n - 1:
            part = self.view(z - t)
            self.up.append(run.remote(part, part, me.device(z=z + 1), (z >= t) & (z < n - 1), z > t))
        then(z - t, z >= t)
        run.arrive(self.down[t - 1])
        if t < n - 1:
            part = self.view(z + t)
            self.down.append(
                run.remote(part, part, me.device(z=z - 1), (z < n - t) & (z > 0), z < n - t - 1)
            )
        then(z + t, z < n - t)


def meet(devices):
    barrier = pltpu.get_barrier_semaphore()
    for device in devices:
        pl.semaphore_signal(barrier, inc=1, device_id=device, device_id_type=MESH)
    pl.semaphore_wait(barrier, len(devices))


def at(start, size, unit):
    return pl.ds(pl.multiple_of(start, unit), size)


def communicate(kernel, out_shapes, ins, out_specs, in_specs, counts, scratch=(), call_id=0, limit=None):
    return pl.pallas_call(
        kernel,
        out_shape=out_shapes,
        in_specs=in_specs,
        out_specs=out_specs,
        scratch_shapes=list(scratch)
        + [
            pltpu.SemaphoreType.DMA((counts[0],)),
            pltpu.SemaphoreType.DMA((counts[0],)),
            pltpu.SemaphoreType.DMA((counts[1],)),
        ],
        compiler_params=pltpu.CompilerParams(
            collective_id=call_id, has_side_effects=True, vmem_limit_bytes=limit or (56 << 20)
        ),
    )(*ins)


HBM = pl.BlockSpec(memory_space=pltpu.HBM)
VMEM = pl.BlockSpec(memory_space=pltpu.VMEM)
SMEM = pl.BlockSpec(memory_space=pltpu.SMEM)


def allowed_and_bias(first, rows, count, ends, slope):
    row = first + lax.broadcasted_iota(jnp.int32, (rows, 1), 0)
    col = lax.broadcasted_iota(jnp.int32, (1, count), 1)
    begin = jnp.zeros((rows, 1), jnp.int32)
    for end in ends:
        begin = jnp.where(row >= end, end, begin)
    allowed = (col >= begin) & (col <= row)
    bias = slope * (col - first).astype(jnp.float32)
    return allowed, bias


def norm_rows(values, gain, shift):
    mean = jnp.mean(values, axis=-1, keepdims=True)
    centred = values - mean
    variance = jnp.mean(centred * centred, axis=-1, keepdims=True)
    return centred * lax.rsqrt(variance + EPS) * gain + shift


def norm_block(src, dst, gain, shift, step=64):
    @pl.loop(0, src.shape[0], step=step)
    def _(i):
        rows = at(i, step, step)
        dst[rows, :] = norm_rows(src[rows, :].astype(jnp.float32), gain[...], shift[...]).astype(dst.dtype)


def front_kernel(
    n_z,
    n_items,
    wq,
    wo,
    wu,
    wd,
    tok,
    cot,
    lens,
    attn_gain,
    attn_shift,
    ffn_gain,
    ffn_shift,
    WQ,
    WOQ,
    WU,
    WD,
    CQ,
    H1,
    QKV,
    O,
    LSE,
    H2,
    MID,
    LQ,
    q_all,
    o_all,
    x_all,
    h1,
    qkv,
    mixed,
    lse,
    h2,
    middle,
    ends,
    send,
    recv,
    near,
):
    me = Place(n_z)
    run = Copies(send, recv, near)
    quarter, other = me.quarter, 2 * (1 - me.core) + me.y
    rows = wq.shape[0]
    third = wq.shape[1] // 3
    cut = third // 4
    chips = 2 * n_z
    span = wu.shape[1] // chips
    unit = span // 4
    local = tok.shape[0]
    count = 2 * local
    half = local // 2
    size = third // HEADS
    heads = HEADS // 4
    meet(
        [me.across_core(), me.across_x(), me.across_y()] + [me.along_z(k) for k in range(1, n_z)]
    )
    mine = at(me.dp * rows, rows, 16)

    into = [q_all.at[mine, p * cut : (p + 1) * cut] for p in range(3)]
    near_q = [run.local(wq.at[:, at(p * third + quarter * cut, cut, 128)], into[p]) for p in range(3)]
    core_q = [
        run.remote(wq.at[:, at(p * third + other * cut, cut, 128)], into[p], me.across_core())
        for p in range(3)
    ]
    keep_x = run.local(tok, x_all.at[quarter])
    keep_lens = run.local(lens, LQ.at[me.core])
    core_lens = run.remote(lens, LQ.at[me.core], me.across_core())

    def halves(h):
        return slice(h * half, (h + 1) * half)

    over_x = [
        run.remote(tok.at[halves(h)], x_all.at[quarter, halves(h)], me.across_y()) for h in range(2)
    ]
    core_x = run.remote(tok, x_all.at[quarter], me.across_core())
    into = [WU.at[mine, s * unit : (s + 1) * unit] for s in range(chips)]
    near_u = [run.local(wu.at[:, at(s * span + quarter * unit, unit, 128)], into[s]) for s in range(chips)]
    core_u = [
        run.remote(wu.at[:, at(s * span + other * unit, unit, 128)], into[s], me.across_core())
        for s in range(chips)
    ]

    def pairs_of(array):
        return lambda z, x=me.x: array.at[at((z * 2 + x) * 2 * rows, 2 * rows, 16)]

    def shard_of(z, x=me.x):
        return o_all.at[at(((z * 2 + x) * 2 + me.core) * rows, rows, 16)]

    def units_of(z, x=me.x):
        return WD.at[at((z * 2 + x) * unit, unit, 16)]

    from_x = {"q": [], "o": [], "u": [], "d": []}
    share_o = []

    def across(name, view):
        def then(z, came):
            part = view(z)
            from_x[name].append((run.remote(part, part, me.across_x(), came, came), z, came))
            if name == "o":
                share_o.append(run.remote(part, part, me.across_core(), came, came))

        return then

    for copy in near_q:
        copy.wait()
    run.arrive(*core_q)
    view_q, view_u = pairs_of(q_all), pairs_of(WU)
    line_q = Line(me, run, view_q(me.z), view_q)
    across("q", view_q)(me.z, None)
    keep_o = run.local(wo, shard_of(me.z))
    keep_x.wait()
    norm_block(x_all.at[quarter], h1.at[quarter], attn_gain, attn_shift)
    run.arrive(core_x)
    line_q.step(1, across("q", view_q))
    line_o = Line(me, run, wo, shard_of)
    share_o.append(run.remote(wo, shard_of(me.z), me.across_core()))
    norm_block(x_all.at[other], h1.at[other], attn_gain, attn_shift)
    line_q.step(2, across("q", view_q))
    beside = 2 * me.core + 1 - me.y
    far = 2 * (1 - me.core) + 1 - me.y
    far_x = []
    for h in range(2):
        run.arrive(over_x[h])
        part = x_all.at[beside, halves(h)]
        far_x.append(run.remote(part, part, me.across_core()))
        if h == 0:
            line_q.step(3, across("q", view_q))
            from_x["o"].append((run.remote(wo, shard_of(me.z), me.across_x()), me.z, None))
            line_o.step(1, across("o", shard_of))
            for copy in near_u:
                copy.wait()
            run.arrive(*core_u)
            line_u = Line(me, run, view_u(me.z), view_u)
        norm_block(x_all.at[beside, halves(h)], h1.at[beside, halves(h)], attn_gain, attn_shift)
    over_c = [run.remote(cot.at[halves(0)], CQ.at[quarter, halves(0)], me.across_y())]
    run.later(cot, CQ.at[quarter])
    run.remote(cot, CQ.at[quarter], me.across_core())
    for h in range(2):
        run.arrive(far_x[h])
        norm_block(x_all.at[far, halves(h)], h1.at[far, halves(h)], attn_gain, attn_shift)
    line_o.step(2, across("o", shard_of))
    own = wd.at[at(me.y * unit, unit, 16)]
    across("u", view_u)(me.z, None)
    run.later(h1, H1)
    for copy, _, _ in from_x["q"]:
        run.arrive(copy)
    run.later(q_all, WQ)

    @pl.loop(0, 4 * local, step=256)
    def _(i):
        block = at(i, 256, 256)
        qkv[block, :] = jnp.dot(
            h1[i // local, at(i % local, 256, 256), :], q_all[...], preferred_element_type=jnp.float32
        ).astype(jnp.bfloat16)

    run.later(qkv, QKV)
    keep_lens.wait()
    run.arrive(core_lens)
    fetch = run.local(LQ, ends)
    fetch.wait()

    def heads_at(owner, head):
        return at(owner * heads * size + head * size, size, 128)

    over_o, near_o = [], []
    line_o.step(3, across("o", shard_of))
    line_d = Line(me, run, own, units_of)
    from_x["d"].append((run.remote(own, units_of(me.z), me.across_x()), me.z, None))
    run.later(own, units_of(me.z))
    pumps = [
        lambda: line_u.step(1, across("u", view_u)),
        lambda: line_u.step(2, across("u", view_u)),
        lambda: line_u.step(3, across("u", view_u)),
        lambda: line_d.step(1, across("d", units_of)),
    ]
    for g in range(2):
        stops = []
        total = 0
        for item in range(n_items - 1):
            total = total + ends[g, 0, item]
            stops.append(total)
        for head in range(heads):
            slope = jnp.exp2(-(jnp.zeros((1, 1), jnp.float32) + (quarter * heads + head + 1)))
            column = heads_at(quarter, head)
            for first in range(0, count, 256):
                start, seen = g * count, first + 256
                here = slice(start + first, start + seen)
                allowed, bias = allowed_and_bias(first, 256, seen, stops, slope)
                keys = qkv[start : start + seen, (heads + head) * size : (heads + head + 1) * size]
                s = times_transposed(qkv[here, head * size : (head + 1) * size], keys) * size**-0.5 + bias
                s = jnp.where(allowed, s, NEVER)
                top = jnp.max(s, axis=-1, keepdims=True)
                w = jnp.exp(s - top)
                sum_w = jnp.sum(w, axis=-1, keepdims=True)
                p = (w * (1.0 / sum_w)).astype(jnp.bfloat16)
                values = qkv[start : start + seen, (2 * heads + head) * size : (2 * heads + head + 1) * size]
                mixed[here, column] = jnp.dot(p, values, preferred_element_type=jnp.float32).astype(
                    jnp.bfloat16
                )
                lse[g, head, first:seen] = top + jnp.log(sum_w)
            part = mixed.at[g * count : (g + 1) * count, column]
            over_o.append(run.remote(part, part, me.across_y()))
            near_o.append(run.remote(part, part, me.across_core()))
            pumps[g * heads + head]()
    run.later(mixed.at[:, at(quarter * heads * size, heads * size, 128)], O)
    run.later(lse, LSE)
    over_c.append(run.remote(cot.at[halves(1)], CQ.at[quarter, halves(1)], me.across_y()))
    run.arrive(over_c[0])
    part = CQ.at[beside, halves(0)]
    run.remote(part, part, me.across_core())
    far_o = []
    for copy, z, came in from_x["o"]:
        run.arrive(copy)
        part = shard_of(z, 1 - me.x)
        far_o.append(run.remote(part, part, me.across_core(), came, came))
    passed = []
    for g in range(2):
        for head in range(heads):
            run.arrive(over_o[g * heads + head])
            part = mixed.at[g * count : (g + 1) * count, heads_at(beside, head)]
            passed.append(run.remote(part, part, me.across_core()))
    line_d.step(2, across("d", units_of))
    keep_o.wait()
    run.arrive(*share_o, *far_o)
    run.later(o_all.at[at(quarter * heads * size, heads * size, 16)], WOQ)
    for g in range(2):
        run.arrive(*near_o[g * heads : (g + 1) * heads], *passed[g * heads : (g + 1) * heads])

        @pl.loop(0, count, step=256)
        def _(i):
            block = at(g * count + i, 256, 256)
            owner, inner = 2 * g + i // local, at(i % local, 256, 256)
            x1 = x_all[owner, inner, :].astype(jnp.float32) + jnp.dot(
                mixed[block, :], o_all[...], preferred_element_type=jnp.float32
            )
            h2[block, :] = norm_rows(x1, ffn_gain[...], ffn_shift[...]).astype(jnp.bfloat16)

            @pl.when(owner == quarter)
            def _():
                middle[inner, :] = x1

        line_d.step(3 + g, across("d", units_of))
    run.later(h2, H2)
    run.later(middle, MID)
    run.arrive(over_c[1])
    part = CQ.at[beside, halves(1)]
    run.remote(part, part, me.across_core())
    run.finish()


def front(n_z, n_items, wq, wo, wu, wd, tok, cot, lens, gains):
    width, low, f32 = wq.shape[0] * 4 * n_z, jnp.bfloat16, jnp.float32
    quarter_ff = wu.shape[1] // 4
    local = tok.shape[0]
    heads, size = HEADS // 4, width // HEADS
    shape = jax.ShapeDtypeStruct
    shapes = [
        shape((width, wq.shape[1] // 4), low),
        shape((width // 4, width), low),
        shape((width, quarter_ff), low),
        shape((quarter_ff, width), low),
        shape((4, local, width), low),
        shape((4, local, width), low),
        shape((4 * local, 3 * width // 4), low),
        shape((4 * local, width // 4), low),
        shape((2, heads, 2 * local, 1), f32),
        shape((4 * local, width), low),
        shape((local, width), f32),
        shape((2,) + lens.shape, lens.dtype),
    ]
    scratch = [
        pltpu.VMEM((width, wq.shape[1] // 4), low),
        pltpu.VMEM((width, width), low),
        pltpu.VMEM((4, local, width), low),
        pltpu.VMEM((4, local, width), low),
        pltpu.VMEM((4 * local, 3 * width // 4), low),
        pltpu.VMEM((4 * local, width), low),
        pltpu.VMEM((2, heads, 2 * local, 1), f32),
        pltpu.VMEM((4 * local, width), low),
        pltpu.VMEM((local, width), f32),
        pltpu.SMEM((2,) + lens.shape, lens.dtype),
    ]
    return communicate(
        functools.partial(front_kernel, n_z, n_items),
        shapes,
        (wq, wo, wu, wd, tok, cot, lens) + tuple(gains),
        [HBM] * 12,
        [HBM] * 7 + [VMEM] * 4,
        (128, 32),
        scratch,
        call_id=1,
    )


def add(*values):
    total = values[0].astype(jnp.float32)
    for value in values[1:]:
        total = total + value.astype(jnp.float32)
    return total


class Share:
    def __init__(self, me, run, src, dst):
        self.me, self.run, self.src, self.dst = me, run, src, dst

    def slot(self, z, x, y):
        return ((z * 2 + x) * 2 + self.me.core) * 2 + y

    def steps(self, cut):
        me, run, src, dst, slot = self.me, self.run, self.src, self.dst, self.slot
        low, middle, high = cut
        first, second, whole = slice(low, middle), slice(middle, high), slice(low, high)
        own = dst.at[slot(me.z, me.x, me.y)]
        run.later(src.at[whole], own.at[whole])
        from_z = [run.remote(src.at[whole], own.at[whole], me.along_z(k)) for k in range(1, me.n_z)]
        xa, xb, ya, yb, late_a, late_b = [], [], [], [], [], []
        yield

        def fan(k):
            here = dst.at[slot(me.z_before(k), me.x, me.y)]
            if k:
                run.arrive(from_z[k - 1])
            there = here if k else src
            xa.append(run.remote(there.at[first], here.at[first], me.across_x()))
            yb.append(run.remote(there.at[second], here.at[second], me.across_y()))
            ya.append(run.remote(there.at[first], here.at[first], me.across_y()))
            xb.append(run.remote(there.at[second], here.at[second], me.across_x()))
            run.remote(there.at[whole], here.at[whole], me.across_core())

        def relay(k):
            z = me.z_before(k)
            run.arrive(xa[k])
            part = dst.at[slot(z, 1 - me.x, me.y), first]
            late_a.append(run.remote(part, part, me.across_y()))
            run.arrive(yb[k])
            part = dst.at[slot(z, me.x, 1 - me.y), second]
            late_b.append(run.remote(part, part, me.across_x()))

        def hand_over(k):
            z = me.z_before(k)
            run.arrive(xb[k])
            part = dst.at[slot(z, 1 - me.x, me.y), whole]
            run.remote(part, part, me.across_core())
            run.arrive(ya[k])
            part = dst.at[slot(z, me.x, 1 - me.y), whole]
            run.remote(part, part, me.across_core())

        def hand_last(k):
            run.arrive(late_a[k], late_b[k])
            part = dst.at[slot(me.z_before(k), 1 - me.x, 1 - me.y), whole]
            run.remote(part, part, me.across_core())

        for i in range(me.n_z + 3):
            for lag, action in enumerate((fan, relay, hand_over, hand_last)):
                if 0 <= i - lag < me.n_z:
                    action(i - lag)
            yield


    def flat_steps(self, cut):
        me, run, src, dst = self.me, self.run, self.src, self.dst
        whole = slice(*cut)
        own = dst.at[self.slot(me.z, me.x, me.y), whole]
        keep = run.local(src.at[whole], own)
        from_y = run.remote(src.at[whole], own, me.across_y())
        run.remote(src.at[whole], own, me.across_core())
        from_z = []

        def pair(z, x):
            return dst.at[pl.ds(self.slot(z, x, 0), 2), whole]

        def along(part):
            from_z.append([run.remote(part, part, me.along_z(k)) for k in range(1, me.n_z)])

        yield
        keep.wait()
        run.arrive(from_y)
        part = pair(me.z, me.x)
        from_x = run.remote(part, part, me.across_x())
        along(part)
        part = dst.at[self.slot(me.z, me.x, 1 - me.y), whole]
        run.remote(part, part, me.across_core())
        yield
        run.arrive(from_x)
        part = pair(me.z, 1 - me.x)
        along(part)
        run.remote(part, part, me.across_core())
        yield
        for k in range(1, me.n_z):
            for i, x in enumerate((me.x, 1 - me.x)):
                run.arrive(from_z[i][k - 1])
                part = pair(me.z_before(k), x)
                run.remote(part, part, me.across_core())
            yield


class ChipSum:
    def __init__(self, me, run, src, own, far, over):
        self.me, self.run, self.src, self.own, self.far, self.over = me, run, src, own, far, over
        self.sent = []

    def send(self, times=1):
        for _ in range(times):
            z = self.me.z_after(len(self.sent) + 1)
            piece = self.src.at[z * 2 + 1 - self.me.x]
            self.sent.append(self.run.remote(piece, self.far.at[z], self.me.across_x()))

    def steps(self, place, then=None):
        me, run = self.me, self.run
        along = []
        for k in range(1, me.n_z + 1):
            z = me.z_after(k)
            run.arrive(self.sent[k - 1])
            if then is not None:
                then()
            part = self.own(z)
            part[...] = add(part[...], self.far[z]).astype(jnp.bfloat16)
            if k < me.n_z:
                along.append(run.remote(part, self.over.at[k - 1], me.along_z(k)))
            yield
        run.arrive(*along)
        place(add(self.own(me.z)[...], *[self.over[k] for k in range(me.n_z - 1)]))
        yield


class QuadSum:
    def __init__(self, me, run, src, own, near, over):
        self.me, self.run, self.own, self.near, self.over = me, run, own, near, over
        self.src, self.given = src, []

    def start(self, y):
        me = self.me
        self.given.append(self.run.remote(self.src.at[2 * (1 - me.core) + y], self.near.at[y], me.across_core()))

    def cross(self, step=128):
        me, own, near = self.me, self.own, self.near
        self.run.arrive(self.given[0])

        @pl.loop(0, self.over.shape[0], step=step)
        def _(i):
            rows = at(i, step, step)
            own[1 - me.y, rows, :] = add(own[1 - me.y, rows, :], near[1 - me.y, rows, :]).astype(jnp.bfloat16)

        self.over_y = self.run.remote(own.at[1 - me.y], self.over, me.across_y())

    def landed(self):
        self.run.arrive(self.given[1], self.over_y)

    def rows(self, rows):
        y = self.me.y
        return add(self.own[y, rows, :], self.near[y, rows, :], self.over[rows, :])


def head_back(qkv, o, lse, do, dqkv, sum_k, sum_v, g, head, heads, size, count, stops, slope):
    scale = size**-0.5
    start = g * count
    sum_k[...] = jnp.zeros_like(sum_k)
    sum_v[...] = jnp.zeros_like(sum_v)

    def columns(part):
        return slice((part * heads + head) * size, (part * heads + head + 1) * size)

    mine = columns(0)
    for first in range(0, count, 256):
        seen = first + 256
        here, past = slice(start + first, start + seen), slice(start, start + seen)
        allowed, bias = allowed_and_bias(first, 256, seen, stops, slope)
        query, keys = qkv[here, mine], qkv[past, columns(1)]
        s = times_transposed(query, keys) * scale + bias
        p = jnp.exp(jnp.where(allowed, s, NEVER) - lse[g, head, first:seen])
        grad = do[here, mine]
        dots = jnp.sum(grad.astype(jnp.float32) * o[here, mine].astype(jnp.float32), axis=-1, keepdims=True)
        sum_v[:seen] += inner_rows(p.astype(jnp.bfloat16), grad)
        ds = (p * (times_transposed(grad, qkv[past, columns(2)]) - dots)).astype(jnp.bfloat16)
        dqkv[here, mine] = (jnp.dot(ds, keys, preferred_element_type=jnp.float32) * scale).astype(jnp.bfloat16)
        sum_k[:seen] += inner_rows(ds, query)
    dqkv[start : start + count, columns(1)] = (sum_k[...] * scale).astype(jnp.bfloat16)
    dqkv[start : start + count, columns(2)] = sum_v[...].astype(jnp.bfloat16)


def norm_parts(values):
    mean = jnp.mean(values, axis=-1, keepdims=True)
    centred = values - mean
    variance = jnp.mean(centred * centred, axis=-1, keepdims=True)
    factor = lax.rsqrt(variance + EPS)
    return centred * factor, factor


def norm_back_rows(grad, unit, factor, gain):
    scaled = grad * gain
    centre = jnp.mean(scaled, axis=-1, keepdims=True)
    along = jnp.mean(scaled * unit, axis=-1, keepdims=True)
    return factor * (scaled - centre - unit * along)


def gelu_and_slope(u):
    root, cube = 0.7978845608028654, 0.044715
    square = u * u
    t = jnp.tanh(root * u * (1.0 + cube * square))
    half = 0.5 * (1.0 + t)
    return u * half, half + 0.5 * u * (1.0 - t * t) * (root * (1.0 + 3.0 * cube * square))


def back_kernel(
    n_z,
    n_items,
    H2,
    C,
    WU,
    WD,
    MID,
    cot_in,
    tok_in,
    H1,
    QKV,
    O,
    LSE,
    WQ,
    WOQ,
    LQ,
    b_up,
    attn_gain,
    ffn_gain,
    b_down,
    BLOCK_OUT,
    GRAD_TOKENS,
    SHARED,
    rows_c,
    rows_h2,
    rows_a,
    rows_du,
    mat_u,
    mat_d,
    part_h2,
    near_h2,
    over_h2,
    part_out,
    near_out,
    over_out,
    grad_d,
    far_d,
    over_d,
    grad_u,
    far_u,
    over_u,
    middle,
    cot,
    lse,
    ends,
    branch,
    sum_k,
    sum_v,
    acc_o,
    grad_q,
    far_q,
    over_q,
    grad_o,
    far_o,
    over_o,
    small,
    slab,
    send,
    recv,
    near,
):
    me = Place(n_z)
    run = Copies(send, recv, near)
    quarter = me.quarter
    other, beside, far = 2 * (1 - me.core) + me.y, 2 * me.core + 1 - me.y, 2 * (1 - me.core) + 1 - me.y
    low, f32 = jnp.bfloat16, jnp.float32
    chips = 2 * n_z
    local, width = tok_in.shape
    count, half = 2 * local, local // 2
    size = width // HEADS
    heads = HEADS // 4
    rows = grad_d.shape[1]
    few = grad_o.shape[1]
    cols = 3 * heads * size
    meet(
        [me.across_core(), me.across_x(), me.across_y()] + [me.along_z(k) for k in range(1, n_z)]
    )
    load_up = [run.local(a, b) for a, b in ((H2, rows_h2), (WU, mat_u))]
    load_down = [run.local(a, b) for a, b in ((C, rows_c), (WD, mat_d))]
    load_mid = [run.local(MID, middle), run.local(cot_in, cot)]
    load_few = [run.local(a, b) for a, b in ((LSE, lse), (LQ, ends))]
    small[...] = jnp.zeros_like(small)
    acc_o[...] = jnp.zeros_like(acc_o)
    group = pl.ds(2 * me.core, 2)
    sum_h2 = QuadSum(me, run, part_h2, part_h2.at[group], near_h2, over_h2)
    sum_out = QuadSum(me, run, part_out, part_out.at[group], near_out, over_out)
    down = ChipSum(me, run, grad_d, lambda z: grad_d.at[z * 2 + me.x], far_d, over_d)
    up = ChipSum(me, run, grad_u, lambda z: grad_u.at[z * 2 + me.x], far_u, over_u)

    def feed(block):
        @pl.loop(0, local, step=256)
        def _(i):
            here, there = at(i, 256, 256), at(block * local + i, 256, 256)
            values, grads = rows_h2[there, :], rows_c[there, :]
            for j in range(0, width, 256):
                part = slice(j, j + 256)
                u = jnp.dot(values, mat_u[:, part], preferred_element_type=f32) + b_up[:, part]
                bent, slope = gelu_and_slope(u)
                rows_a[there, part] = bent.astype(low)
                du = times_transposed(grads, mat_d[part, :]) * slope
                rows_du[block, here, part] = du.astype(low)
                small[5:6, part] += jnp.sum(du, axis=0, keepdims=True)
            part_h2[block, here, :] = times_transposed(rows_du[block, here, :], mat_u[...]).astype(low)

    def feed_out(block):
        @pl.loop(0, local, step=256)
        def _(i):
            here, there = at(i, 256, 256), at(block * local + i, 256, 256)
            part_out[block, here, :] = jnp.dot(rows_a[there, :], mat_d[...], preferred_element_type=f32).astype(low)

    def weight_grad(into, left, right):
        @pl.loop(0, chips // 2)
        def _(i):
            columns = at(i * 2 * rows, 2 * rows, 128)
            total = inner_rows(left(columns, 0), right(0))
            for block in range(1, 4):
                total = total + inner_rows(left(columns, block), right(block))
            into[pl.ds(2 * i, 2)] = total.reshape(2, rows, total.shape[1]).astype(low)

    def block_rows(block):
        return slice(block * local, (block + 1) * local)

    share = Share(me, run, slab, SHARED)

    def to_slab(start, columns=slice(None)):
        def place(value):
            slab[start : start + value.shape[0], columns] = value.astype(low)

        return place

    base = 2 * rows + few
    kept = rows - few

    def place_q(value):
        slab[base : base + kept, :cols] = value[:kept].astype(low)
        for i in range(3):
            slab[base + i * few : base + (i + 1) * few, cols:] = value[
                kept:, i * heads * size : (i + 1) * heads * size
            ].astype(low)

    def chain(total, place, *then):
        yield from total.steps(place)
        for thread in then:
            yield from thread

    run_down = chain(down, to_slab(0), share.steps((0, rows // 4, rows)))
    run_up = chain(up, to_slab(rows), share.steps((rows, rows + rows // 2, 2 * rows)))

    def pump(thread, times=1):
        for _ in range(times):
            next(thread, None)

    for copy in load_up + load_down:
        copy.wait()
    feed(far)
    sum_h2.start(1 - me.y)
    feed(other)
    sum_h2.start(me.y)
    feed(beside)
    sum_h2.cross()
    feed(quarter)
    weight_grad(grad_d, lambda columns, b: rows_a[block_rows(b), columns], lambda b: rows_c[block_rows(b), :])
    down.send(n_z)
    weight_grad(grad_u, lambda columns, b: rows_h2[block_rows(b), columns], lambda b: rows_du[b])
    up.send(n_z)
    qkv, o = rows_c.at[:, :cols], rows_c.at[:, cols:]
    dqkv, do = rows_h2.at[:, :cols], rows_h2.at[:, cols:]
    h1, part_h1 = rows_a, rows_du
    w_q, w_o = mat_u.at[:, :cols], mat_d.at[: heads * size]
    load_o = [run.local(O, o)]
    load_few += [run.local(QKV, qkv), run.local(WQ, w_q)]
    pump(run_down, 2)
    for copy in load_mid:
        copy.wait()
    sum_h2.landed()

    @pl.loop(0, local, step=64)
    def _(i):
        here = at(i, 64, 64)
        unit, factor = norm_parts(middle[here, :])
        grad, c = sum_h2.rows(here), cot[here, :].astype(f32)
        total = c + norm_back_rows(grad, unit, factor, ffn_gain[...])
        branch[quarter, here, :] = total.astype(low)
        small[2:3] += jnp.sum(grad * unit, axis=0, keepdims=True)
        small[3:4] += jnp.sum(grad, axis=0, keepdims=True)
        small[4:5] += jnp.sum(c, axis=0, keepdims=True)

    load_few.append(run.local(tok_in, cot))
    own = branch.at[quarter]
    over_b = []
    for h in range(2):
        part = branch.at[quarter, h * half : (h + 1) * half]
        over_b.append(run.remote(part, part, me.across_y()))
    core_b = run.remote(own, own, me.across_core())
    pump(run_down)
    feed_out(far)
    sum_out.start(1 - me.y)
    feed_out(other)
    sum_out.start(me.y)
    feed_out(beside)
    feed_out(quarter)
    load_o.append(run.local(WOQ, w_o))
    load_few.append(run.local(H1, h1))

    def project_back(block, start, size_b):
        @pl.loop(0, size_b, step=256)
        def _(i):
            here = at(start + i, 256, 256)
            there = at(block * local + start + i, 256, 256)
            values = branch[block, here, :]
            do[there, :] = times_transposed(values, w_o[...]).astype(low)
            acc_o[...] += inner_rows(o[there, :], values)

    for copy in load_o:
        copy.wait()
    project_back(quarter, 0, local)
    pump(run_down)
    run.arrive(core_b)
    project_back(other, 0, local)
    pump(run_up)
    far_b = []

    def pass_on(h):
        run.arrive(over_b[h])
        part = branch.at[beside, h * half : (h + 1) * half]
        far_b.append(run.remote(part, part, me.across_core()))
        project_back(beside, h * half, half)

    pass_on(0)
    pump(run_down)
    pump(run_up)
    pump(run_down, 2)
    sum_out.cross()
    pass_on(1)
    pump(run_up)
    for h in range(2):
        run.arrive(far_b[h])
        project_back(far, h * half, half)
    grad_o[...] = acc_o[...].reshape(chips, few, width).astype(low)
    total_o = ChipSum(me, run, grad_o, lambda z: grad_o.at[z * 2 + me.x], far_o, over_o)
    total_o.send(n_z)
    run_o = chain(total_o, to_slab(2 * rows), share.flat_steps((2 * rows, base)))
    for copy in load_few:
        copy.wait()
    for g in range(2):
        stops = []
        end = 0
        for item in range(n_items - 1):
            end = end + ends[g, 0, item]
            stops.append(end)
        for head in range(heads):
            slope = jnp.exp2(-(jnp.zeros((1, 1), f32) + (quarter * heads + head + 1)))
            head_back(qkv, o, lse, do, dqkv, sum_k, sum_v, g, head, heads, size, count, stops, slope)
            if 2 * g + head == 1:
                pump(run_down)

    weight_grad(grad_q, lambda columns, b: h1[block_rows(b), columns], lambda b: dqkv[block_rows(b), :])
    total_q = ChipSum(me, run, grad_q, lambda z: grad_q.at[z * 2 + me.x], far_q, over_q)
    total_q.send(n_z)
    summed = []

    def after_q():
        while not summed:
            yield
        yield from share.steps((base + 48, base + 80, 3 * rows))

    def place_and_tell(value):
        place_q(value)
        summed.append(True)

    run_q = chain(total_q, place_and_tell, share.steps((base, base + 16, base + 48)))
    run_r = after_q()
    pump(run_down)

    def project_in(block):
        @pl.loop(0, local, step=256)
        def _(i):
            part_h1[block, at(i, 256, 256), :] = times_transposed(
                dqkv[at(block * local + i, 256, 256), :], w_q[...]
            ).astype(low)

    project_in(far)
    sum_h1 = QuadSum(me, run, part_h1, part_h1.at[group], near_h2, over_h2)
    sum_h1.start(1 - me.y)
    project_in(other)
    sum_h1.start(me.y)
    project_in(beside)
    pump(run_q)
    project_in(quarter)
    pump(run_o)
    pump(run_up)
    sum_h1.cross()
    pump(run_up)
    pump(run_q)
    pump(run_up)
    pump(run_o)
    pump(run_up)
    pump(run_down)
    sum_h1.landed()

    @pl.loop(0, local, step=64)
    def _(i):
        here = at(i, 64, 64)
        unit, factor = norm_parts(cot[here, :].astype(f32))
        grad = sum_h1.rows(here)
        base = branch[quarter, here, :].astype(f32)
        cot[here, :] = (base + norm_back_rows(grad, unit, factor, attn_gain[...])).astype(low)
        small[0:1] += jnp.sum(grad * unit, axis=0, keepdims=True)
        small[1:2] += jnp.sum(grad, axis=0, keepdims=True)

    run.later(cot, GRAD_TOKENS)
    slab[3 * rows :, :] = small[...].astype(low)
    last = share.flat_steps((3 * rows, slab.shape[0]))
    sum_out.landed()

    @pl.loop(0, local, step=64)
    def _(i):
        here = at(i, 64, 64)
        part_out[quarter, here, :] = (middle[here, :] + sum_out.rows(here) + b_down[...]).astype(low)

    run.later(part_out.at[quarter], BLOCK_OUT)
    threads = [last, run_q, run_r, run_up, run_o, run_down]
    for _ in range(16):
        for thread in threads:
            pump(thread)
    run.finish()


def back(n_z, n_items, feed, mid, cot, tok, saved, lq, b_up, attn_gain, ffn_gain, b_down):
    low, f32 = jnp.bfloat16, jnp.float32
    local, width = tok.shape
    chips = 2 * n_z
    heads, size = HEADS // 4, width // HEADS
    rows, few = width // chips, width // 4 // chips
    cols = 3 * heads * size
    shape = jax.ShapeDtypeStruct
    block, four, flat = (local, width), (4, local, width), (4 * local, width)
    deep = 3 * rows + 16
    v = pltpu.VMEM

    def sums(piece):
        return [v((chips,) + piece, low), v((n_z,) + piece, low), v((n_z - 1,) + piece, low)]

    scratch = (
        [v(flat, low)] * 3
        + [v(four, low)]
        + [v((width, width), low)] * 2
        + [v(four, low), v((2,) + block, low), v(block, low)] * 2
        + sums((rows, width)) * 2
        + [v(block, f32), v(block, low), v(saved[3].shape, f32), pltpu.SMEM(lq.shape, lq.dtype)]
        + [v(four, low)]
        + [v((2 * local, size), f32)] * 2
        + [v((heads * size, width), f32)]
        + sums((rows, cols))
        + sums((few, width))
        + [v((16, width), f32), v((deep, width), low)]
    )
    return communicate(
        functools.partial(back_kernel, n_z, n_items),
        [shape(block, low), shape(block, low), shape((4 * chips, deep, width), low)],
        tuple(feed) + (mid, cot, tok) + tuple(saved) + (lq, b_up, attn_gain, ffn_gain, b_down),
        [HBM] * 3,
        [HBM] * (len(feed) + 3 + len(saved) + 1) + [VMEM] * 4,
        (320, 48),
        scratch,
        call_id=2,
        limit=63 << 20,
    )


def unfold_kernel(rows, head_cols, few, shared, down, up, qkv, out, small, bias):
    f32 = jnp.float32
    width = shared.shape[-1]
    chips = up.shape[1] // width * 2
    unit = width // chips
    third = qkv.shape[1] // 3

    @pl.when(pl.program_id(0) == 0)
    def _():
        small[...] = jnp.zeros_like(small)
        bias[...] = jnp.zeros_like(bias)

    for q in range(4):
        down[q * rows : (q + 1) * rows] = shared[q, :rows].astype(f32)
        for s in range(chips):
            start = (s * 4 + q) * unit
            up[:, start : start + unit] = shared[q, rows : 2 * rows, s * unit : (s + 1) * unit].astype(f32)
        base, kept = 2 * rows + few, rows - few
        for i in range(3):
            here = slice(i * third + q * head_cols, i * third + (q + 1) * head_cols)
            qkv[:kept, here] = shared[q, base : base + kept, i * head_cols : (i + 1) * head_cols].astype(f32)
            qkv[kept:, here] = shared[q, base + i * few : base + (i + 1) * few, 3 * head_cols :].astype(f32)
        out[q] = shared[q, 2 * rows : base].astype(f32)
        extra = shared[q, 3 * rows :].astype(f32)
        small[...] += extra
        bias[q : q + 1] += extra[5:6]


def unfold(shared, rows, few, ff):
    devices, deep, width = shared.shape
    chips = devices // 4
    f32 = jnp.float32
    head_cols = width // 4
    return pl.pallas_call(
        functools.partial(unfold_kernel, rows, head_cols, few),
        grid=(chips,),
        in_specs=[pl.BlockSpec((4, deep, width), lambda s: (s, 0, 0))],
        out_specs=[
            pl.BlockSpec((4 * rows, width), lambda s: (s, 0)),
            pl.BlockSpec((rows, ff), lambda s: (s, 0)),
            pl.BlockSpec((rows, 3 * width), lambda s: (s, 0)),
            pl.BlockSpec((4, None, few, width), lambda s: (0, s, 0, 0)),
            pl.BlockSpec((deep - 3 * rows, width), lambda s: (0, 0)),
            pl.BlockSpec((4, width), lambda s: (0, 0)),
        ],
        out_shape=[
            jax.ShapeDtypeStruct((ff, width), f32),
            jax.ShapeDtypeStruct((width, ff), f32),
            jax.ShapeDtypeStruct((width, 3 * width), f32),
            jax.ShapeDtypeStruct((4, chips, few, width), f32),
            jax.ShapeDtypeStruct((deep - 3 * rows, width), f32),
            jax.ShapeDtypeStruct((4, width), f32),
        ],
        compiler_params=pltpu.CompilerParams(vmem_limit_bytes=56 << 20),
    )(shared)


def on_quad(
    tokens,
    lengths,
    attn_gain,
    attn_shift,
    w_qkv,
    w_out,
    ffn_gain,
    ffn_shift,
    w_up,
    b_up,
    w_down,
    b_down,
    cotangent,
):
    low = jnp.bfloat16
    local, width = tokens.shape
    n_dp = lax.axis_size("dp")
    n_z, chips = n_dp // 4, n_dp // 2
    size = width // HEADS
    heads = HEADS // 4
    count = 2 * local
    me = Place(n_z)
    lens = jnp.zeros((8, 128), jnp.int32).at[:1, : lengths.shape[1]].set(lengths)
    gains = [value.reshape(1, width) for value in (attn_gain, attn_shift, ffn_gain, ffn_shift)]
    WQ, WOQ, WU, WD, CQ, h1, qkv, o, lse, h2, middle, LQ = front(
        n_z, lengths.shape[1], w_qkv, w_out, w_up, w_down, tokens, cotangent, lens, gains
    )
    unit = w_up.shape[1] // chips // 4
    bias = lax.dynamic_index_in_dim(b_up.reshape(chips, 4, unit), me.quarter, 1, keepdims=False).reshape(-1)
    block_out, grad_tokens, shared = back(
        n_z,
        lengths.shape[1],
        [h2, CQ.reshape(4 * local, width), WU, WD],
        middle,
        cotangent,
        tokens,
        [h1.reshape(4 * local, width), qkv, o, lse, WQ, WOQ],
        LQ,
        bias.reshape(1, width),
        gains[0],
        gains[2],
        b_down.reshape(1, width),
    )
    rows, few = width // chips, width // 4 // chips
    ff = w_up.shape[1]
    grad_w_down, grad_w_up, grad_w_qkv, grad_w_out, vectors, bias = unfold(shared, rows, few, ff)
    return (
        block_out,
        grad_tokens,
        vectors[0],
        vectors[1],
        grad_w_qkv,
        grad_w_out.reshape(width, width),
        vectors[2],
        vectors[3],
        grad_w_up,
        jnp.transpose(bias.reshape(4, chips, unit), (1, 0, 2)).reshape(ff),
        grad_w_down,
        vectors[4],
    )


def solution(mesh):
    n_dp, n_seq = mesh.shape["dp"], mesh.shape["seq"]
    quad = n_seq == 2 and n_dp % 4 == 0 and n_dp >= 8 and n_dp <= 16
    return jax.shard_map(
        on_quad if quad else on_device,
        mesh=mesh,
        in_specs=(
            P(("dp", "seq"), None),
            P("dp", None),
            P(),
            P(),
            P("dp", None),
            P("dp", None),
            P(),
            P(),
            P("dp", None),
            P(),
            P("dp", None),
            P(),
            P(("dp", "seq"), None),
        ),
        out_specs=(
            P(("dp", "seq"), None),
            P(("dp", "seq"), None),
            P(),
            P(),
            P(),
            P(),
            P(),
            P(),
            P(),
            P(),
            P(),
            P(),
        ),
        check_vma=False,
    )
```

```python
import functools

import jax
import jax.numpy as jnp
from jax import lax
from jax.experimental import pallas as pl
from jax.experimental.pallas import tpu as pltpu
from jax.sharding import PartitionSpec as P

HEADS = 8


EPS = 1e-05
NEVER = -1000000000.0


def inner_rows(left, right):
    return lax.dot_general(
        left, right, (((0,), (0,)), ((), ())), preferred_element_type=jnp.float32
    )


def times_transposed(left, right):
    return lax.dot_general(
        left, right, (((1,), (1,)), ((), ())), preferred_element_type=jnp.float32
    )


def smooth_act(values):
    return jax.nn.gelu(values, approximate=True)


def norm_forward(values, gain, shift):
    mean = jnp.mean(values, axis=-1, keepdims=True)
    centred = values - mean
    variance = jnp.mean(centred * centred, axis=-1, keepdims=True)
    factor = lax.rsqrt(variance + EPS)
    normed = centred * factor
    return (normed * gain + shift, normed, factor)


def norm_backward(grad_out, normed, factor, gain):
    grad_normed = grad_out * gain
    centre_term = jnp.mean(grad_normed, axis=-1, keepdims=True)
    along_term = jnp.mean(grad_normed * normed, axis=-1, keepdims=True)
    grad_in = factor * (grad_normed - centre_term - normed * along_term)
    return (grad_in, jnp.sum(grad_out * normed, axis=0), jnp.sum(grad_out, axis=0))


def item_ids(item_lengths, count):
    item_ends = jnp.cumsum(item_lengths, dtype=jnp.int32)
    places = jnp.arange(count, dtype=jnp.int32)
    hits = (places[:, None] >= item_ends[None, :]).astype(jnp.int32)
    return jnp.sum(hits, axis=1, dtype=jnp.int32)


def block_scores(query_block, keys, start, item_of, slopes):
    rows = query_block.shape[0]
    count = keys.shape[0]
    scale = query_block.shape[-1] ** (-0.5)
    raw = jnp.einsum("qhd,khd->hqk", query_block, keys, preferred_element_type=jnp.float32)
    row_places = start + jnp.arange(rows, dtype=jnp.int32)
    col_places = jnp.arange(count, dtype=jnp.int32)
    distance = (row_places[:, None] - col_places[None, :]).astype(jnp.float32)
    row_items = lax.dynamic_slice_in_dim(item_of, start, rows)
    allowed = (row_items[:, None] == item_of[None, :]) & (
        col_places[None, :] <= row_places[:, None]
    )
    scores = raw * scale - slopes[:, None, None] * distance[None]
    return jnp.where(allowed[None], scores, jnp.float32(-1000000000.0))


def attend(heads_qkv, item_of, slopes):
    count = heads_qkv.shape[0]
    rows = min(512, count)
    queries = heads_qkv[:, 0]
    keys = heads_qkv[:, 1]
    values = heads_qkv[:, 2]

    def one_block(index):
        start = index * rows
        query_block = lax.dynamic_slice_in_dim(queries, start, rows)
        scores = block_scores(query_block, keys, start, item_of, slopes)
        top = jnp.max(scores, axis=-1, keepdims=True)
        weights = jnp.exp(scores - top)
        total = jnp.sum(weights, axis=-1, keepdims=True)
        probs = (weights / total).astype(jnp.bfloat16)
        mixed = jnp.einsum("hqk,khd->qhd", probs, values, preferred_element_type=jnp.float32)
        return (mixed.astype(jnp.bfloat16), (top + jnp.log(total))[..., 0])

    mixed, log_norm = lax.map(one_block, jnp.arange(count // rows, dtype=jnp.int32))
    return (mixed.reshape(count, mixed.shape[2], mixed.shape[3]), log_norm)


def attend_back(heads_qkv, heads_out, grad_heads, log_norm, item_of, slopes):
    count = heads_qkv.shape[0]
    rows = min(512, count)
    queries = heads_qkv[:, 0]
    keys = heads_qkv[:, 1]
    values = heads_qkv[:, 2]
    scale = queries.shape[-1] ** (-0.5)
    row_dots = jnp.sum(grad_heads.astype(jnp.float32) * heads_out.astype(jnp.float32), axis=-1)

    def one_block(carry, index):
        grad_keys, grad_values = carry
        start = index * rows
        query_block = lax.dynamic_slice_in_dim(queries, start, rows)
        grad_block = lax.dynamic_slice_in_dim(grad_heads, start, rows)
        dots = lax.dynamic_slice_in_dim(row_dots, start, rows)
        scores = block_scores(query_block, keys, start, item_of, slopes)
        probs = jnp.exp(scores - log_norm[index][:, :, None])
        probs_low = probs.astype(jnp.bfloat16)
        grad_values = grad_values + jnp.einsum(
            "hqk,qhd->khd", probs_low, grad_block, preferred_element_type=jnp.float32
        )
        grad_probs = jnp.einsum(
            "qhd,khd->hqk", grad_block, values, preferred_element_type=jnp.float32
        )
        grad_scores = (probs * (grad_probs - jnp.transpose(dots)[:, :, None])).astype(jnp.bfloat16)
        grad_query = (
            jnp.einsum("hqk,khd->qhd", grad_scores, keys, preferred_element_type=jnp.float32)
            * scale
        )
        grad_keys = (
            grad_keys
            + jnp.einsum(
                "hqk,qhd->khd", grad_scores, query_block, preferred_element_type=jnp.float32
            )
            * scale
        )
        return ((grad_keys, grad_values), grad_query)

    empty = jnp.zeros(keys.shape, jnp.float32)
    (grad_keys, grad_values), grad_query = lax.scan(
        one_block, (empty, empty), jnp.arange(count // rows, dtype=jnp.int32)
    )
    grad_query = grad_query.reshape(keys.shape)
    return jnp.stack([grad_query, grad_keys, grad_values], axis=1).astype(jnp.bfloat16)


def on_device(
    tokens,
    lengths,
    attn_gain,
    attn_shift,
    w_qkv,
    w_out,
    ffn_gain,
    ffn_shift,
    w_up,
    b_up,
    w_down,
    b_down,
    cotangent,
):
    w_qkv, w_out, w_up, w_down = (
        lax.all_gather(w_qkv, "dp", axis=0, tiled=True),
        lax.all_gather(w_out, "dp", axis=0, tiled=True),
        lax.all_gather(w_up, "dp", axis=0, tiled=True),
        lax.all_gather(w_down, "dp", axis=0, tiled=True),
    )
    local, width = tokens.shape
    groups = lax.axis_size("seq")
    per_head = width // HEADS
    local_heads = HEADS // groups
    count = local * groups
    item_of = item_ids(lengths[0], count)
    first_head = lax.axis_index("seq") * local_heads
    exponents = (first_head + jnp.arange(local_heads, dtype=jnp.int32) + 1).astype(jnp.float32)
    slopes = jnp.exp2(-exponents)
    inputs = tokens.astype(jnp.float32)
    normed_in, unit_in, factor_in = norm_forward(inputs, attn_gain, attn_shift)
    first_in = normed_in.astype(jnp.bfloat16)
    projected = jnp.dot(first_in, w_qkv, preferred_element_type=jnp.float32).astype(jnp.bfloat16)
    projected = projected.reshape(local, 3, HEADS, per_head)
    heads_qkv = lax.all_to_all(projected, "seq", split_axis=2, concat_axis=0, tiled=True)
    heads_out, log_norm = attend(heads_qkv, item_of, slopes)
    joined = lax.all_to_all(heads_out, "seq", split_axis=0, concat_axis=1, tiled=True).reshape(
        local, width
    )
    middle = inputs + jnp.dot(joined, w_out, preferred_element_type=jnp.float32)
    normed_mid, unit_mid, factor_mid = norm_forward(middle, ffn_gain, ffn_shift)
    second_in = normed_mid.astype(jnp.bfloat16)
    pre_act = jnp.dot(second_in, w_up, preferred_element_type=jnp.float32) + b_up
    act_value, act_pull = jax.vjp(smooth_act, pre_act)
    active = act_value.astype(jnp.bfloat16)
    block_out = (
        middle + jnp.dot(active, w_down, preferred_element_type=jnp.float32) + b_down
    ).astype(jnp.bfloat16)
    grad_out = cotangent.astype(jnp.float32)
    grad_b_down = jnp.sum(grad_out, axis=0)
    grad_w_down = inner_rows(active, cotangent)
    grad_active = times_transposed(cotangent, w_down)
    grad_pre = act_pull(grad_active)[0]
    grad_b_up = jnp.sum(grad_pre, axis=0)
    grad_pre_low = grad_pre.astype(jnp.bfloat16)
    grad_w_up = inner_rows(second_in, grad_pre_low)
    grad_second = times_transposed(grad_pre_low, w_up)
    grad_mid_norm, grad_ffn_gain, grad_ffn_shift = norm_backward(
        grad_second, unit_mid, factor_mid, ffn_gain
    )
    grad_middle = grad_out + grad_mid_norm
    grad_branch = grad_middle.astype(jnp.bfloat16)
    grad_w_out = inner_rows(joined, grad_branch)
    grad_joined = (
        times_transposed(grad_branch, w_out).astype(jnp.bfloat16).reshape(local, HEADS, per_head)
    )
    grad_heads = lax.all_to_all(grad_joined, "seq", split_axis=1, concat_axis=0, tiled=True)
    grad_qkv_heads = attend_back(heads_qkv, heads_out, grad_heads, log_norm, item_of, slopes)
    grad_projected = lax.all_to_all(
        grad_qkv_heads, "seq", split_axis=0, concat_axis=2, tiled=True
    ).reshape(local, 3 * width)
    grad_w_qkv = inner_rows(first_in, grad_projected)
    grad_first = times_transposed(grad_projected, w_qkv)
    grad_in_norm, grad_attn_gain, grad_attn_shift = norm_backward(
        grad_first, unit_in, factor_in, attn_gain
    )
    grad_tokens = (grad_middle + grad_in_norm).astype(jnp.bfloat16)
    all_part = (
        lax.psum_scatter(
            grad_attn_gain.astype(jnp.bfloat16), "dp", scatter_dimension=0, tiled=True
        ).astype(jnp.float32),
        lax.psum_scatter(
            grad_attn_shift.astype(jnp.bfloat16), "dp", scatter_dimension=0, tiled=True
        ).astype(jnp.float32),
        lax.psum_scatter(
            grad_w_qkv.astype(jnp.bfloat16), "dp", scatter_dimension=0, tiled=True
        ).astype(jnp.float32),
        lax.psum_scatter(
            grad_w_out.astype(jnp.bfloat16), "dp", scatter_dimension=0, tiled=True
        ).astype(jnp.float32),
        lax.psum_scatter(
            grad_ffn_gain.astype(jnp.bfloat16), "dp", scatter_dimension=0, tiled=True
        ).astype(jnp.float32),
        lax.psum_scatter(
            grad_ffn_shift.astype(jnp.bfloat16), "dp", scatter_dimension=0, tiled=True
        ).astype(jnp.float32),
        lax.psum_scatter(
            grad_w_up.astype(jnp.bfloat16), "dp", scatter_dimension=0, tiled=True
        ).astype(jnp.float32),
        lax.psum_scatter(
            grad_b_up.astype(jnp.bfloat16), "dp", scatter_dimension=0, tiled=True
        ).astype(jnp.float32),
        lax.psum_scatter(
            grad_w_down.astype(jnp.bfloat16), "dp", scatter_dimension=0, tiled=True
        ).astype(jnp.float32),
        lax.psum_scatter(
            grad_b_down.astype(jnp.bfloat16), "dp", scatter_dimension=0, tiled=True
        ).astype(jnp.float32),
    )
    all_part = (
        lax.psum(all_part[0].astype(jnp.bfloat16), "seq").astype(jnp.float32),
        lax.psum(all_part[1].astype(jnp.bfloat16), "seq").astype(jnp.float32),
        lax.psum(all_part[2].astype(jnp.bfloat16), "seq").astype(jnp.float32),
        lax.psum(all_part[3].astype(jnp.bfloat16), "seq").astype(jnp.float32),
        lax.psum(all_part[4].astype(jnp.bfloat16), "seq").astype(jnp.float32),
        lax.psum(all_part[5].astype(jnp.bfloat16), "seq").astype(jnp.float32),
        lax.psum(all_part[6].astype(jnp.bfloat16), "seq").astype(jnp.float32),
        lax.psum(all_part[7].astype(jnp.bfloat16), "seq").astype(jnp.float32),
        lax.psum(all_part[8].astype(jnp.bfloat16), "seq").astype(jnp.float32),
        lax.psum(all_part[9].astype(jnp.bfloat16), "seq").astype(jnp.float32),
    )
    summed = (
        lax.all_gather(all_part[0].astype(jnp.bfloat16), "dp", axis=0, tiled=True).astype(
            jnp.float32
        ),
        lax.all_gather(all_part[1].astype(jnp.bfloat16), "dp", axis=0, tiled=True).astype(
            jnp.float32
        ),
        lax.all_gather(all_part[2].astype(jnp.bfloat16), "dp", axis=0, tiled=True).astype(
            jnp.float32
        ),
        lax.all_gather(all_part[3].astype(jnp.bfloat16), "dp", axis=0, tiled=True).astype(
            jnp.float32
        ),
        lax.all_gather(all_part[4].astype(jnp.bfloat16), "dp", axis=0, tiled=True).astype(
            jnp.float32
        ),
        lax.all_gather(all_part[5].astype(jnp.bfloat16), "dp", axis=0, tiled=True).astype(
            jnp.float32
        ),
        lax.all_gather(all_part[6].astype(jnp.bfloat16), "dp", axis=0, tiled=True).astype(
            jnp.float32
        ),
        lax.all_gather(all_part[7].astype(jnp.bfloat16), "dp", axis=0, tiled=True).astype(
            jnp.float32
        ),
        lax.all_gather(all_part[8].astype(jnp.bfloat16), "dp", axis=0, tiled=True).astype(
            jnp.float32
        ),
        lax.all_gather(all_part[9].astype(jnp.bfloat16), "dp", axis=0, tiled=True).astype(
            jnp.float32
        ),
    )
    return (
        block_out,
        grad_tokens,
        summed[0],
        summed[1],
        summed[2],
        summed[3],
        summed[4],
        summed[5],
        summed[6],
        summed[7],
        summed[8],
        summed[9],
    )


MESH = pl.DeviceIdType.MESH


class Place:
    def __init__(self, n_z):
        dp = lax.axis_index("dp")
        self.n_z = n_z
        self.dp = dp
        self.y = lax.axis_index("seq")
        self.core = dp % 2
        self.chip = dp // 2
        self.x = self.chip % 2
        self.z = self.chip // 2
        self.quarter = 2 * self.core + self.y

    def device(self, z=None, x=None, core=None, y=None):
        z = self.z if z is None else z
        x = self.x if x is None else x
        core = self.core if core is None else core
        y = self.y if y is None else y
        return ((z * 2 + x) * 2 + core, y)

    def across_core(self):
        return self.device(core=1 - self.core)

    def across_x(self):
        return self.device(x=1 - self.x)

    def across_y(self):
        return self.device(y=1 - self.y)

    def z_after(self, k):
        return (self.z + k) % self.n_z

    def z_before(self, k):
        return (self.z + self.n_z - k) % self.n_z

    def along_z(self, k):
        return self.device(z=self.z_after(k))


class Copy:
    def __init__(self, copy, sends, lands):
        self.copy, self.sends, self.lands, self.landed = copy, sends, lands, False

    def guarded(self, condition, action):
        if condition is None:
            action()
        else:
            pl.when(condition)(action)


class Copies:
    def __init__(self, send, recv, near):
        self.send, self.recv, self.near = send, recv, near
        self.all, self.n, self.m, self.local_open = [], 0, 0, []

    def remote(self, src, dst, device, sends=None, lands=None):
        copy = Copy(
            pltpu.make_async_remote_copy(
                src_ref=src,
                dst_ref=dst,
                send_sem=self.send.at[self.n],
                recv_sem=self.recv.at[self.n],
                device_id=device,
                device_id_type=MESH,
            ),
            sends,
            lands,
        )
        self.n += 1
        copy.guarded(sends, copy.copy.start)
        self.all.append(copy)
        return copy

    def local(self, src, dst):
        copy = pltpu.make_async_copy(src, dst, self.near.at[self.m])
        self.m += 1
        copy.start()
        return copy

    def later(self, src, dst):
        self.local_open.append(self.local(src, dst))

    def arrive(self, *copies):
        for copy in copies:
            if not copy.landed:
                copy.guarded(copy.lands, copy.copy.wait_recv)
                copy.landed = True

    def finish(self):
        self.arrive(*self.all)
        for copy in self.all:
            copy.guarded(copy.sends, copy.copy.wait_send)
        for copy in self.local_open:
            copy.wait()


class Line:
    def __init__(self, me, run, own, view):
        self.me, self.run, self.view = me, run, view
        n, z = me.n_z, me.z
        self.up = [run.remote(own, view(z), me.device(z=z + 1), z < n - 1, z > 0)]
        self.down = [run.remote(own, view(z), me.device(z=z - 1), z > 0, z < n - 1)]

    def step(self, t, then):
        me, run, n, z = self.me, self.run, self.me.n_z, self.me.z
        if t >= n:
            return
        run.arrive(self.up[t - 1])
        if t < n - 1:
            part = self.view(z - t)
            self.up.append(run.remote(part, part, me.device(z=z + 1), (z >= t) & (z < n - 1), z > t))
        then(z - t, z >= t)
        run.arrive(self.down[t - 1])
        if t < n - 1:
            part = self.view(z + t)
            self.down.append(
                run.remote(part, part, me.device(z=z - 1), (z < n - t) & (z > 0), z < n - t - 1)
            )
        then(z + t, z < n - t)


def meet(devices):
    barrier = pltpu.get_barrier_semaphore()
    for device in devices:
        pl.semaphore_signal(barrier, inc=1, device_id=device, device_id_type=MESH)
    pl.semaphore_wait(barrier, len(devices))


def at(start, size, unit):
    return pl.ds(pl.multiple_of(start, unit), size)


def communicate(kernel, out_shapes, ins, out_specs, in_specs, counts, scratch=(), call_id=0, limit=None):
    return pl.pallas_call(
        kernel,
        out_shape=out_shapes,
        in_specs=in_specs,
        out_specs=out_specs,
        scratch_shapes=list(scratch)
        + [
            pltpu.SemaphoreType.DMA((counts[0],)),
            pltpu.SemaphoreType.DMA((counts[0],)),
            pltpu.SemaphoreType.DMA((counts[1],)),
        ],
        compiler_params=pltpu.CompilerParams(
            collective_id=call_id, has_side_effects=True, vmem_limit_bytes=limit or (56 << 20)
        ),
    )(*ins)


HBM = pl.BlockSpec(memory_space=pltpu.HBM)
VMEM = pl.BlockSpec(memory_space=pltpu.VMEM)
SMEM = pl.BlockSpec(memory_space=pltpu.SMEM)


def allowed_and_bias(first, rows, count, ends, slope):
    row = first + lax.broadcasted_iota(jnp.int32, (rows, 1), 0)
    col = lax.broadcasted_iota(jnp.int32, (1, count), 1)
    begin = jnp.zeros((rows, 1), jnp.int32)
    for end in ends:
        begin = jnp.where(row >= end, end, begin)
    allowed = (col >= begin) & (col <= row)
    bias = slope * (col - first).astype(jnp.float32)
    return allowed, bias


def norm_rows(values, gain, shift):
    mean = jnp.mean(values, axis=-1, keepdims=True)
    centred = values - mean
    variance = jnp.mean(centred * centred, axis=-1, keepdims=True)
    return centred * lax.rsqrt(variance + EPS) * gain + shift


def norm_block(src, dst, gain, shift, step=64):
    @pl.loop(0, src.shape[0], step=step)
    def _(i):
        rows = at(i, step, step)
        dst[rows, :] = norm_rows(src[rows, :].astype(jnp.float32), gain[...], shift[...]).astype(dst.dtype)


def front_kernel(
    n_z,
    n_items,
    wq,
    wo,
    wu,
    wd,
    tok,
    cot,
    lens,
    attn_gain,
    attn_shift,
    ffn_gain,
    ffn_shift,
    WQ,
    WOQ,
    WU,
    WD,
    CQ,
    H1,
    QKV,
    O,
    LSE,
    H2,
    MID,
    LQ,
    q_all,
    o_all,
    x_all,
    h1,
    qkv,
    mixed,
    lse,
    h2,
    middle,
    ends,
    send,
    recv,
    near,
):
    me = Place(n_z)
    run = Copies(send, recv, near)
    quarter, other = me.quarter, 2 * (1 - me.core) + me.y
    rows = wq.shape[0]
    third = wq.shape[1] // 3
    cut = third // 4
    chips = 2 * n_z
    span = wu.shape[1] // chips
    unit = span // 4
    local = tok.shape[0]
    count = 2 * local
    half = local // 2
    size = third // HEADS
    heads = HEADS // 4
    meet(
        [me.across_core(), me.across_x(), me.across_y()] + [me.along_z(k) for k in range(1, n_z)]
    )
    mine = at(me.dp * rows, rows, 16)

    into = [q_all.at[mine, p * cut : (p + 1) * cut] for p in range(3)]
    near_q = [run.local(wq.at[:, at(p * third + quarter * cut, cut, 128)], into[p]) for p in range(3)]
    core_q = [
        run.remote(wq.at[:, at(p * third + other * cut, cut, 128)], into[p], me.across_core())
        for p in range(3)
    ]
    keep_x = run.local(tok, x_all.at[quarter])
    keep_lens = run.local(lens, LQ.at[me.core])
    core_lens = run.remote(lens, LQ.at[me.core], me.across_core())

    def halves(h):
        return slice(h * half, (h + 1) * half)

    over_x = [
        run.remote(tok.at[halves(h)], x_all.at[quarter, halves(h)], me.across_y()) for h in range(2)
    ]
    core_x = run.remote(tok, x_all.at[quarter], me.across_core())
    into = [WU.at[mine, s * unit : (s + 1) * unit] for s in range(chips)]
    near_u = [run.local(wu.at[:, at(s * span + quarter * unit, unit, 128)], into[s]) for s in range(chips)]
    core_u = [
        run.remote(wu.at[:, at(s * span + other * unit, unit, 128)], into[s], me.across_core())
        for s in range(chips)
    ]

    def pairs_of(array):
        return lambda z, x=me.x: array.at[at((z * 2 + x) * 2 * rows, 2 * rows, 16)]

    def shard_of(z, x=me.x):
        return o_all.at[at(((z * 2 + x) * 2 + me.core) * rows, rows, 16)]

    def units_of(z, x=me.x):
        return WD.at[at((z * 2 + x) * unit, unit // 2, 16)]

    def late_units_of(z, x=me.x):
        return WD.at[at((z * 2 + x) * unit + unit // 2, unit // 2, 16)]

    from_x = {"q": [], "o": [], "u": [], "d": []}
    share_o = []

    def across(name, view):
        def then(z, came):
            part = view(z)
            from_x[name].append((run.remote(part, part, me.across_x(), came, came), z, came))
            if name == "o":
                share_o.append(run.remote(part, part, me.across_core(), came, came))

        return then

    for copy in near_q:
        copy.wait()
    run.arrive(*core_q)
    view_q, view_u = pairs_of(q_all), pairs_of(WU)
    line_q = Line(me, run, view_q(me.z), view_q)
    across("q", view_q)(me.z, None)
    keep_o = run.local(wo, shard_of(me.z))
    keep_x.wait()
    norm_block(x_all.at[quarter], h1.at[quarter], attn_gain, attn_shift)
    run.arrive(core_x)
    line_q.step(1, across("q", view_q))
    line_o = Line(me, run, wo, shard_of)
    share_o.append(run.remote(wo, shard_of(me.z), me.across_core()))
    norm_block(x_all.at[other], h1.at[other], attn_gain, attn_shift)
    line_q.step(2, across("q", view_q))
    beside = 2 * me.core + 1 - me.y
    far = 2 * (1 - me.core) + 1 - me.y
    far_x = []
    for h in range(2):
        run.arrive(over_x[h])
        part = x_all.at[beside, halves(h)]
        far_x.append(run.remote(part, part, me.across_core()))
        if h == 0:
            line_q.step(3, across("q", view_q))
            from_x["o"].append((run.remote(wo, shard_of(me.z), me.across_x()), me.z, None))
            line_o.step(1, across("o", shard_of))
            for copy in near_u:
                copy.wait()
            run.arrive(*core_u)
            line_u = Line(me, run, view_u(me.z), view_u)
        norm_block(x_all.at[beside, halves(h)], h1.at[beside, halves(h)], attn_gain, attn_shift)
    over_c = [run.remote(cot.at[halves(0)], CQ.at[quarter, halves(0)], me.across_y())]
    run.remote(cot, CQ.at[quarter], me.across_core())
    for h in range(2):
        run.arrive(far_x[h])
        norm_block(x_all.at[far, halves(h)], h1.at[far, halves(h)], attn_gain, attn_shift)
    line_o.step(2, across("o", shard_of))
    part_d = unit // 2
    own = wd.at[at(me.y * unit, part_d, 16)]
    own_late = wd.at[at(me.y * unit + part_d, part_d, 16)]
    across("u", view_u)(me.z, None)
    run.later(h1, H1)
    for copy, _, _ in from_x["q"]:
        run.arrive(copy)
    run.later(q_all, WQ)

    @pl.loop(0, 4 * local, step=256)
    def _(i):
        block = at(i, 256, 256)
        qkv[block, :] = jnp.dot(
            h1[i // local, at(i % local, 256, 256), :], q_all[...], preferred_element_type=jnp.float32
        ).astype(jnp.bfloat16)

    run.later(qkv, QKV)
    keep_lens.wait()
    run.arrive(core_lens)
    fetch = run.local(LQ, ends)
    fetch.wait()

    def heads_at(owner, head):
        return at(owner * heads * size + head * size, size, 128)

    over_o, near_o = [], []
    line_o.step(3, across("o", shard_of))
    line_d = Line(me, run, own, units_of)
    from_x["d"].append((run.remote(own, units_of(me.z), me.across_x()), me.z, None))
    run.later(own, units_of(me.z))
    swap_d = run.remote(own_late, late_units_of(me.z), me.across_x())
    line_e = Line(me, run, own_late, late_units_of)
    run.later(own_late, late_units_of(me.z))
    pumps = [
        lambda: line_u.step(1, across("u", view_u)),
        lambda: line_u.step(2, across("u", view_u)),
        lambda: line_u.step(3, across("u", view_u)),
        lambda: line_d.step(1, across("d", units_of)),
    ]
    for g in range(2):
        stops = []
        total = 0
        for item in range(n_items - 1):
            total = total + ends[g, 0, item]
            stops.append(total)
        for head in range(heads):
            slope = jnp.exp2(-(jnp.zeros((1, 1), jnp.float32) + (quarter * heads + head + 1)))
            column = heads_at(quarter, head)
            for first in range(0, count, 256):
                start, seen = g * count, first + 256
                here = slice(start + first, start + seen)
                allowed, bias = allowed_and_bias(first, 256, seen, stops, slope)
                keys = qkv[start : start + seen, (heads + head) * size : (heads + head + 1) * size]
                s = times_transposed(qkv[here, head * size : (head + 1) * size], keys) * size**-0.5 + bias
                s = jnp.where(allowed, s, NEVER)
                top = jnp.max(s, axis=-1, keepdims=True)
                w = jnp.exp(s - top)
                sum_w = jnp.sum(w, axis=-1, keepdims=True)
                p = (w * (1.0 / sum_w)).astype(jnp.bfloat16)
                values = qkv[start : start + seen, (2 * heads + head) * size : (2 * heads + head + 1) * size]
                mixed[here, column] = jnp.dot(p, values, preferred_element_type=jnp.float32).astype(
                    jnp.bfloat16
                )
                lse[g, head, first:seen] = top + jnp.log(sum_w)
            part = mixed.at[g * count : (g + 1) * count, column]
            over_o.append(run.remote(part, part, me.across_y()))
            near_o.append(run.remote(part, part, me.across_core()))
            pumps[g * heads + head]()
    run.later(mixed.at[:, at(quarter * heads * size, heads * size, 128)], O)
    run.later(lse, LSE)
    over_c.append(run.remote(cot.at[halves(1)], CQ.at[quarter, halves(1)], me.across_y()))
    run.arrive(over_c[0])
    part = CQ.at[beside, halves(0)]
    run.remote(part, part, me.across_core())
    far_o = []
    for copy, z, came in from_x["o"]:
        run.arrive(copy)
        part = shard_of(z, 1 - me.x)
        far_o.append(run.remote(part, part, me.across_core(), came, came))
    line_e.step(1, lambda z, came: None)
    run.arrive(swap_d)
    beyond = late_units_of(me.z, 1 - me.x)
    line_f = Line(me, run, beyond, lambda z: late_units_of(z, 1 - me.x))
    passed = []
    for g in range(2):
        for head in range(heads):
            run.arrive(over_o[g * heads + head])
            part = mixed.at[g * count : (g + 1) * count, heads_at(beside, head)]
            passed.append(run.remote(part, part, me.across_core()))
    line_d.step(2, across("d", units_of))
    keep_o.wait()
    run.arrive(*share_o, *far_o)
    run.later(o_all.at[at(quarter * heads * size, heads * size, 16)], WOQ)
    for g in range(2):
        run.arrive(*near_o[g * heads : (g + 1) * heads], *passed[g * heads : (g + 1) * heads])

        @pl.loop(0, count, step=256)
        def _(i):
            block = at(g * count + i, 256, 256)
            owner, inner = 2 * g + i // local, at(i % local, 256, 256)
            x1 = x_all[owner, inner, :].astype(jnp.float32) + jnp.dot(
                mixed[block, :], o_all[...], preferred_element_type=jnp.float32
            )
            h2[block, :] = norm_rows(x1, ffn_gain[...], ffn_shift[...]).astype(jnp.bfloat16)

            @pl.when(owner == quarter)
            def _():
                middle[inner, :] = x1

        line_d.step(3 + g, across("d", units_of))
        line_e.step(2 + g, lambda z, came: None)
        line_f.step(1 + g, lambda z, came: None)
    run.later(h2, H2)
    run.later(middle, MID)
    line_f.step(3, lambda z, came: None)
    run.arrive(over_c[1])
    part = CQ.at[beside, halves(1)]
    run.remote(part, part, me.across_core())
    run.finish()


def front(n_z, n_items, wq, wo, wu, wd, tok, cot, lens, gains):
    width, low, f32 = wq.shape[0] * 4 * n_z, jnp.bfloat16, jnp.float32
    quarter_ff = wu.shape[1] // 4
    local = tok.shape[0]
    heads, size = HEADS // 4, width // HEADS
    shape = jax.ShapeDtypeStruct
    shapes = [
        shape((width, wq.shape[1] // 4), low),
        shape((width // 4, width), low),
        shape((width, quarter_ff), low),
        shape((quarter_ff, width), low),
        shape((4, local, width), low),
        shape((4, local, width), low),
        shape((4 * local, 3 * width // 4), low),
        shape((4 * local, width // 4), low),
        shape((2, heads, 2 * local, 1), f32),
        shape((4 * local, width), low),
        shape((local, width), f32),
        shape((2,) + lens.shape, lens.dtype),
    ]
    scratch = [
        pltpu.VMEM((width, wq.shape[1] // 4), low),
        pltpu.VMEM((width, width), low),
        pltpu.VMEM((4, local, width), low),
        pltpu.VMEM((4, local, width), low),
        pltpu.VMEM((4 * local, 3 * width // 4), low),
        pltpu.VMEM((4 * local, width), low),
        pltpu.VMEM((2, heads, 2 * local, 1), f32),
        pltpu.VMEM((4 * local, width), low),
        pltpu.VMEM((local, width), f32),
        pltpu.SMEM((2,) + lens.shape, lens.dtype),
    ]
    return communicate(
        functools.partial(front_kernel, n_z, n_items),
        shapes,
        (wq, wo, wu, wd, tok, cot, lens) + tuple(gains),
        [HBM] * 12,
        [HBM] * 7 + [VMEM] * 4,
        (144, 34),
        scratch,
        call_id=1,
    )


def add(*values):
    total = values[0].astype(jnp.float32)
    for value in values[1:]:
        total = total + value.astype(jnp.float32)
    return total


class Share:
    def __init__(self, me, run, src, dst):
        self.me, self.run, self.src, self.dst = me, run, src, dst

    def slot(self, z, x, y):
        return ((z * 2 + x) * 2 + self.me.core) * 2 + y

    def steps(self, cut):
        me, run, src, dst, slot = self.me, self.run, self.src, self.dst, self.slot
        low, middle, high = cut
        first, second, whole = slice(low, middle), slice(middle, high), slice(low, high)
        own = dst.at[slot(me.z, me.x, me.y)]
        run.later(src.at[whole], own.at[whole])
        from_z = [run.remote(src.at[whole], own.at[whole], me.along_z(k)) for k in range(1, me.n_z)]
        xa, xb, ya, yb, late_a, late_b = [], [], [], [], [], []
        yield

        def fan(k):
            here = dst.at[slot(me.z_before(k), me.x, me.y)]
            if k:
                run.arrive(from_z[k - 1])
            there = here if k else src
            xa.append(run.remote(there.at[first], here.at[first], me.across_x()))
            yb.append(run.remote(there.at[second], here.at[second], me.across_y()))
            ya.append(run.remote(there.at[first], here.at[first], me.across_y()))
            xb.append(run.remote(there.at[second], here.at[second], me.across_x()))
            run.remote(there.at[whole], here.at[whole], me.across_core())

        def relay(k):
            z = me.z_before(k)
            run.arrive(xa[k])
            part = dst.at[slot(z, 1 - me.x, me.y), first]
            late_a.append(run.remote(part, part, me.across_y()))
            run.arrive(yb[k])
            part = dst.at[slot(z, me.x, 1 - me.y), second]
            late_b.append(run.remote(part, part, me.across_x()))

        def hand_over(k):
            z = me.z_before(k)
            run.arrive(xb[k])
            part = dst.at[slot(z, 1 - me.x, me.y), whole]
            run.remote(part, part, me.across_core())
            run.arrive(ya[k])
            part = dst.at[slot(z, me.x, 1 - me.y), whole]
            run.remote(part, part, me.across_core())

        def hand_last(k):
            run.arrive(late_a[k], late_b[k])
            part = dst.at[slot(me.z_before(k), 1 - me.x, 1 - me.y), whole]
            run.remote(part, part, me.across_core())

        for i in range(me.n_z + 3):
            for lag, action in enumerate((fan, relay, hand_over, hand_last)):
                if 0 <= i - lag < me.n_z:
                    action(i - lag)
            yield


    def flat_steps(self, cut):
        me, run, src, dst = self.me, self.run, self.src, self.dst
        whole = slice(*cut)
        own = dst.at[self.slot(me.z, me.x, me.y), whole]
        keep = run.local(src.at[whole], own)
        from_y = run.remote(src.at[whole], own, me.across_y())
        run.remote(src.at[whole], own, me.across_core())
        from_z = []

        def pair(z, x):
            return dst.at[pl.ds(self.slot(z, x, 0), 2), whole]

        def along(part):
            from_z.append([run.remote(part, part, me.along_z(k)) for k in range(1, me.n_z)])

        yield
        keep.wait()
        run.arrive(from_y)
        part = pair(me.z, me.x)
        from_x = run.remote(part, part, me.across_x())
        along(part)
        part = dst.at[self.slot(me.z, me.x, 1 - me.y), whole]
        run.remote(part, part, me.across_core())
        yield
        run.arrive(from_x)
        part = pair(me.z, 1 - me.x)
        along(part)
        run.remote(part, part, me.across_core())
        yield
        for k in range(1, me.n_z):
            for i, x in enumerate((me.x, 1 - me.x)):
                run.arrive(from_z[i][k - 1])
                part = pair(me.z_before(k), x)
                run.remote(part, part, me.across_core())
            yield


class ChipSum:
    def __init__(self, me, run, src, own, far, over):
        self.me, self.run, self.src, self.own, self.far, self.over = me, run, src, own, far, over
        self.sent = []

    def send(self, times=1):
        for _ in range(times):
            z = self.me.z_after(len(self.sent) + 1)
            piece = self.src.at[z * 2 + 1 - self.me.x]
            self.sent.append(self.run.remote(piece, self.far.at[z], self.me.across_x()))

    def steps(self, place, then=None):
        me, run = self.me, self.run
        along = []
        for k in range(1, me.n_z + 1):
            z = me.z_after(k)
            run.arrive(self.sent[k - 1])
            if then is not None:
                then()
            part = self.own(z)
            part[...] = add(part[...], self.far[z]).astype(jnp.bfloat16)
            if k < me.n_z:
                along.append(run.remote(part, self.over.at[k - 1], me.along_z(k)))
            yield
        run.arrive(*along)
        place(add(self.own(me.z)[...], *[self.over[k] for k in range(me.n_z - 1)]))
        yield


class QuadSum:
    def __init__(self, me, run, src, own, near, over):
        self.me, self.run, self.own, self.near, self.over = me, run, own, near, over
        self.src, self.given = src, []

    def start(self, y):
        me = self.me
        self.given.append(self.run.remote(self.src.at[2 * (1 - me.core) + y], self.near.at[y], me.across_core()))

    def cross(self, step=128):
        me, own, near = self.me, self.own, self.near
        self.run.arrive(self.given[0])

        @pl.loop(0, self.over.shape[0], step=step)
        def _(i):
            rows = at(i, step, step)
            own[1 - me.y, rows, :] = add(own[1 - me.y, rows, :], near[1 - me.y, rows, :]).astype(jnp.bfloat16)

        self.over_y = self.run.remote(own.at[1 - me.y], self.over, me.across_y())

    def landed(self):
        self.run.arrive(self.given[1], self.over_y)

    def rows(self, rows):
        y = self.me.y
        return add(self.own[y, rows, :], self.near[y, rows, :], self.over[rows, :])


def head_back(qkv, o, lse, do, dqkv, sum_k, sum_v, g, head, heads, size, count, stops, slope):
    scale = size**-0.5
    start = g * count
    sum_k[...] = jnp.zeros_like(sum_k)
    sum_v[...] = jnp.zeros_like(sum_v)

    def columns(part):
        return slice((part * heads + head) * size, (part * heads + head + 1) * size)

    mine = columns(0)
    for first in range(0, count, 256):
        seen = first + 256
        here, past = slice(start + first, start + seen), slice(start, start + seen)
        allowed, bias = allowed_and_bias(first, 256, seen, stops, slope)
        query, keys = qkv[here, mine], qkv[past, columns(1)]
        s = times_transposed(query, keys) * scale + bias
        p = jnp.exp(jnp.where(allowed, s, NEVER) - lse[g, head, first:seen])
        grad = do[here, mine]
        dots = jnp.sum(grad.astype(jnp.float32) * o[here, mine].astype(jnp.float32), axis=-1, keepdims=True)
        sum_v[:seen] += inner_rows(p.astype(jnp.bfloat16), grad)
        ds = (p * (times_transposed(grad, qkv[past, columns(2)]) - dots)).astype(jnp.bfloat16)
        dqkv[here, mine] = (jnp.dot(ds, keys, preferred_element_type=jnp.float32) * scale).astype(jnp.bfloat16)
        sum_k[:seen] += inner_rows(ds, query)
    dqkv[start : start + count, columns(1)] = (sum_k[...] * scale).astype(jnp.bfloat16)
    dqkv[start : start + count, columns(2)] = sum_v[...].astype(jnp.bfloat16)


def norm_parts(values):
    mean = jnp.mean(values, axis=-1, keepdims=True)
    centred = values - mean
    variance = jnp.mean(centred * centred, axis=-1, keepdims=True)
    factor = lax.rsqrt(variance + EPS)
    return centred * factor, factor


def norm_back_rows(grad, unit, factor, gain):
    scaled = grad * gain
    centre = jnp.mean(scaled, axis=-1, keepdims=True)
    along = jnp.mean(scaled * unit, axis=-1, keepdims=True)
    return factor * (scaled - centre - unit * along)


def gelu_and_slope(u):
    root, cube = 0.7978845608028654, 0.044715
    square = u * u
    t = jnp.tanh(root * u * (1.0 + cube * square))
    half = 0.5 * (1.0 + t)
    return u * half, half + 0.5 * u * (1.0 - t * t) * (root * (1.0 + 3.0 * cube * square))


def back_kernel(
    n_z,
    n_items,
    H2,
    C,
    WU,
    WD,
    MID,
    cot_in,
    tok_in,
    H1,
    QKV,
    O,
    LSE,
    WQ,
    WOQ,
    LQ,
    b_up,
    attn_gain,
    ffn_gain,
    b_down,
    BLOCK_OUT,
    GRAD_TOKENS,
    SHARED,
    rows_c,
    rows_h2,
    rows_a,
    rows_du,
    mat_u,
    mat_d,
    part_h2,
    near_h2,
    over_h2,
    part_out,
    near_out,
    over_out,
    grad_d,
    far_d,
    over_d,
    grad_u,
    far_u,
    over_u,
    middle,
    cot,
    lse,
    ends,
    branch,
    sum_k,
    sum_v,
    acc_o,
    grad_q,
    far_q,
    over_q,
    grad_o,
    far_o,
    over_o,
    small,
    slab,
    send,
    recv,
    near,
):
    me = Place(n_z)
    run = Copies(send, recv, near)
    quarter = me.quarter
    other, beside, far = 2 * (1 - me.core) + me.y, 2 * me.core + 1 - me.y, 2 * (1 - me.core) + 1 - me.y
    low, f32 = jnp.bfloat16, jnp.float32
    chips = 2 * n_z
    local, width = tok_in.shape
    count, half = 2 * local, local // 2
    size = width // HEADS
    heads = HEADS // 4
    rows = grad_d.shape[1]
    few = grad_o.shape[1]
    cols = 3 * heads * size
    meet(
        [me.across_core(), me.across_x(), me.across_y()] + [me.along_z(k) for k in range(1, n_z)]
    )

    def fetch(block, grads=None):
        here = at(block * local, local, 256)
        return [
            run.local(H2.at[here], rows_h2.at[here]),
            run.local(C.at[here] if grads is None else grads, rows_c.at[here]),
        ]

    load_first = [run.local(WU, mat_u)] + fetch(far) + [run.local(WD, mat_d)]
    load_next = [fetch(other), fetch(beside), fetch(quarter, cot_in)]
    load_mid = [run.local(MID, middle), run.local(cot_in, cot)]
    load_few = [run.local(a, b) for a, b in ((LSE, lse), (LQ, ends))]
    small[...] = jnp.zeros_like(small)
    acc_o[...] = jnp.zeros_like(acc_o)
    group = pl.ds(2 * me.core, 2)
    sum_h2 = QuadSum(me, run, part_h2, part_h2.at[group], near_h2, over_h2)
    sum_out = QuadSum(me, run, part_out, part_out.at[group], near_out, over_out)
    down = ChipSum(me, run, grad_d, lambda z: grad_d.at[z * 2 + me.x], far_d, over_d)
    up = ChipSum(me, run, grad_u, lambda z: grad_u.at[z * 2 + me.x], far_u, over_u)

    def feed(block):
        @pl.loop(0, local, step=256)
        def _(i):
            here, there = at(i, 256, 256), at(block * local + i, 256, 256)
            values, grads = rows_h2[there, :], rows_c[there, :]
            for j in range(0, width, 256):
                part = slice(j, j + 256)
                u = jnp.dot(values, mat_u[:, part], preferred_element_type=f32) + b_up[:, part]
                bent, slope = gelu_and_slope(u)
                rows_a[there, part] = bent.astype(low)
                du = times_transposed(grads, mat_d[part, :]) * slope
                rows_du[block, here, part] = du.astype(low)
                small[5:6, part] += jnp.sum(du, axis=0, keepdims=True)
            part_h2[block, here, :] = times_transposed(rows_du[block, here, :], mat_u[...]).astype(low)

    def feed_out(block):
        @pl.loop(0, local, step=256)
        def _(i):
            here, there = at(i, 256, 256), at(block * local + i, 256, 256)
            part_out[block, here, :] = jnp.dot(rows_a[there, :], mat_d[...], preferred_element_type=f32).astype(low)

    def weight_grad(into, left, right):
        @pl.loop(0, chips // 2)
        def _(i):
            columns = at(i * 2 * rows, 2 * rows, 128)
            total = inner_rows(left(columns, 0), right(0))
            for block in range(1, 4):
                total = total + inner_rows(left(columns, block), right(block))
            into[pl.ds(2 * i, 2)] = total.reshape(2, rows, total.shape[1]).astype(low)

    def block_rows(block):
        return slice(block * local, (block + 1) * local)

    share = Share(me, run, slab, SHARED)

    def to_slab(start, columns=slice(None)):
        def place(value):
            slab[start : start + value.shape[0], columns] = value.astype(low)

        return place

    base = 2 * rows + few
    kept = rows - few

    def place_q(value):
        slab[base : base + kept, :cols] = value[:kept].astype(low)
        for i in range(3):
            slab[base + i * few : base + (i + 1) * few, cols:] = value[
                kept:, i * heads * size : (i + 1) * heads * size
            ].astype(low)

    def chain(total, place, *then):
        yield from total.steps(place)
        for thread in then:
            yield from thread

    run_down = chain(down, to_slab(0), share.steps((0, rows // 4, rows)))
    run_up = chain(up, to_slab(rows), share.steps((rows, rows + rows // 2, 2 * rows)))

    def pump(thread, times=1):
        for _ in range(times):
            next(thread, None)


    def await_all(copies):
        for copy in copies:
            copy.wait()

    await_all(load_first)
    feed(far)
    sum_h2.start(1 - me.y)
    await_all(load_next[0])
    feed(other)
    sum_h2.start(me.y)
    await_all(load_next[1])
    feed(beside)
    sum_h2.cross()
    await_all(load_next[2])
    feed(quarter)
    weight_grad(grad_d, lambda columns, b: rows_a[block_rows(b), columns], lambda b: rows_c[block_rows(b), :])
    down.send(n_z)
    weight_grad(grad_u, lambda columns, b: rows_h2[block_rows(b), columns], lambda b: rows_du[b])
    up.send(n_z)
    qkv, o = rows_c.at[:, :cols], rows_c.at[:, cols:]
    dqkv, do = rows_h2.at[:, :cols], rows_h2.at[:, cols:]
    h1, part_h1 = rows_a, rows_du
    w_q, w_o = mat_u.at[:, :cols], mat_d.at[: heads * size]
    load_o = [run.local(O, o)]
    load_few += [run.local(QKV, qkv), run.local(WQ, w_q)]
    pump(run_down, 2)
    for copy in load_mid:
        copy.wait()
    sum_h2.landed()

    @pl.loop(0, local, step=64)
    def _(i):
        here = at(i, 64, 64)
        unit, factor = norm_parts(middle[here, :])
        grad, c = sum_h2.rows(here), cot[here, :].astype(f32)
        total = c + norm_back_rows(grad, unit, factor, ffn_gain[...])
        branch[quarter, here, :] = total.astype(low)
        small[2:3] += jnp.sum(grad * unit, axis=0, keepdims=True)
        small[3:4] += jnp.sum(grad, axis=0, keepdims=True)
        small[4:5] += jnp.sum(c, axis=0, keepdims=True)

    load_few.append(run.local(tok_in, cot))
    own = branch.at[quarter]
    over_b = []
    for h in range(2):
        part = branch.at[quarter, h * half : (h + 1) * half]
        over_b.append(run.remote(part, part, me.across_y()))
    core_b = run.remote(own, own, me.across_core())
    pump(run_down)
    feed_out(far)
    sum_out.start(1 - me.y)
    feed_out(other)
    sum_out.start(me.y)
    feed_out(beside)
    feed_out(quarter)
    load_o.append(run.local(WOQ, w_o))
    load_few.append(run.local(H1, h1))

    def project_back(block, start, size_b):
        @pl.loop(0, size_b, step=256)
        def _(i):
            here = at(start + i, 256, 256)
            there = at(block * local + start + i, 256, 256)
            values = branch[block, here, :]
            do[there, :] = times_transposed(values, w_o[...]).astype(low)
            acc_o[...] += inner_rows(o[there, :], values)

    for copy in load_o:
        copy.wait()
    project_back(quarter, 0, local)
    pump(run_down)
    run.arrive(core_b)
    project_back(other, 0, local)
    pump(run_up)
    far_b = []

    def pass_on(h):
        run.arrive(over_b[h])
        part = branch.at[beside, h * half : (h + 1) * half]
        far_b.append(run.remote(part, part, me.across_core()))
        project_back(beside, h * half, half)

    pass_on(0)
    pump(run_down)
    pump(run_up)
    pump(run_down, 2)
    sum_out.cross()
    pass_on(1)
    pump(run_up)
    for h in range(2):
        run.arrive(far_b[h])
        project_back(far, h * half, half)
    grad_o[...] = acc_o[...].reshape(chips, few, width).astype(low)
    total_o = ChipSum(me, run, grad_o, lambda z: grad_o.at[z * 2 + me.x], far_o, over_o)
    total_o.send(n_z)
    run_o = chain(total_o, to_slab(2 * rows), share.flat_steps((2 * rows, base)))
    for copy in load_few:
        copy.wait()
    for g in range(2):
        stops = []
        end = 0
        for item in range(n_items - 1):
            end = end + ends[g, 0, item]
            stops.append(end)
        for head in range(heads):
            slope = jnp.exp2(-(jnp.zeros((1, 1), f32) + (quarter * heads + head + 1)))
            head_back(qkv, o, lse, do, dqkv, sum_k, sum_v, g, head, heads, size, count, stops, slope)
            if 2 * g + head == 1:
                pump(run_down)

    weight_grad(grad_q, lambda columns, b: h1[block_rows(b), columns], lambda b: dqkv[block_rows(b), :])
    total_q = ChipSum(me, run, grad_q, lambda z: grad_q.at[z * 2 + me.x], far_q, over_q)
    total_q.send(n_z)
    summed = []

    def after_q():
        while not summed:
            yield
        yield from share.steps((base + 48, base + 80, 3 * rows))

    def place_and_tell(value):
        place_q(value)
        summed.append(True)

    run_q = chain(total_q, place_and_tell, share.steps((base, base + 16, base + 48)))
    run_r = after_q()
    pump(run_down)

    def project_in(block):
        @pl.loop(0, local, step=256)
        def _(i):
            part_h1[block, at(i, 256, 256), :] = times_transposed(
                dqkv[at(block * local + i, 256, 256), :], w_q[...]
            ).astype(low)

    project_in(far)
    sum_h1 = QuadSum(me, run, part_h1, part_h1.at[group], near_h2, over_h2)
    sum_h1.start(1 - me.y)
    project_in(other)
    sum_h1.start(me.y)
    project_in(beside)
    pump(run_q)
    project_in(quarter)
    pump(run_o)
    pump(run_up)
    sum_h1.cross()
    pump(run_up)
    pump(run_q)
    pump(run_up)
    pump(run_o)
    pump(run_up)
    pump(run_down)
    sum_h1.landed()

    @pl.loop(0, local, step=64)
    def _(i):
        here = at(i, 64, 64)
        unit, factor = norm_parts(cot[here, :].astype(f32))
        grad = sum_h1.rows(here)
        base = branch[quarter, here, :].astype(f32)
        cot[here, :] = (base + norm_back_rows(grad, unit, factor, attn_gain[...])).astype(low)
        small[0:1] += jnp.sum(grad * unit, axis=0, keepdims=True)
        small[1:2] += jnp.sum(grad, axis=0, keepdims=True)

    run.later(cot, GRAD_TOKENS)
    slab[3 * rows :, :] = small[...].astype(low)
    last = share.flat_steps((3 * rows, slab.shape[0]))
    sum_out.landed()

    @pl.loop(0, local, step=64)
    def _(i):
        here = at(i, 64, 64)
        part_out[quarter, here, :] = (middle[here, :] + sum_out.rows(here) + b_down[...]).astype(low)

    run.later(part_out.at[quarter], BLOCK_OUT)
    threads = [last, run_q, run_r, run_up, run_o, run_down]
    for _ in range(16):
        for thread in threads:
            pump(thread)
    run.finish()


def back(n_z, n_items, feed, mid, cot, tok, saved, lq, b_up, attn_gain, ffn_gain, b_down):
    low, f32 = jnp.bfloat16, jnp.float32
    local, width = tok.shape
    chips = 2 * n_z
    heads, size = HEADS // 4, width // HEADS
    rows, few = width // chips, width // 4 // chips
    cols = 3 * heads * size
    shape = jax.ShapeDtypeStruct
    block, four, flat = (local, width), (4, local, width), (4 * local, width)
    deep = 3 * rows + 16
    v = pltpu.VMEM

    def sums(piece):
        return [v((chips,) + piece, low), v((n_z,) + piece, low), v((n_z - 1,) + piece, low)]

    scratch = (
        [v(flat, low)] * 3
        + [v(four, low)]
        + [v((width, width), low)] * 2
        + [v(four, low), v((2,) + block, low), v(block, low)] * 2
        + sums((rows, width)) * 2
        + [v(block, f32), v(block, low), v(saved[3].shape, f32), pltpu.SMEM(lq.shape, lq.dtype)]
        + [v(four, low)]
        + [v((2 * local, size), f32)] * 2
        + [v((heads * size, width), f32)]
        + sums((rows, cols))
        + sums((few, width))
        + [v((16, width), f32), v((deep, width), low)]
    )
    return communicate(
        functools.partial(back_kernel, n_z, n_items),
        [shape(block, low), shape(block, low), shape((4 * chips, deep, width), low)],
        tuple(feed) + (mid, cot, tok) + tuple(saved) + (lq, b_up, attn_gain, ffn_gain, b_down),
        [HBM] * 3,
        [HBM] * (len(feed) + 3 + len(saved) + 1) + [VMEM] * 4,
        (320, 48),
        scratch,
        call_id=2,
        limit=63 << 20,
    )


def unfold_kernel(rows, head_cols, few, shared, down, up, qkv, out, small, bias):
    f32 = jnp.float32
    width = shared.shape[-1]
    chips = up.shape[1] // width * 2
    unit = width // chips
    third = qkv.shape[1] // 3

    @pl.when(pl.program_id(0) == 0)
    def _():
        small[...] = jnp.zeros_like(small)
        bias[...] = jnp.zeros_like(bias)

    for q in range(4):
        down[q * rows : (q + 1) * rows] = shared[q, :rows].astype(f32)
        for s in range(chips):
            start = (s * 4 + q) * unit
            up[:, start : start + unit] = shared[q, rows : 2 * rows, s * unit : (s + 1) * unit].astype(f32)
        base, kept = 2 * rows + few, rows - few
        for i in range(3):
            here = slice(i * third + q * head_cols, i * third + (q + 1) * head_cols)
            qkv[:kept, here] = shared[q, base : base + kept, i * head_cols : (i + 1) * head_cols].astype(f32)
            qkv[kept:, here] = shared[q, base + i * few : base + (i + 1) * few, 3 * head_cols :].astype(f32)
        out[q] = shared[q, 2 * rows : base].astype(f32)
        extra = shared[q, 3 * rows :].astype(f32)
        small[...] += extra
        bias[q : q + 1] += extra[5:6]


def unfold(shared, rows, few, ff):
    devices, deep, width = shared.shape
    chips = devices // 4
    f32 = jnp.float32
    head_cols = width // 4
    return pl.pallas_call(
        functools.partial(unfold_kernel, rows, head_cols, few),
        grid=(chips,),
        in_specs=[pl.BlockSpec((4, deep, width), lambda s: (s, 0, 0))],
        out_specs=[
            pl.BlockSpec((4 * rows, width), lambda s: (s, 0)),
            pl.BlockSpec((rows, ff), lambda s: (s, 0)),
            pl.BlockSpec((rows, 3 * width), lambda s: (s, 0)),
            pl.BlockSpec((4, None, few, width), lambda s: (0, s, 0, 0)),
            pl.BlockSpec((deep - 3 * rows, width), lambda s: (0, 0)),
            pl.BlockSpec((4, width), lambda s: (0, 0)),
        ],
        out_shape=[
            jax.ShapeDtypeStruct((ff, width), f32),
            jax.ShapeDtypeStruct((width, ff), f32),
            jax.ShapeDtypeStruct((width, 3 * width), f32),
            jax.ShapeDtypeStruct((4, chips, few, width), f32),
            jax.ShapeDtypeStruct((deep - 3 * rows, width), f32),
            jax.ShapeDtypeStruct((4, width), f32),
        ],
        compiler_params=pltpu.CompilerParams(vmem_limit_bytes=56 << 20),
    )(shared)


def on_quad(
    tokens,
    lengths,
    attn_gain,
    attn_shift,
    w_qkv,
    w_out,
    ffn_gain,
    ffn_shift,
    w_up,
    b_up,
    w_down,
    b_down,
    cotangent,
):
    low = jnp.bfloat16
    local, width = tokens.shape
    n_dp = lax.axis_size("dp")
    n_z, chips = n_dp // 4, n_dp // 2
    size = width // HEADS
    heads = HEADS // 4
    count = 2 * local
    me = Place(n_z)
    lens = jnp.zeros((8, 128), jnp.int32).at[:1, : lengths.shape[1]].set(lengths)
    gains = [value.reshape(1, width) for value in (attn_gain, attn_shift, ffn_gain, ffn_shift)]
    WQ, WOQ, WU, WD, CQ, h1, qkv, o, lse, h2, middle, LQ = front(
        n_z, lengths.shape[1], w_qkv, w_out, w_up, w_down, tokens, cotangent, lens, gains
    )
    unit = w_up.shape[1] // chips // 4
    bias = lax.dynamic_index_in_dim(b_up.reshape(chips, 4, unit), me.quarter, 1, keepdims=False).reshape(-1)
    block_out, grad_tokens, shared = back(
        n_z,
        lengths.shape[1],
        [h2, CQ.reshape(4 * local, width), WU, WD],
        middle,
        cotangent,
        tokens,
        [h1.reshape(4 * local, width), qkv, o, lse, WQ, WOQ],
        LQ,
        bias.reshape(1, width),
        gains[0],
        gains[2],
        b_down.reshape(1, width),
    )
    rows, few = width // chips, width // 4 // chips
    ff = w_up.shape[1]
    grad_w_down, grad_w_up, grad_w_qkv, grad_w_out, vectors, bias = unfold(shared, rows, few, ff)
    return (
        block_out,
        grad_tokens,
        vectors[0],
        vectors[1],
        grad_w_qkv,
        grad_w_out.reshape(width, width),
        vectors[2],
        vectors[3],
        grad_w_up,
        jnp.transpose(bias.reshape(4, chips, unit), (1, 0, 2)).reshape(ff),
        grad_w_down,
        vectors[4],
    )


def solution(mesh):
    n_dp, n_seq = mesh.shape["dp"], mesh.shape["seq"]
    quad = n_seq == 2 and n_dp % 4 == 0 and n_dp >= 8 and n_dp <= 16
    return jax.shard_map(
        on_quad if quad else on_device,
        mesh=mesh,
        in_specs=(
            P(("dp", "seq"), None),
            P("dp", None),
            P(),
            P(),
            P("dp", None),
            P("dp", None),
            P(),
            P(),
            P("dp", None),
            P(),
            P("dp", None),
            P(),
            P(("dp", "seq"), None),
        ),
        out_specs=(
            P(("dp", "seq"), None),
            P(("dp", "seq"), None),
            P(),
            P(),
            P(),
            P(),
            P(),
            P(),
            P(),
            P(),
            P(),
            P(),
        ),
        check_vma=False,
    )
```

```python
import functools

import jax
import jax.numpy as jnp
from jax import lax
from jax.experimental import pallas as pl
from jax.experimental.pallas import tpu as pltpu
from jax.sharding import PartitionSpec as P

HEADS = 8


EPS = 1e-05
NEVER = -1000000000.0


def inner_rows(left, right):
    return lax.dot_general(
        left, right, (((0,), (0,)), ((), ())), preferred_element_type=jnp.float32
    )


def times_transposed(left, right):
    return lax.dot_general(
        left, right, (((1,), (1,)), ((), ())), preferred_element_type=jnp.float32
    )


def smooth_act(values):
    return jax.nn.gelu(values, approximate=True)


def norm_forward(values, gain, shift):
    mean = jnp.mean(values, axis=-1, keepdims=True)
    centred = values - mean
    variance = jnp.mean(centred * centred, axis=-1, keepdims=True)
    factor = lax.rsqrt(variance + EPS)
    normed = centred * factor
    return (normed * gain + shift, normed, factor)


def norm_backward(grad_out, normed, factor, gain):
    grad_normed = grad_out * gain
    centre_term = jnp.mean(grad_normed, axis=-1, keepdims=True)
    along_term = jnp.mean(grad_normed * normed, axis=-1, keepdims=True)
    grad_in = factor * (grad_normed - centre_term - normed * along_term)
    return (grad_in, jnp.sum(grad_out * normed, axis=0), jnp.sum(grad_out, axis=0))


def item_ids(item_lengths, count):
    item_ends = jnp.cumsum(item_lengths, dtype=jnp.int32)
    places = jnp.arange(count, dtype=jnp.int32)
    hits = (places[:, None] >= item_ends[None, :]).astype(jnp.int32)
    return jnp.sum(hits, axis=1, dtype=jnp.int32)


def block_scores(query_block, keys, start, item_of, slopes):
    rows = query_block.shape[0]
    count = keys.shape[0]
    scale = query_block.shape[-1] ** (-0.5)
    raw = jnp.einsum("qhd,khd->hqk", query_block, keys, preferred_element_type=jnp.float32)
    row_places = start + jnp.arange(rows, dtype=jnp.int32)
    col_places = jnp.arange(count, dtype=jnp.int32)
    distance = (row_places[:, None] - col_places[None, :]).astype(jnp.float32)
    row_items = lax.dynamic_slice_in_dim(item_of, start, rows)
    allowed = (row_items[:, None] == item_of[None, :]) & (
        col_places[None, :] <= row_places[:, None]
    )
    scores = raw * scale - slopes[:, None, None] * distance[None]
    return jnp.where(allowed[None], scores, jnp.float32(-1000000000.0))


def attend(heads_qkv, item_of, slopes):
    count = heads_qkv.shape[0]
    rows = min(512, count)
    queries = heads_qkv[:, 0]
    keys = heads_qkv[:, 1]
    values = heads_qkv[:, 2]

    def one_block(index):
        start = index * rows
        query_block = lax.dynamic_slice_in_dim(queries, start, rows)
        scores = block_scores(query_block, keys, start, item_of, slopes)
        top = jnp.max(scores, axis=-1, keepdims=True)
        weights = jnp.exp(scores - top)
        total = jnp.sum(weights, axis=-1, keepdims=True)
        probs = (weights / total).astype(jnp.bfloat16)
        mixed = jnp.einsum("hqk,khd->qhd", probs, values, preferred_element_type=jnp.float32)
        return (mixed.astype(jnp.bfloat16), (top + jnp.log(total))[..., 0])

    mixed, log_norm = lax.map(one_block, jnp.arange(count // rows, dtype=jnp.int32))
    return (mixed.reshape(count, mixed.shape[2], mixed.shape[3]), log_norm)


def attend_back(heads_qkv, heads_out, grad_heads, log_norm, item_of, slopes):
    count = heads_qkv.shape[0]
    rows = min(512, count)
    queries = heads_qkv[:, 0]
    keys = heads_qkv[:, 1]
    values = heads_qkv[:, 2]
    scale = queries.shape[-1] ** (-0.5)
    row_dots = jnp.sum(grad_heads.astype(jnp.float32) * heads_out.astype(jnp.float32), axis=-1)

    def one_block(carry, index):
        grad_keys, grad_values = carry
        start = index * rows
        query_block = lax.dynamic_slice_in_dim(queries, start, rows)
        grad_block = lax.dynamic_slice_in_dim(grad_heads, start, rows)
        dots = lax.dynamic_slice_in_dim(row_dots, start, rows)
        scores = block_scores(query_block, keys, start, item_of, slopes)
        probs = jnp.exp(scores - log_norm[index][:, :, None])
        probs_low = probs.astype(jnp.bfloat16)
        grad_values = grad_values + jnp.einsum(
            "hqk,qhd->khd", probs_low, grad_block, preferred_element_type=jnp.float32
        )
        grad_probs = jnp.einsum(
            "qhd,khd->hqk", grad_block, values, preferred_element_type=jnp.float32
        )
        grad_scores = (probs * (grad_probs - jnp.transpose(dots)[:, :, None])).astype(jnp.bfloat16)
        grad_query = (
            jnp.einsum("hqk,khd->qhd", grad_scores, keys, preferred_element_type=jnp.float32)
            * scale
        )
        grad_keys = (
            grad_keys
            + jnp.einsum(
                "hqk,qhd->khd", grad_scores, query_block, preferred_element_type=jnp.float32
            )
            * scale
        )
        return ((grad_keys, grad_values), grad_query)

    empty = jnp.zeros(keys.shape, jnp.float32)
    (grad_keys, grad_values), grad_query = lax.scan(
        one_block, (empty, empty), jnp.arange(count // rows, dtype=jnp.int32)
    )
    grad_query = grad_query.reshape(keys.shape)
    return jnp.stack([grad_query, grad_keys, grad_values], axis=1).astype(jnp.bfloat16)


def on_device(
    tokens,
    lengths,
    attn_gain,
    attn_shift,
    w_qkv,
    w_out,
    ffn_gain,
    ffn_shift,
    w_up,
    b_up,
    w_down,
    b_down,
    cotangent,
):
    w_qkv, w_out, w_up, w_down = (
        lax.all_gather(w_qkv, "dp", axis=0, tiled=True),
        lax.all_gather(w_out, "dp", axis=0, tiled=True),
        lax.all_gather(w_up, "dp", axis=0, tiled=True),
        lax.all_gather(w_down, "dp", axis=0, tiled=True),
    )
    local, width = tokens.shape
    groups = lax.axis_size("seq")
    per_head = width // HEADS
    local_heads = HEADS // groups
    count = local * groups
    item_of = item_ids(lengths[0], count)
    first_head = lax.axis_index("seq") * local_heads
    exponents = (first_head + jnp.arange(local_heads, dtype=jnp.int32) + 1).astype(jnp.float32)
    slopes = jnp.exp2(-exponents)
    inputs = tokens.astype(jnp.float32)
    normed_in, unit_in, factor_in = norm_forward(inputs, attn_gain, attn_shift)
    first_in = normed_in.astype(jnp.bfloat16)
    projected = jnp.dot(first_in, w_qkv, preferred_element_type=jnp.float32).astype(jnp.bfloat16)
    projected = projected.reshape(local, 3, HEADS, per_head)
    heads_qkv = lax.all_to_all(projected, "seq", split_axis=2, concat_axis=0, tiled=True)
    heads_out, log_norm = attend(heads_qkv, item_of, slopes)
    joined = lax.all_to_all(heads_out, "seq", split_axis=0, concat_axis=1, tiled=True).reshape(
        local, width
    )
    middle = inputs + jnp.dot(joined, w_out, preferred_element_type=jnp.float32)
    normed_mid, unit_mid, factor_mid = norm_forward(middle, ffn_gain, ffn_shift)
    second_in = normed_mid.astype(jnp.bfloat16)
    pre_act = jnp.dot(second_in, w_up, preferred_element_type=jnp.float32) + b_up
    act_value, act_pull = jax.vjp(smooth_act, pre_act)
    active = act_value.astype(jnp.bfloat16)
    block_out = (
        middle + jnp.dot(active, w_down, preferred_element_type=jnp.float32) + b_down
    ).astype(jnp.bfloat16)
    grad_out = cotangent.astype(jnp.float32)
    grad_b_down = jnp.sum(grad_out, axis=0)
    grad_w_down = inner_rows(active, cotangent)
    grad_active = times_transposed(cotangent, w_down)
    grad_pre = act_pull(grad_active)[0]
    grad_b_up = jnp.sum(grad_pre, axis=0)
    grad_pre_low = grad_pre.astype(jnp.bfloat16)
    grad_w_up = inner_rows(second_in, grad_pre_low)
    grad_second = times_transposed(grad_pre_low, w_up)
    grad_mid_norm, grad_ffn_gain, grad_ffn_shift = norm_backward(
        grad_second, unit_mid, factor_mid, ffn_gain
    )
    grad_middle = grad_out + grad_mid_norm
    grad_branch = grad_middle.astype(jnp.bfloat16)
    grad_w_out = inner_rows(joined, grad_branch)
    grad_joined = (
        times_transposed(grad_branch, w_out).astype(jnp.bfloat16).reshape(local, HEADS, per_head)
    )
    grad_heads = lax.all_to_all(grad_joined, "seq", split_axis=1, concat_axis=0, tiled=True)
    grad_qkv_heads = attend_back(heads_qkv, heads_out, grad_heads, log_norm, item_of, slopes)
    grad_projected = lax.all_to_all(
        grad_qkv_heads, "seq", split_axis=0, concat_axis=2, tiled=True
    ).reshape(local, 3 * width)
    grad_w_qkv = inner_rows(first_in, grad_projected)
    grad_first = times_transposed(grad_projected, w_qkv)
    grad_in_norm, grad_attn_gain, grad_attn_shift = norm_backward(
        grad_first, unit_in, factor_in, attn_gain
    )
    grad_tokens = (grad_middle + grad_in_norm).astype(jnp.bfloat16)
    all_part = (
        lax.psum_scatter(
            grad_attn_gain.astype(jnp.bfloat16), "dp", scatter_dimension=0, tiled=True
        ).astype(jnp.float32),
        lax.psum_scatter(
            grad_attn_shift.astype(jnp.bfloat16), "dp", scatter_dimension=0, tiled=True
        ).astype(jnp.float32),
        lax.psum_scatter(
            grad_w_qkv.astype(jnp.bfloat16), "dp", scatter_dimension=0, tiled=True
        ).astype(jnp.float32),
        lax.psum_scatter(
            grad_w_out.astype(jnp.bfloat16), "dp", scatter_dimension=0, tiled=True
        ).astype(jnp.float32),
        lax.psum_scatter(
            grad_ffn_gain.astype(jnp.bfloat16), "dp", scatter_dimension=0, tiled=True
        ).astype(jnp.float32),
        lax.psum_scatter(
            grad_ffn_shift.astype(jnp.bfloat16), "dp", scatter_dimension=0, tiled=True
        ).astype(jnp.float32),
        lax.psum_scatter(
            grad_w_up.astype(jnp.bfloat16), "dp", scatter_dimension=0, tiled=True
        ).astype(jnp.float32),
        lax.psum_scatter(
            grad_b_up.astype(jnp.bfloat16), "dp", scatter_dimension=0, tiled=True
        ).astype(jnp.float32),
        lax.psum_scatter(
            grad_w_down.astype(jnp.bfloat16), "dp", scatter_dimension=0, tiled=True
        ).astype(jnp.float32),
        lax.psum_scatter(
            grad_b_down.astype(jnp.bfloat16), "dp", scatter_dimension=0, tiled=True
        ).astype(jnp.float32),
    )
    all_part = (
        lax.psum(all_part[0].astype(jnp.bfloat16), "seq").astype(jnp.float32),
        lax.psum(all_part[1].astype(jnp.bfloat16), "seq").astype(jnp.float32),
        lax.psum(all_part[2].astype(jnp.bfloat16), "seq").astype(jnp.float32),
        lax.psum(all_part[3].astype(jnp.bfloat16), "seq").astype(jnp.float32),
        lax.psum(all_part[4].astype(jnp.bfloat16), "seq").astype(jnp.float32),
        lax.psum(all_part[5].astype(jnp.bfloat16), "seq").astype(jnp.float32),
        lax.psum(all_part[6].astype(jnp.bfloat16), "seq").astype(jnp.float32),
        lax.psum(all_part[7].astype(jnp.bfloat16), "seq").astype(jnp.float32),
        lax.psum(all_part[8].astype(jnp.bfloat16), "seq").astype(jnp.float32),
        lax.psum(all_part[9].astype(jnp.bfloat16), "seq").astype(jnp.float32),
    )
    summed = (
        lax.all_gather(all_part[0].astype(jnp.bfloat16), "dp", axis=0, tiled=True).astype(
            jnp.float32
        ),
        lax.all_gather(all_part[1].astype(jnp.bfloat16), "dp", axis=0, tiled=True).astype(
            jnp.float32
        ),
        lax.all_gather(all_part[2].astype(jnp.bfloat16), "dp", axis=0, tiled=True).astype(
            jnp.float32
        ),
        lax.all_gather(all_part[3].astype(jnp.bfloat16), "dp", axis=0, tiled=True).astype(
            jnp.float32
        ),
        lax.all_gather(all_part[4].astype(jnp.bfloat16), "dp", axis=0, tiled=True).astype(
            jnp.float32
        ),
        lax.all_gather(all_part[5].astype(jnp.bfloat16), "dp", axis=0, tiled=True).astype(
            jnp.float32
        ),
        lax.all_gather(all_part[6].astype(jnp.bfloat16), "dp", axis=0, tiled=True).astype(
            jnp.float32
        ),
        lax.all_gather(all_part[7].astype(jnp.bfloat16), "dp", axis=0, tiled=True).astype(
            jnp.float32
        ),
        lax.all_gather(all_part[8].astype(jnp.bfloat16), "dp", axis=0, tiled=True).astype(
            jnp.float32
        ),
        lax.all_gather(all_part[9].astype(jnp.bfloat16), "dp", axis=0, tiled=True).astype(
            jnp.float32
        ),
    )
    return (
        block_out,
        grad_tokens,
        summed[0],
        summed[1],
        summed[2],
        summed[3],
        summed[4],
        summed[5],
        summed[6],
        summed[7],
        summed[8],
        summed[9],
    )


MESH = pl.DeviceIdType.MESH


class Place:
    def __init__(self, n_z):
        dp = lax.axis_index("dp")
        self.n_z = n_z
        self.dp = dp
        self.y = lax.axis_index("seq")
        self.core = dp % 2
        self.chip = dp // 2
        self.x = self.chip % 2
        self.z = self.chip // 2
        self.quarter = 2 * self.core + self.y

    def device(self, z=None, x=None, core=None, y=None):
        z = self.z if z is None else z
        x = self.x if x is None else x
        core = self.core if core is None else core
        y = self.y if y is None else y
        return ((z * 2 + x) * 2 + core, y)

    def across_core(self):
        return self.device(core=1 - self.core)

    def across_x(self):
        return self.device(x=1 - self.x)

    def across_y(self):
        return self.device(y=1 - self.y)

    def z_after(self, k):
        return (self.z + k) % self.n_z

    def z_before(self, k):
        return (self.z + self.n_z - k) % self.n_z

    def along_z(self, k):
        return self.device(z=self.z_after(k))


class Copy:
    def __init__(self, copy, sends, lands):
        self.copy, self.sends, self.lands, self.landed = copy, sends, lands, False

    def guarded(self, condition, action):
        if condition is None:
            action()
        else:
            pl.when(condition)(action)


class Copies:
    def __init__(self, send, recv, near):
        self.send, self.recv, self.near = send, recv, near
        self.all, self.n, self.m, self.local_open = [], 0, 0, []

    def remote(self, src, dst, device, sends=None, lands=None):
        copy = Copy(
            pltpu.make_async_remote_copy(
                src_ref=src,
                dst_ref=dst,
                send_sem=self.send.at[self.n],
                recv_sem=self.recv.at[self.n],
                device_id=device,
                device_id_type=MESH,
            ),
            sends,
            lands,
        )
        self.n += 1
        copy.guarded(sends, copy.copy.start)
        self.all.append(copy)
        return copy

    def local(self, src, dst):
        copy = pltpu.make_async_copy(src, dst, self.near.at[self.m])
        self.m += 1
        copy.start()
        return copy

    def later(self, src, dst):
        self.local_open.append(self.local(src, dst))

    def arrive(self, *copies):
        for copy in copies:
            if not copy.landed:
                copy.guarded(copy.lands, copy.copy.wait_recv)
                copy.landed = True

    def finish(self):
        self.arrive(*self.all)
        for copy in self.all:
            copy.guarded(copy.sends, copy.copy.wait_send)
        for copy in self.local_open:
            copy.wait()


class Line:
    def __init__(self, me, run, own, view):
        self.me, self.run, self.view = me, run, view
        n, z = me.n_z, me.z
        self.up = [run.remote(own, view(z), me.device(z=z + 1), z < n - 1, z > 0)]
        self.down = [run.remote(own, view(z), me.device(z=z - 1), z > 0, z < n - 1)]

    def step(self, t, then):
        me, run, n, z = self.me, self.run, self.me.n_z, self.me.z
        if t >= n:
            return
        run.arrive(self.up[t - 1])
        if t < n - 1:
            part = self.view(z - t)
            self.up.append(run.remote(part, part, me.device(z=z + 1), (z >= t) & (z < n - 1), z > t))
        then(z - t, z >= t)
        run.arrive(self.down[t - 1])
        if t < n - 1:
            part = self.view(z + t)
            self.down.append(
                run.remote(part, part, me.device(z=z - 1), (z < n - t) & (z > 0), z < n - t - 1)
            )
        then(z + t, z < n - t)


def meet(devices):
    barrier = pltpu.get_barrier_semaphore()
    for device in devices:
        pl.semaphore_signal(barrier, inc=1, device_id=device, device_id_type=MESH)
    pl.semaphore_wait(barrier, len(devices))


def at(start, size, unit):
    return pl.ds(pl.multiple_of(start, unit), size)


def communicate(kernel, out_shapes, ins, out_specs, in_specs, counts, scratch=(), call_id=0, limit=None):
    return pl.pallas_call(
        kernel,
        out_shape=out_shapes,
        in_specs=in_specs,
        out_specs=out_specs,
        scratch_shapes=list(scratch)
        + [
            pltpu.SemaphoreType.DMA((counts[0],)),
            pltpu.SemaphoreType.DMA((counts[0],)),
            pltpu.SemaphoreType.DMA((counts[1],)),
        ],
        compiler_params=pltpu.CompilerParams(
            collective_id=call_id, has_side_effects=True, vmem_limit_bytes=limit or (56 << 20)
        ),
    )(*ins)


HBM = pl.BlockSpec(memory_space=pltpu.HBM)
VMEM = pl.BlockSpec(memory_space=pltpu.VMEM)
SMEM = pl.BlockSpec(memory_space=pltpu.SMEM)


def allowed_and_bias(first, rows, count, ends, slope):
    row = first + lax.broadcasted_iota(jnp.int32, (rows, 1), 0)
    col = lax.broadcasted_iota(jnp.int32, (1, count), 1)
    begin = jnp.zeros((rows, 1), jnp.int32)
    for end in ends:
        begin = jnp.where(row >= end, end, begin)
    allowed = (col >= begin) & (col <= row)
    bias = slope * (col - first).astype(jnp.float32)
    return allowed, bias


def norm_rows(values, gain, shift):
    mean = jnp.mean(values, axis=-1, keepdims=True)
    centred = values - mean
    variance = jnp.mean(centred * centred, axis=-1, keepdims=True)
    return centred * lax.rsqrt(variance + EPS) * gain + shift


def norm_block(src, dst, gain, shift, step=64):
    @pl.loop(0, src.shape[0], step=step)
    def _(i):
        rows = at(i, step, step)
        dst[rows, :] = norm_rows(src[rows, :].astype(jnp.float32), gain[...], shift[...]).astype(dst.dtype)


def front_kernel(
    n_z,
    n_items,
    wq,
    wo,
    wu,
    wd,
    tok,
    cot,
    lens,
    attn_gain,
    attn_shift,
    ffn_gain,
    ffn_shift,
    WQ,
    WOQ,
    WU,
    WD,
    CQ,
    H1,
    QKV,
    O,
    LSE,
    H2,
    MID,
    LQ,
    q_all,
    o_all,
    x_all,
    h1,
    qkv,
    mixed,
    lse,
    h2,
    middle,
    ends,
    send,
    recv,
    near,
):
    me = Place(n_z)
    run = Copies(send, recv, near)
    quarter, other = me.quarter, 2 * (1 - me.core) + me.y
    rows = wq.shape[0]
    third = wq.shape[1] // 3
    cut = third // 4
    chips = 2 * n_z
    span = wu.shape[1] // chips
    unit = span // 4
    local = tok.shape[0]
    count = 2 * local
    half = local // 2
    size = third // HEADS
    heads = HEADS // 4
    meet(
        [me.across_core(), me.across_x(), me.across_y()] + [me.along_z(k) for k in range(1, n_z)]
    )
    mine = at(me.dp * rows, rows, 16)

    into = [q_all.at[mine, p * cut : (p + 1) * cut] for p in range(3)]
    near_q = [run.local(wq.at[:, at(p * third + quarter * cut, cut, 128)], into[p]) for p in range(3)]
    core_q = [
        run.remote(wq.at[:, at(p * third + other * cut, cut, 128)], into[p], me.across_core())
        for p in range(3)
    ]
    keep_x = run.local(tok, x_all.at[quarter])
    keep_lens = run.local(lens, LQ.at[me.core])
    core_lens = run.remote(lens, LQ.at[me.core], me.across_core())

    def halves(h):
        return slice(h * half, (h + 1) * half)

    over_x = [
        run.remote(tok.at[halves(h)], x_all.at[quarter, halves(h)], me.across_y()) for h in range(2)
    ]
    core_x = run.remote(tok, x_all.at[quarter], me.across_core())
    into = [WU.at[mine, s * unit : (s + 1) * unit] for s in range(chips)]
    near_u = [run.local(wu.at[:, at(s * span + quarter * unit, unit, 128)], into[s]) for s in range(chips)]
    core_u = [
        run.remote(wu.at[:, at(s * span + other * unit, unit, 128)], into[s], me.across_core())
        for s in range(chips)
    ]

    def pairs_of(array):
        return lambda z, x=me.x: array.at[at((z * 2 + x) * 2 * rows, 2 * rows, 16)]

    def shard_of(z, x=me.x):
        return o_all.at[at(((z * 2 + x) * 2 + me.core) * rows, rows, 16)]

    def units_of(z, x=me.x):
        return WD.at[at((z * 2 + x) * unit, unit // 2, 16)]

    def late_units_of(z, x=me.x):
        return WD.at[at((z * 2 + x) * unit + unit // 2, unit // 2, 16)]

    from_x = {"q": [], "o": [], "u": [], "d": []}
    share_o = []

    def across(name, view):
        def then(z, came):
            part = view(z)
            from_x[name].append((run.remote(part, part, me.across_x(), came, came), z, came))
            if name == "o":
                share_o.append(run.remote(part, part, me.across_core(), came, came))

        return then

    for copy in near_q:
        copy.wait()
    run.arrive(*core_q)
    view_q, view_u = pairs_of(q_all), pairs_of(WU)
    line_q = Line(me, run, view_q(me.z), view_q)
    across("q", view_q)(me.z, None)
    keep_o = run.local(wo, shard_of(me.z))
    keep_x.wait()
    norm_block(x_all.at[quarter], h1.at[quarter], attn_gain, attn_shift)
    run.arrive(core_x)
    line_q.step(1, across("q", view_q))
    line_o = Line(me, run, wo, shard_of)
    share_o.append(run.remote(wo, shard_of(me.z), me.across_core()))
    norm_block(x_all.at[other], h1.at[other], attn_gain, attn_shift)
    line_q.step(2, across("q", view_q))
    beside = 2 * me.core + 1 - me.y
    far = 2 * (1 - me.core) + 1 - me.y
    far_x = []
    for h in range(2):
        run.arrive(over_x[h])
        part = x_all.at[beside, halves(h)]
        far_x.append(run.remote(part, part, me.across_core()))
        if h == 0:
            line_q.step(3, across("q", view_q))
            from_x["o"].append((run.remote(wo, shard_of(me.z), me.across_x()), me.z, None))
            line_o.step(1, across("o", shard_of))
            for copy in near_u:
                copy.wait()
            run.arrive(*core_u)
            line_u = Line(me, run, view_u(me.z), view_u)
        norm_block(x_all.at[beside, halves(h)], h1.at[beside, halves(h)], attn_gain, attn_shift)
    over_c = [run.remote(cot.at[halves(0)], CQ.at[quarter, halves(0)], me.across_y())]
    run.remote(cot, CQ.at[quarter], me.across_core())
    for h in range(2):
        run.arrive(far_x[h])
        norm_block(x_all.at[far, halves(h)], h1.at[far, halves(h)], attn_gain, attn_shift)
    line_o.step(2, across("o", shard_of))
    part_d = unit // 2
    own = wd.at[at(me.y * unit, part_d, 16)]
    own_late = wd.at[at(me.y * unit + part_d, part_d, 16)]
    across("u", view_u)(me.z, None)
    run.later(h1, H1)
    for copy, _, _ in from_x["q"]:
        run.arrive(copy)
    run.later(q_all, WQ)

    @pl.loop(0, 4 * local, step=256)
    def _(i):
        block = at(i, 256, 256)
        qkv[block, :] = jnp.dot(
            h1[i // local, at(i % local, 256, 256), :], q_all[...], preferred_element_type=jnp.float32
        ).astype(jnp.bfloat16)

    run.later(qkv, QKV)
    keep_lens.wait()
    run.arrive(core_lens)
    fetch = run.local(LQ, ends)
    fetch.wait()

    def heads_at(owner, head):
        return at(owner * heads * size + head * size, size, 128)

    over_o, near_o = [], []
    line_o.step(3, across("o", shard_of))
    line_d = Line(me, run, own, units_of)
    from_x["d"].append((run.remote(own, units_of(me.z), me.across_x()), me.z, None))
    run.later(own, units_of(me.z))
    swap_d = run.remote(own_late, late_units_of(me.z), me.across_x())
    line_e = Line(me, run, own_late, late_units_of)
    run.later(own_late, late_units_of(me.z))
    pumps = [
        lambda: line_u.step(1, across("u", view_u)),
        lambda: line_u.step(2, across("u", view_u)),
        lambda: line_u.step(3, across("u", view_u)),
        lambda: line_d.step(1, across("d", units_of)),
    ]
    for g in range(2):
        stops = []
        total = 0
        for item in range(n_items - 1):
            total = total + ends[g, 0, item]
            stops.append(total)
        for head in range(heads):
            slope = jnp.exp2(-(jnp.zeros((1, 1), jnp.float32) + (quarter * heads + head + 1)))
            column = heads_at(quarter, head)
            for first in range(0, count, 256):
                start, seen = g * count, first + 256
                here = slice(start + first, start + seen)
                allowed, bias = allowed_and_bias(first, 256, seen, stops, slope)
                keys = qkv[start : start + seen, (heads + head) * size : (heads + head + 1) * size]
                s = times_transposed(qkv[here, head * size : (head + 1) * size], keys) * size**-0.5 + bias
                s = jnp.where(allowed, s, NEVER)
                top = jnp.max(s, axis=-1, keepdims=True)
                w = jnp.exp(s - top)
                sum_w = jnp.sum(w, axis=-1, keepdims=True)
                p = (w * (1.0 / sum_w)).astype(jnp.bfloat16)
                values = qkv[start : start + seen, (2 * heads + head) * size : (2 * heads + head + 1) * size]
                mixed[here, column] = jnp.dot(p, values, preferred_element_type=jnp.float32).astype(
                    jnp.bfloat16
                )
                lse[g, head, first:seen] = top + jnp.log(sum_w)
            part = mixed.at[g * count : (g + 1) * count, column]
            over_o.append(run.remote(part, part, me.across_y()))
            near_o.append(run.remote(part, part, me.across_core()))
            pumps[g * heads + head]()
    run.later(mixed.at[:, at(quarter * heads * size, heads * size, 128)], O)
    run.later(lse, LSE)
    over_c.append(run.remote(cot.at[halves(1)], CQ.at[quarter, halves(1)], me.across_y()))
    run.arrive(over_c[0])
    part = CQ.at[beside, halves(0)]
    run.remote(part, part, me.across_core())
    far_o = []
    for copy, z, came in from_x["o"]:
        run.arrive(copy)
        part = shard_of(z, 1 - me.x)
        far_o.append(run.remote(part, part, me.across_core(), came, came))
    line_e.step(1, lambda z, came: None)
    run.arrive(swap_d)
    beyond = late_units_of(me.z, 1 - me.x)
    line_f = Line(me, run, beyond, lambda z: late_units_of(z, 1 - me.x))
    passed = []
    for g in range(2):
        for head in range(heads):
            run.arrive(over_o[g * heads + head])
            part = mixed.at[g * count : (g + 1) * count, heads_at(beside, head)]
            passed.append(run.remote(part, part, me.across_core()))
    line_d.step(2, across("d", units_of))
    keep_o.wait()
    run.arrive(*share_o, *far_o)
    run.later(o_all.at[at(quarter * heads * size, heads * size, 16)], WOQ)
    for g in range(2):
        run.arrive(*near_o[g * heads : (g + 1) * heads], *passed[g * heads : (g + 1) * heads])

        @pl.loop(0, count, step=256)
        def _(i):
            block = at(g * count + i, 256, 256)
            owner, inner = 2 * g + i // local, at(i % local, 256, 256)
            x1 = x_all[owner, inner, :].astype(jnp.float32) + jnp.dot(
                mixed[block, :], o_all[...], preferred_element_type=jnp.float32
            )
            h2[block, :] = norm_rows(x1, ffn_gain[...], ffn_shift[...]).astype(jnp.bfloat16)

            @pl.when(owner == quarter)
            def _():
                middle[inner, :] = x1

        line_d.step(3 + g, across("d", units_of))
        line_e.step(2 + g, lambda z, came: None)
        line_f.step(1 + g, lambda z, came: None)
    run.later(h2, H2)
    run.later(middle, MID)
    line_f.step(3, lambda z, came: None)
    run.arrive(over_c[1])
    part = CQ.at[beside, halves(1)]
    run.remote(part, part, me.across_core())
    run.finish()


def front(n_z, n_items, wq, wo, wu, wd, tok, cot, lens, gains):
    width, low, f32 = wq.shape[0] * 4 * n_z, jnp.bfloat16, jnp.float32
    quarter_ff = wu.shape[1] // 4
    local = tok.shape[0]
    heads, size = HEADS // 4, width // HEADS
    shape = jax.ShapeDtypeStruct
    shapes = [
        shape((width, wq.shape[1] // 4), low),
        shape((width // 4, width), low),
        shape((width, quarter_ff), low),
        shape((quarter_ff, width), low),
        shape((4, local, width), low),
        shape((4, local, width), low),
        shape((4 * local, 3 * width // 4), low),
        shape((4 * local, width // 4), low),
        shape((2, heads, 2 * local, 1), f32),
        shape((4 * local, width), low),
        shape((local, width), f32),
        shape((2,) + lens.shape, lens.dtype),
    ]
    scratch = [
        pltpu.VMEM((width, wq.shape[1] // 4), low),
        pltpu.VMEM((width, width), low),
        pltpu.VMEM((4, local, width), low),
        pltpu.VMEM((4, local, width), low),
        pltpu.VMEM((4 * local, 3 * width // 4), low),
        pltpu.VMEM((4 * local, width), low),
        pltpu.VMEM((2, heads, 2 * local, 1), f32),
        pltpu.VMEM((4 * local, width), low),
        pltpu.VMEM((local, width), f32),
        pltpu.SMEM((2,) + lens.shape, lens.dtype),
    ]
    return communicate(
        functools.partial(front_kernel, n_z, n_items),
        shapes,
        (wq, wo, wu, wd, tok, cot, lens) + tuple(gains),
        [HBM] * 12,
        [HBM] * 7 + [VMEM] * 4,
        (144, 34),
        scratch,
        call_id=1,
    )


def add(*values):
    total = values[0].astype(jnp.float32)
    for value in values[1:]:
        total = total + value.astype(jnp.float32)
    return total


class Share:
    def __init__(self, me, run, src, dst):
        self.me, self.run, self.src, self.dst = me, run, src, dst

    def slot(self, z, x, y):
        return ((z * 2 + x) * 2 + self.me.core) * 2 + y

    def steps(self, cut):
        me, run, src, dst, slot = self.me, self.run, self.src, self.dst, self.slot
        low, middle, high = cut
        first, second, whole = slice(low, middle), slice(middle, high), slice(low, high)
        own = dst.at[slot(me.z, me.x, me.y)]
        run.later(src.at[whole], own.at[whole])
        from_z = [run.remote(src.at[whole], own.at[whole], me.along_z(k)) for k in range(1, me.n_z)]
        xa, xb, ya, yb, late_a, late_b = [], [], [], [], [], []
        yield

        def fan(k):
            here = dst.at[slot(me.z_before(k), me.x, me.y)]
            if k:
                run.arrive(from_z[k - 1])
            there = here if k else src
            xa.append(run.remote(there.at[first], here.at[first], me.across_x()))
            yb.append(run.remote(there.at[second], here.at[second], me.across_y()))
            ya.append(run.remote(there.at[first], here.at[first], me.across_y()))
            xb.append(run.remote(there.at[second], here.at[second], me.across_x()))
            run.remote(there.at[whole], here.at[whole], me.across_core())

        def relay(k):
            z = me.z_before(k)
            run.arrive(xa[k])
            part = dst.at[slot(z, 1 - me.x, me.y), first]
            late_a.append(run.remote(part, part, me.across_y()))
            run.arrive(yb[k])
            part = dst.at[slot(z, me.x, 1 - me.y), second]
            late_b.append(run.remote(part, part, me.across_x()))

        def hand_over(k):
            z = me.z_before(k)
            run.arrive(xb[k])
            part = dst.at[slot(z, 1 - me.x, me.y), whole]
            run.remote(part, part, me.across_core())
            run.arrive(ya[k])
            part = dst.at[slot(z, me.x, 1 - me.y), whole]
            run.remote(part, part, me.across_core())

        def hand_last(k):
            run.arrive(late_a[k], late_b[k])
            part = dst.at[slot(me.z_before(k), 1 - me.x, 1 - me.y), whole]
            run.remote(part, part, me.across_core())

        for i in range(me.n_z + 3):
            for lag, action in enumerate((fan, relay, hand_over, hand_last)):
                if 0 <= i - lag < me.n_z:
                    action(i - lag)
            yield


    def flat_steps(self, cut):
        me, run, src, dst = self.me, self.run, self.src, self.dst
        whole = slice(*cut)
        own = dst.at[self.slot(me.z, me.x, me.y), whole]
        keep = run.local(src.at[whole], own)
        from_y = run.remote(src.at[whole], own, me.across_y())
        run.remote(src.at[whole], own, me.across_core())
        from_z = []

        def pair(z, x):
            return dst.at[pl.ds(self.slot(z, x, 0), 2), whole]

        def along(part):
            from_z.append([run.remote(part, part, me.along_z(k)) for k in range(1, me.n_z)])

        yield
        keep.wait()
        run.arrive(from_y)
        part = pair(me.z, me.x)
        from_x = run.remote(part, part, me.across_x())
        along(part)
        part = dst.at[self.slot(me.z, me.x, 1 - me.y), whole]
        run.remote(part, part, me.across_core())
        yield
        run.arrive(from_x)
        part = pair(me.z, 1 - me.x)
        along(part)
        run.remote(part, part, me.across_core())
        yield
        for k in range(1, me.n_z):
            for i, x in enumerate((me.x, 1 - me.x)):
                run.arrive(from_z[i][k - 1])
                part = pair(me.z_before(k), x)
                run.remote(part, part, me.across_core())
            yield


class ChipSum:
    def __init__(self, me, run, src, own, far, over):
        self.me, self.run, self.src, self.own, self.far, self.over = me, run, src, own, far, over
        self.sent = []

    def send(self, times=1):
        for _ in range(times):
            z = self.me.z_after(len(self.sent) + 1)
            piece = self.src.at[z * 2 + 1 - self.me.x]
            self.sent.append(self.run.remote(piece, self.far.at[z], self.me.across_x()))

    def steps(self, place, then=None):
        me, run = self.me, self.run
        along = []
        for k in range(1, me.n_z + 1):
            z = me.z_after(k)
            run.arrive(self.sent[k - 1])
            if then is not None:
                then()
            part = self.own(z)
            part[...] = add(part[...], self.far[z]).astype(jnp.bfloat16)
            if k < me.n_z:
                along.append(run.remote(part, self.over.at[k - 1], me.along_z(k)))
            yield
        run.arrive(*along)
        place(add(self.own(me.z)[...], *[self.over[k] for k in range(me.n_z - 1)]))
        yield


class QuadSum:
    def __init__(self, me, run, src, own, near, over):
        self.me, self.run, self.own, self.near, self.over = me, run, own, near, over
        self.src, self.given = src, []

    def start(self, y):
        me = self.me
        self.given.append(self.run.remote(self.src.at[2 * (1 - me.core) + y], self.near.at[y], me.across_core()))

    def cross(self, step=128):
        me, own, near = self.me, self.own, self.near
        self.run.arrive(self.given[0])

        @pl.loop(0, self.over.shape[0], step=step)
        def _(i):
            rows = at(i, step, step)
            own[1 - me.y, rows, :] = add(own[1 - me.y, rows, :], near[1 - me.y, rows, :]).astype(jnp.bfloat16)

        self.over_y = self.run.remote(own.at[1 - me.y], self.over, me.across_y())

    def landed(self):
        self.run.arrive(self.given[1], self.over_y)

    def rows(self, rows):
        y = self.me.y
        return add(self.own[y, rows, :], self.near[y, rows, :], self.over[rows, :])


def head_back(qkv, o, lse, do, dqkv, sum_k, sum_v, g, head, heads, size, count, stops, slope):
    scale = size**-0.5
    start = g * count
    sum_k[...] = jnp.zeros_like(sum_k)
    sum_v[...] = jnp.zeros_like(sum_v)

    def columns(part):
        return slice((part * heads + head) * size, (part * heads + head + 1) * size)

    mine = columns(0)
    for first in range(0, count, 256):
        seen = first + 256
        here, past = slice(start + first, start + seen), slice(start, start + seen)
        allowed, bias = allowed_and_bias(first, 256, seen, stops, slope)
        query, keys = qkv[here, mine], qkv[past, columns(1)]
        s = times_transposed(query, keys) * scale + bias
        p = jnp.exp(jnp.where(allowed, s, NEVER) - lse[g, head, first:seen])
        grad = do[here, mine]
        dots = jnp.sum(grad.astype(jnp.float32) * o[here, mine].astype(jnp.float32), axis=-1, keepdims=True)
        sum_v[:seen] += inner_rows(p.astype(jnp.bfloat16), grad)
        ds = (p * (times_transposed(grad, qkv[past, columns(2)]) - dots)).astype(jnp.bfloat16)
        dqkv[here, mine] = (jnp.dot(ds, keys, preferred_element_type=jnp.float32) * scale).astype(jnp.bfloat16)
        sum_k[:seen] += inner_rows(ds, query)
    dqkv[start : start + count, columns(1)] = (sum_k[...] * scale).astype(jnp.bfloat16)
    dqkv[start : start + count, columns(2)] = sum_v[...].astype(jnp.bfloat16)


def norm_parts(values):
    mean = jnp.mean(values, axis=-1, keepdims=True)
    centred = values - mean
    variance = jnp.mean(centred * centred, axis=-1, keepdims=True)
    factor = lax.rsqrt(variance + EPS)
    return centred * factor, factor


def norm_back_rows(grad, unit, factor, gain):
    scaled = grad * gain
    centre = jnp.mean(scaled, axis=-1, keepdims=True)
    along = jnp.mean(scaled * unit, axis=-1, keepdims=True)
    return factor * (scaled - centre - unit * along)


def gelu_and_slope(u):
    root, cube = 0.7978845608028654, 0.044715
    square = u * u
    t = jnp.tanh(root * u * (1.0 + cube * square))
    half = 0.5 * (1.0 + t)
    return u * half, half + 0.5 * u * (1.0 - t * t) * (root * (1.0 + 3.0 * cube * square))


def back_kernel(
    n_z,
    n_items,
    H2,
    C,
    WU,
    WD,
    MID,
    cot_in,
    tok_in,
    H1,
    QKV,
    O,
    LSE,
    WQ,
    WOQ,
    LQ,
    b_up,
    attn_gain,
    ffn_gain,
    b_down,
    BLOCK_OUT,
    GRAD_TOKENS,
    SHARED,
    rows_c,
    rows_h2,
    rows_a,
    rows_du,
    mat_u,
    mat_d,
    part_h2,
    near_h2,
    over_h2,
    part_out,
    near_out,
    over_out,
    grad_d,
    far_d,
    over_d,
    grad_u,
    far_u,
    over_u,
    middle,
    cot,
    lse,
    ends,
    branch,
    sum_k,
    sum_v,
    acc_o,
    grad_q,
    far_q,
    over_q,
    grad_o,
    far_o,
    over_o,
    small,
    slab,
    send,
    recv,
    near,
):
    me = Place(n_z)
    run = Copies(send, recv, near)
    quarter = me.quarter
    other, beside, far = 2 * (1 - me.core) + me.y, 2 * me.core + 1 - me.y, 2 * (1 - me.core) + 1 - me.y
    low, f32 = jnp.bfloat16, jnp.float32
    chips = 2 * n_z
    local, width = tok_in.shape
    count, half = 2 * local, local // 2
    size = width // HEADS
    heads = HEADS // 4
    rows = grad_d.shape[1]
    few = grad_o.shape[1]
    cols = 3 * heads * size
    meet(
        [me.across_core(), me.across_x(), me.across_y()] + [me.along_z(k) for k in range(1, n_z)]
    )

    def fetch(block, grads=None):
        here = at(block * local, local, 256)
        return [
            run.local(H2.at[here], rows_h2.at[here]),
            run.local(C.at[here] if grads is None else grads, rows_c.at[here]),
        ]

    load_first = [run.local(WU, mat_u)] + fetch(far) + [run.local(WD, mat_d)]
    load_next = [fetch(other), fetch(beside), fetch(quarter, cot_in)]
    load_mid = [run.local(MID, middle), run.local(cot_in, cot)]
    load_few = [run.local(a, b) for a, b in ((LSE, lse), (LQ, ends))]
    small[...] = jnp.zeros_like(small)
    acc_o[...] = jnp.zeros_like(acc_o)
    group = pl.ds(2 * me.core, 2)
    sum_h2 = QuadSum(me, run, part_h2, part_h2.at[group], near_h2, over_h2)
    sum_out = QuadSum(me, run, part_out, part_out.at[group], near_out, over_out)
    down = ChipSum(me, run, grad_d, lambda z: grad_d.at[z * 2 + me.x], far_d, over_d)
    up = ChipSum(me, run, grad_u, lambda z: grad_u.at[z * 2 + me.x], far_u, over_u)

    def feed(block):
        @pl.loop(0, local, step=512)
        def _(i):
            here, there = at(i, 512, 256), at(block * local + i, 512, 256)
            values, grads = rows_h2[there, :], rows_c[there, :]
            for j in range(0, width, 256):
                part = slice(j, j + 256)
                u = jnp.dot(values, mat_u[:, part], preferred_element_type=f32) + b_up[:, part]
                bent, slope = gelu_and_slope(u)
                rows_a[there, part] = bent.astype(low)
                du = times_transposed(grads, mat_d[part, :]) * slope
                rows_du[block, here, part] = du.astype(low)
                small[5:6, part] += jnp.sum(du, axis=0, keepdims=True)
            part_h2[block, here, :] = times_transposed(rows_du[block, here, :], mat_u[...]).astype(low)

    def feed_out(block):
        @pl.loop(0, local, step=256)
        def _(i):
            here, there = at(i, 256, 256), at(block * local + i, 256, 256)
            part_out[block, here, :] = jnp.dot(rows_a[there, :], mat_d[...], preferred_element_type=f32).astype(low)

    def weight_grad(into, left, right):
        @pl.loop(0, chips // 2)
        def _(i):
            columns = at(i * 2 * rows, 2 * rows, 128)
            total = inner_rows(left(columns, 0), right(0))
            for block in range(1, 4):
                total = total + inner_rows(left(columns, block), right(block))
            into[pl.ds(2 * i, 2)] = total.reshape(2, rows, total.shape[1]).astype(low)

    def block_rows(block):
        return slice(block * local, (block + 1) * local)

    share = Share(me, run, slab, SHARED)

    def to_slab(start, columns=slice(None)):
        def place(value):
            slab[start : start + value.shape[0], columns] = value.astype(low)

        return place

    base = 2 * rows + few
    kept = rows - few

    def place_q(value):
        slab[base : base + kept, :cols] = value[:kept].astype(low)
        for i in range(3):
            slab[base + i * few : base + (i + 1) * few, cols:] = value[
                kept:, i * heads * size : (i + 1) * heads * size
            ].astype(low)

    def chain(total, place, *then):
        yield from total.steps(place)
        for thread in then:
            yield from thread

    run_down = chain(down, to_slab(0), share.steps((0, 3 * rows // 8, rows)))
    run_up = chain(up, to_slab(rows), share.steps((rows, rows + rows // 2, 2 * rows)))

    def pump(thread, times=1):
        for _ in range(times):
            next(thread, None)


    def await_all(copies):
        for copy in copies:
            copy.wait()

    await_all(load_first)
    feed(far)
    sum_h2.start(1 - me.y)
    await_all(load_next[0])
    feed(other)
    sum_h2.start(me.y)
    await_all(load_next[1])
    feed(beside)
    sum_h2.cross()
    await_all(load_next[2])
    feed(quarter)
    weight_grad(grad_d, lambda columns, b: rows_a[block_rows(b), columns], lambda b: rows_c[block_rows(b), :])
    down.send(n_z)
    weight_grad(grad_u, lambda columns, b: rows_h2[block_rows(b), columns], lambda b: rows_du[b])
    up.send(n_z)
    qkv, o = rows_c.at[:, :cols], rows_c.at[:, cols:]
    dqkv, do = rows_h2.at[:, :cols], rows_h2.at[:, cols:]
    h1, part_h1 = rows_a, rows_du
    w_q, w_o = mat_u.at[:, :cols], mat_d.at[: heads * size]
    load_o = [run.local(O, o)]
    load_few += [run.local(QKV, qkv), run.local(WQ, w_q)]
    pump(run_down, 2)
    for copy in load_mid:
        copy.wait()
    sum_h2.landed()

    @pl.loop(0, local, step=64)
    def _(i):
        here = at(i, 64, 64)
        unit, factor = norm_parts(middle[here, :])
        grad, c = sum_h2.rows(here), cot[here, :].astype(f32)
        total = c + norm_back_rows(grad, unit, factor, ffn_gain[...])
        branch[quarter, here, :] = total.astype(low)
        small[2:3] += jnp.sum(grad * unit, axis=0, keepdims=True)
        small[3:4] += jnp.sum(grad, axis=0, keepdims=True)
        small[4:5] += jnp.sum(c, axis=0, keepdims=True)

    load_few.append(run.local(tok_in, cot))
    own = branch.at[quarter]
    over_b = []
    for h in range(2):
        part = branch.at[quarter, h * half : (h + 1) * half]
        over_b.append(run.remote(part, part, me.across_y()))
    core_b = run.remote(own, own, me.across_core())
    pump(run_down)
    feed_out(far)
    sum_out.start(1 - me.y)
    feed_out(other)
    sum_out.start(me.y)
    feed_out(beside)
    feed_out(quarter)
    load_o.append(run.local(WOQ, w_o))
    load_few.append(run.local(H1, h1))

    def project_back(block, start, size_b):
        @pl.loop(0, size_b, step=256)
        def _(i):
            here = at(start + i, 256, 256)
            there = at(block * local + start + i, 256, 256)
            values = branch[block, here, :]
            do[there, :] = times_transposed(values, w_o[...]).astype(low)
            acc_o[...] += inner_rows(o[there, :], values)

    for copy in load_o:
        copy.wait()
    project_back(quarter, 0, local)
    pump(run_down)
    run.arrive(core_b)
    project_back(other, 0, local)
    pump(run_up)
    far_b = []

    def pass_on(h):
        run.arrive(over_b[h])
        part = branch.at[beside, h * half : (h + 1) * half]
        far_b.append(run.remote(part, part, me.across_core()))
        project_back(beside, h * half, half)

    pass_on(0)
    pump(run_down)
    pump(run_up)
    pump(run_down, 2)
    sum_out.cross()
    pass_on(1)
    pump(run_up)
    for h in range(2):
        run.arrive(far_b[h])
        project_back(far, h * half, half)
    grad_o[...] = acc_o[...].reshape(chips, few, width).astype(low)
    total_o = ChipSum(me, run, grad_o, lambda z: grad_o.at[z * 2 + me.x], far_o, over_o)
    total_o.send(n_z)
    run_o = chain(total_o, to_slab(2 * rows), share.flat_steps((2 * rows, base)))
    for copy in load_few:
        copy.wait()
    for g in range(2):
        stops = []
        end = 0
        for item in range(n_items - 1):
            end = end + ends[g, 0, item]
            stops.append(end)
        for head in range(heads):
            slope = jnp.exp2(-(jnp.zeros((1, 1), f32) + (quarter * heads + head + 1)))
            head_back(qkv, o, lse, do, dqkv, sum_k, sum_v, g, head, heads, size, count, stops, slope)
            if 2 * g + head == 1:
                pump(run_down)

    weight_grad(grad_q, lambda columns, b: h1[block_rows(b), columns], lambda b: dqkv[block_rows(b), :])
    total_q = ChipSum(me, run, grad_q, lambda z: grad_q.at[z * 2 + me.x], far_q, over_q)
    total_q.send(n_z)
    summed = []

    def after_q():
        while not summed:
            yield
        yield from share.steps((base + 48, base + 80, 3 * rows))

    def place_and_tell(value):
        place_q(value)
        summed.append(True)

    run_q = chain(total_q, place_and_tell, share.steps((base, base + 16, base + 48)))
    run_r = after_q()
    pump(run_down)

    def project_in(block):
        @pl.loop(0, local, step=256)
        def _(i):
            part_h1[block, at(i, 256, 256), :] = times_transposed(
                dqkv[at(block * local + i, 256, 256), :], w_q[...]
            ).astype(low)

    project_in(far)
    sum_h1 = QuadSum(me, run, part_h1, part_h1.at[group], near_h2, over_h2)
    sum_h1.start(1 - me.y)
    project_in(other)
    sum_h1.start(me.y)
    project_in(beside)
    pump(run_q)
    project_in(quarter)
    pump(run_o)
    pump(run_up)
    sum_h1.cross()
    pump(run_up)
    pump(run_q)
    pump(run_up)
    pump(run_o)
    pump(run_up)
    pump(run_down)
    sum_h1.landed()

    @pl.loop(0, local, step=64)
    def _(i):
        here = at(i, 64, 64)
        unit, factor = norm_parts(cot[here, :].astype(f32))
        grad = sum_h1.rows(here)
        base = branch[quarter, here, :].astype(f32)
        cot[here, :] = (base + norm_back_rows(grad, unit, factor, attn_gain[...])).astype(low)
        small[0:1] += jnp.sum(grad * unit, axis=0, keepdims=True)
        small[1:2] += jnp.sum(grad, axis=0, keepdims=True)

    run.later(cot, GRAD_TOKENS)
    slab[3 * rows :, :] = small[...].astype(low)
    last = share.flat_steps((3 * rows, slab.shape[0]))
    sum_out.landed()

    @pl.loop(0, local, step=64)
    def _(i):
        here = at(i, 64, 64)
        part_out[quarter, here, :] = (middle[here, :] + sum_out.rows(here) + b_down[...]).astype(low)

    run.later(part_out.at[quarter], BLOCK_OUT)
    threads = [last, run_q, run_r, run_up, run_o, run_down]
    for _ in range(16):
        for thread in threads:
            pump(thread)
    run.finish()


def back(n_z, n_items, feed, mid, cot, tok, saved, lq, b_up, attn_gain, ffn_gain, b_down):
    low, f32 = jnp.bfloat16, jnp.float32
    local, width = tok.shape
    chips = 2 * n_z
    heads, size = HEADS // 4, width // HEADS
    rows, few = width // chips, width // 4 // chips
    cols = 3 * heads * size
    shape = jax.ShapeDtypeStruct
    block, four, flat = (local, width), (4, local, width), (4 * local, width)
    deep = 3 * rows + 16
    v = pltpu.VMEM

    def sums(piece):
        return [v((chips,) + piece, low), v((n_z,) + piece, low), v((n_z - 1,) + piece, low)]

    scratch = (
        [v(flat, low)] * 3
        + [v(four, low)]
        + [v((width, width), low)] * 2
        + [v(four, low), v((2,) + block, low), v(block, low)] * 2
        + sums((rows, width)) * 2
        + [v(block, f32), v(block, low), v(saved[3].shape, f32), pltpu.SMEM(lq.shape, lq.dtype)]
        + [v(four, low)]
        + [v((2 * local, size), f32)] * 2
        + [v((heads * size, width), f32)]
        + sums((rows, cols))
        + sums((few, width))
        + [v((16, width), f32), v((deep, width), low)]
    )
    return communicate(
        functools.partial(back_kernel, n_z, n_items),
        [shape(block, low), shape(block, low), shape((4 * chips, deep, width), low)],
        tuple(feed) + (mid, cot, tok) + tuple(saved) + (lq, b_up, attn_gain, ffn_gain, b_down),
        [HBM] * 3,
        [HBM] * (len(feed) + 3 + len(saved) + 1) + [VMEM] * 4,
        (320, 48),
        scratch,
        call_id=2,
        limit=63 << 20,
    )


def unfold_kernel(rows, head_cols, few, shared, down, up, qkv, out, small, bias):
    f32 = jnp.float32
    width = shared.shape[-1]
    chips = up.shape[1] // width * 2
    unit = width // chips
    third = qkv.shape[1] // 3

    @pl.when(pl.program_id(0) == 0)
    def _():
        small[...] = jnp.zeros_like(small)
        bias[...] = jnp.zeros_like(bias)

    for q in range(4):
        down[q * rows : (q + 1) * rows] = shared[q, :rows].astype(f32)
        for s in range(chips):
            start = (s * 4 + q) * unit
            up[:, start : start + unit] = shared[q, rows : 2 * rows, s * unit : (s + 1) * unit].astype(f32)
        base, kept = 2 * rows + few, rows - few
        for i in range(3):
            here = slice(i * third + q * head_cols, i * third + (q + 1) * head_cols)
            qkv[:kept, here] = shared[q, base : base + kept, i * head_cols : (i + 1) * head_cols].astype(f32)
            qkv[kept:, here] = shared[q, base + i * few : base + (i + 1) * few, 3 * head_cols :].astype(f32)
        out[q] = shared[q, 2 * rows : base].astype(f32)
        extra = shared[q, 3 * rows :].astype(f32)
        small[...] += extra
        bias[q : q + 1] += extra[5:6]


def unfold(shared, rows, few, ff):
    devices, deep, width = shared.shape
    chips = devices // 4
    f32 = jnp.float32
    head_cols = width // 4
    return pl.pallas_call(
        functools.partial(unfold_kernel, rows, head_cols, few),
        grid=(chips,),
        in_specs=[pl.BlockSpec((4, deep, width), lambda s: (s, 0, 0))],
        out_specs=[
            pl.BlockSpec((4 * rows, width), lambda s: (s, 0)),
            pl.BlockSpec((rows, ff), lambda s: (s, 0)),
            pl.BlockSpec((rows, 3 * width), lambda s: (s, 0)),
            pl.BlockSpec((4, None, few, width), lambda s: (0, s, 0, 0)),
            pl.BlockSpec((deep - 3 * rows, width), lambda s: (0, 0)),
            pl.BlockSpec((4, width), lambda s: (0, 0)),
        ],
        out_shape=[
            jax.ShapeDtypeStruct((ff, width), f32),
            jax.ShapeDtypeStruct((width, ff), f32),
            jax.ShapeDtypeStruct((width, 3 * width), f32),
            jax.ShapeDtypeStruct((4, chips, few, width), f32),
            jax.ShapeDtypeStruct((deep - 3 * rows, width), f32),
            jax.ShapeDtypeStruct((4, width), f32),
        ],
        compiler_params=pltpu.CompilerParams(vmem_limit_bytes=56 << 20),
    )(shared)


def on_quad(
    tokens,
    lengths,
    attn_gain,
    attn_shift,
    w_qkv,
    w_out,
    ffn_gain,
    ffn_shift,
    w_up,
    b_up,
    w_down,
    b_down,
    cotangent,
):
    low = jnp.bfloat16
    local, width = tokens.shape
    n_dp = lax.axis_size("dp")
    n_z, chips = n_dp // 4, n_dp // 2
    size = width // HEADS
    heads = HEADS // 4
    count = 2 * local
    me = Place(n_z)
    lens = jnp.zeros((8, 128), jnp.int32).at[:1, : lengths.shape[1]].set(lengths)
    gains = [value.reshape(1, width) for value in (attn_gain, attn_shift, ffn_gain, ffn_shift)]
    WQ, WOQ, WU, WD, CQ, h1, qkv, o, lse, h2, middle, LQ = front(
        n_z, lengths.shape[1], w_qkv, w_out, w_up, w_down, tokens, cotangent, lens, gains
    )
    unit = w_up.shape[1] // chips // 4
    bias = lax.dynamic_index_in_dim(b_up.reshape(chips, 4, unit), me.quarter, 1, keepdims=False).reshape(-1)
    block_out, grad_tokens, shared = back(
        n_z,
        lengths.shape[1],
        [h2, CQ.reshape(4 * local, width), WU, WD],
        middle,
        cotangent,
        tokens,
        [h1.reshape(4 * local, width), qkv, o, lse, WQ, WOQ],
        LQ,
        bias.reshape(1, width),
        gains[0],
        gains[2],
        b_down.reshape(1, width),
    )
    rows, few = width // chips, width // 4 // chips
    ff = w_up.shape[1]
    grad_w_down, grad_w_up, grad_w_qkv, grad_w_out, vectors, bias = unfold(shared, rows, few, ff)
    return (
        block_out,
        grad_tokens,
        vectors[0],
        vectors[1],
        grad_w_qkv,
        grad_w_out.reshape(width, width),
        vectors[2],
        vectors[3],
        grad_w_up,
        jnp.transpose(bias.reshape(4, chips, unit), (1, 0, 2)).reshape(ff),
        grad_w_down,
        vectors[4],
    )


def solution(mesh):
    n_dp, n_seq = mesh.shape["dp"], mesh.shape["seq"]
    quad = n_seq == 2 and n_dp % 4 == 0 and n_dp >= 8 and n_dp <= 16
    return jax.shard_map(
        on_quad if quad else on_device,
        mesh=mesh,
        in_specs=(
            P(("dp", "seq"), None),
            P("dp", None),
            P(),
            P(),
            P("dp", None),
            P("dp", None),
            P(),
            P(),
            P("dp", None),
            P(),
            P("dp", None),
            P(),
            P(("dp", "seq"), None),
        ),
        out_specs=(
            P(("dp", "seq"), None),
            P(("dp", "seq"), None),
            P(),
            P(),
            P(),
            P(),
            P(),
            P(),
            P(),
            P(),
            P(),
            P(),
        ),
        check_vma=False,
    )
```
